256 devices in a mesh: px: 4 (over x), py: 2 (over y_hi), fr: 32 (over z, y_lo, core).
Axes of the slice: x: 4, y: 4 (y_hi: 2, y_lo: 2; y = y_hi * 2 + y_lo), z: 8, core: 2. Of those that a mesh axis runs over, the one named last changes fastest.
Arguments:
- water_voxel: int32 [128, 8, 4, 128], P('fr', 'px', 'py'), may hold values from 0 to 23039, as said below
- water_offset: float32 [128, 8, 4, 3, 128], P('fr', 'px', 'py'), may hold values from -0.25 to 0.25
- water_angles: float32 [128, 8, 4, 3, 128], P('fr', 'px', 'py'), may hold values from -3.140625 to 3.140625
- water_count: int32 [128, 8, 4], P('fr', 'px', 'py'), may hold values from 16 to 128, as said below
- solute_frac: float32 [8, 4, 3, 128], P('px', 'py'), may hold values from 0 to 1
- solute_type: int32 [8, 4, 128], P('px', 'py'), may hold values from 0 to 31
- type_sigma: float32 [32], replicated, may hold values from 2.4 to 3.9
- type_well: float32 [32], replicated, may hold values from 0.02 to 0.3
- type_charge: float32 [32], replicated, may hold values from -1 to 1
Outputs:
- gist_grid: float32 [13, 8, 4, 23040], P(None, 'px', 'py', 'fr')
The draws below stay inside these ranges and needn't reach their ends.
Inputs may be any that keep to these rules, and one draw needn't show every extreme that they name: `water_count`: at most 128 waters in a cell; some cell holds 128 in every frame; the slots below the count hold waters. `water_voxel`: in each frame and cell, each of the 32 aligned ranges of 720 voxels holds exactly 4 of the slots; some slot lies at voxel 0 and some at voxel 23040 - 1.
All inputs are finite; a program needn't handle non-finite values.
Results may differ from the reference program's by a relative error of at most 0.0003.
Values sent between devices are 32-bit elements; how exact they have to be, the bound alone decides.
No kernel may reach another device: no remote copies, remote signals or barrier semaphores. Data moves between devices by JAX's collectives and lax.ppermute only.
A program may use at most 64 MiB of HBM per device.

```python
import math
import jax
import jax.numpy as jnp
from jax import lax

CELL_XY = 24
SLAB = 40
SLOTS = 128
SOLUTE = 128
NTYPES = 32
FRAMES = 128
GCX = 8
GCY = 4
CELL_VOX = 23040


def draw_water_count(key, part):
    key_level = jax.random.fold_in(key, 11)
    key_jitter = jax.random.fold_in(key, 23)
    density_level = jax.random.randint(key_level, (1, GCX, GCY), 0, 4)
    first_x = lax.broadcasted_iota(jnp.int32, (1, GCX, GCY), 1) == 0
    first_y = lax.broadcasted_iota(jnp.int32, (1, GCX, GCY), 2) == 0
    density_level = jnp.where(first_x & first_y, 0, density_level)
    jitter = jax.random.randint(key_jitter, (FRAMES, GCX, GCY), 0, SLOTS // 8 + 1)
    base_count = jnp.right_shift(jnp.int32(SLOTS), density_level)
    counts = jnp.where(density_level == 0, SLOTS, jnp.minimum(SLOTS, base_count + jitter))
    return counts.astype(jnp.int32)


def draw_water_voxel(key, part):
    key_rank = jax.random.fold_in(key, 37)
    key_place = jax.random.fold_in(key, 41)
    shape = (FRAMES, GCX, GCY, SLOTS)
    share = CELL_VOX // 32
    per_band = SLOTS // 32
    score = jax.random.randint(key_rank, shape, 0, 1048576) * SLOTS + lax.broadcasted_iota(jnp.int32, shape, 3)
    slot_rank = jnp.argsort(jnp.argsort(score, axis=-1), axis=-1).astype(jnp.int32)
    band = slot_rank // per_band
    within = jax.random.randint(key_place, shape, 0, share)
    within = jnp.where(slot_rank == 0, 0, jnp.where(slot_rank == SLOTS - 1, share - 1, within))
    return (band * share + within).astype(jnp.int32)


def set_ends(drawn, key, least, largest):
    longest = drawn.shape.index(max(drawn.shape))
    spots = []
    for shift in (0, 1):
        where = [jax.random.randint(jax.random.fold_in(key, axis), (), 0, length) for axis, length in enumerate(drawn.shape)]
        where[longest] = (where[longest] + shift) % drawn.shape[longest]
        spots.append(tuple(where))
    return drawn.at[spots[0]].set(least).at[spots[1]].set(largest)


def steps_of(rng, extent, split, low, top_value):
    level = 1.0
    for dim, shards_of in split:
        heights = jax.random.uniform(jax.random.fold_in(jax.random.fold_in(rng, 6), dim), (shards_of,), jnp.float32, low / len(split), top_value / len(split))
        level = level * jnp.repeat(jnp.exp(heights), extent[dim] // shards_of).reshape((-1,) + (1,) * (len(extent) - 1 - dim))
    return level


def scatter_about(own_key, shape, spread, bound, kind=jnp.bfloat16):
    values = jax.random.normal(own_key, shape, jnp.float32) * spread
    return jnp.minimum(jnp.maximum(values, -bound), bound).astype(kind)


def setup_inputs(seed: int = 0) -> dict:
    splits = jax.random.split(jax.random.key(seed), 10)
    return {
        "water_voxel": draw_water_voxel(jax.random.fold_in(splits[9], 71), 0),
        "water_offset": jnp.clip(jax.random.uniform(splits[1], (FRAMES, GCX, GCY, 3, SLOTS), jnp.float32, -0.25, 0.25) * steps_of(splits[1], (FRAMES, GCX, GCY, 3, SLOTS), ((0, 32), (1, 4), (2, 2)), -0.4, 0.0), -0.25, 0.25),
        "water_angles": jnp.clip(jax.random.uniform(splits[2], (FRAMES, GCX, GCY, 3, SLOTS), jnp.float32, -3.140625, 3.140625), -3.140625, 3.140625),
        "water_count": draw_water_count(jax.random.fold_in(splits[9], 71), 0),
        "solute_frac": jnp.clip(1.0 * jax.random.uniform(splits[4], (GCX, GCY, 3, SOLUTE), jnp.float32) ** steps_of(splits[4], (GCX, GCY, 3, SOLUTE), ((0, 4), (1, 2)), -0.2, 0.2), 0.0, 1.0),
        "solute_type": set_ends(jax.random.randint(splits[5], (GCX, GCY, SOLUTE), 0, NTYPES), jax.random.fold_in(splits[5], 1), 0, NTYPES - 1).astype(jnp.int32),
        "type_sigma": jnp.clip(jax.random.uniform(splits[6], (NTYPES,), jnp.float32, 2.4, 3.9), 2.4, 3.9),
        "type_well": jnp.clip(jnp.exp(jax.random.uniform(splits[7], (NTYPES,), jnp.float32, math.log(0.02), math.log(0.3))), 0.02, 0.3),
        "type_charge": scatter_about(splits[8], (NTYPES,), 0.4, 1.0, jnp.float32),
    }


spacing = 0.5
soft_sq = 9.0
sigma_water = 3.1507
eps_water = 0.1521
k_dipole = 79.4
k_charge = 162.3
rho_bulk = 0.0334
pair_index = ((0, 0), (0, 1), (0, 2), (0, 3), (1, 1), (1, 2), (1, 3), (2, 2), (2, 3), (3, 3))

def water_parts(voxel_id, offset, angles, counts):
    plane_size = CELL_XY * SLAB
    cell_x = voxel_id // plane_size
    cell_y = voxel_id // SLAB % CELL_XY
    cell_z = voxel_id % SLAB
    lattice = jnp.stack([cell_x, cell_y, cell_z], axis=-2).astype(offset.dtype)
    position = spacing * (lattice + 0.5) + offset
    half_b = 0.5 * angles[..., 1, :]
    plus_half = 0.5 * (angles[..., 0, :] + angles[..., 2, :])
    minus_half = 0.5 * (angles[..., 0, :] - angles[..., 2, :])
    quat_w = jnp.cos(half_b) * jnp.cos(plus_half)
    quat_x = -jnp.sin(half_b) * jnp.sin(minus_half)
    quat_y = jnp.sin(half_b) * jnp.cos(minus_half)
    quat_z = jnp.cos(half_b) * jnp.sin(plus_half)
    dipole = jnp.stack([2.0 * (quat_x * quat_z + quat_w * quat_y), 2.0 * (quat_y * quat_z - quat_w * quat_x), 1.0 - 2.0 * (quat_x * quat_x + quat_y * quat_y)], axis=-2)
    slot_count = voxel_id.shape[-1]
    filled = (jnp.arange(slot_count, dtype=jnp.int32) < counts[..., None]).astype(offset.dtype)
    features = jnp.concatenate([position, dipole, filled[..., None, :]], axis=-2)
    quaternion = jnp.stack([quat_w, quat_x, quat_y, quat_z], axis=-2)
    return (features, quaternion)

def solute_features(solute_frac, sigma_atom, root_atom, charge_atom):
    cell_box = jnp.array([spacing * CELL_XY, spacing * CELL_XY, spacing * SLAB], dtype=solute_frac.dtype)[:, None]
    place = solute_frac * cell_box
    return jnp.concatenate([place, jnp.stack([sigma_atom, root_atom, charge_atom], axis=-2)], axis=-2)

def energies(own, water_pad, solute_pad):
    cells_x, cells_y, slot_count = (own.shape[0], own.shape[1], own.shape[3])
    cutoff = spacing * CELL_XY
    position = own[:, :, 0:3]
    filled = own[:, :, 6]
    dipole_own = own[:, :, 3:6, :, None]
    not_self = 1.0 - jnp.eye(slot_count, dtype=own.dtype)
    water_water = jnp.zeros((cells_x, cells_y, slot_count), own.dtype)
    solute_water = jnp.zeros((cells_x, cells_y, slot_count), own.dtype)
    for step_x in (-1, 0, 1):
        for step_y in (-1, 0, 1):
            shift_vec = jnp.array([step_x * cutoff, step_y * cutoff, 0.0], dtype=own.dtype)[:, None, None]
            others = water_pad[1 + step_x:1 + step_x + cells_x, 1 + step_y:1 + step_y + cells_y]
            separation = others[:, :, 0:3, None, :] + shift_vec - position[:, :, :, :, None]
            dist_sq = lax.optimization_barrier(jnp.sum(separation * separation, axis=2))
            inverse = 1.0 / (dist_sq + soft_sq)
            switch = jnp.square(jnp.maximum(0.0, 1.0 - dist_sq / (cutoff * cutoff)))
            ratio_cube = (sigma_water * sigma_water * inverse) ** 3
            lj_term = 4.0 * eps_water * (ratio_cube * ratio_cube - ratio_cube)
            dipole_other = others[:, :, 3:6, None, :]
            aligned = lax.optimization_barrier(jnp.sum(dipole_own * dipole_other, axis=2))
            along_own = lax.optimization_barrier(jnp.sum(dipole_own * separation, axis=2))
            along_other = lax.optimization_barrier(jnp.sum(dipole_other * separation, axis=2))
            dipolar = k_dipole * (aligned - 3.0 * along_own * along_other * inverse) * inverse * jnp.sqrt(inverse)
            pair_energy = (lj_term + dipolar) * switch * filled[:, :, :, None] * others[:, :, 6, None, :]
            if step_x == 0 and step_y == 0:
                pair_energy = pair_energy * not_self
            water_water = water_water + 0.5 * lax.optimization_barrier(jnp.sum(pair_energy, axis=3))
            solute_atoms = solute_pad[1 + step_x:1 + step_x + cells_x, 1 + step_y:1 + step_y + cells_y]
            away = position[:, :, :, :, None] - solute_atoms[:, :, 0:3, None, :] - shift_vec
            dist_solute = lax.optimization_barrier(jnp.sum(away * away, axis=2))
            inverse_solute = 1.0 / (dist_solute + soft_sq)
            switch_solute = jnp.square(jnp.maximum(0.0, 1.0 - dist_solute / (cutoff * cutoff)))
            sigma_mix = 0.5 * (sigma_water + solute_atoms[:, :, 3, None, :])
            ratio_solute = (sigma_mix * sigma_mix * inverse_solute) ** 3
            lj_solute = 4.0 * jnp.sqrt(eps_water) * solute_atoms[:, :, 4, None, :] * (ratio_solute * ratio_solute - ratio_solute)
            charge_term = -k_charge * solute_atoms[:, :, 5, None, :] * lax.optimization_barrier(jnp.sum(dipole_own * away, axis=2)) * inverse_solute * jnp.sqrt(inverse_solute)
            solute_water = solute_water + lax.optimization_barrier(jnp.sum((lj_solute + charge_term) * switch_solute, axis=3)) * filled
    return (water_water, solute_water)

def records(features, quaternion, water_water, solute_water):
    filled = features[..., 6, :]
    moments = [quaternion[..., first_comp, :] * quaternion[..., second_comp, :] * filled for first_comp, second_comp in pair_index]
    return jnp.stack([filled, solute_water, water_water] + moments, axis=-2)

def finish(totals, frame_total):
    counted = totals[0]
    density = counted / (frame_total * rho_bulk * spacing ** 3)
    scaled = totals[1:] / jnp.maximum(counted, 1.0)
    return jnp.concatenate([density[None], scaled], axis=0)

def reference(water_voxel, water_offset, water_angles, water_count, solute_frac, solute_type, type_sigma, type_well, type_charge):
    solute = solute_features(solute_frac, type_sigma[solute_type], jnp.sqrt(type_well)[solute_type], type_charge[solute_type])
    solute_pad = jnp.pad(solute, ((1, 1), (1, 1), (0, 0), (0, 0)))
    frame_total, grid_x, grid_y, slot_count = water_voxel.shape
    cell_vox = CELL_XY * CELL_XY * SLAB
    cell_number = jnp.arange(grid_x * grid_y, dtype=jnp.int32).reshape(grid_x, grid_y, 1)

    def one_frame(totals, inputs):
        voxel_id, offset, angles, counts = inputs
        features, quaternion = water_parts(voxel_id, offset, angles, counts)
        water_pad = jnp.pad(features, ((1, 1), (1, 1), (0, 0), (0, 0)))
        water_water, solute_water = energies(features, water_pad, solute_pad)
        record = records(features, quaternion, water_water, solute_water)
        flat_index = (cell_number * cell_vox + voxel_id).reshape(-1)
        values = jnp.moveaxis(record, 2, 0).reshape(13, -1)
        return (totals.at[:, flat_index].add(values), None)
    totals = jnp.zeros((13, grid_x * grid_y * cell_vox), jnp.float32)
    totals, unused = lax.scan(one_frame, totals, (water_voxel, water_offset, water_angles, water_count))
    totals = totals.reshape(13, grid_x, grid_y, cell_vox)
    return finish(totals, frame_total)
```

```python
import functools

import jax
import jax.numpy as jnp
from jax import lax
from jax.experimental import pallas as pl
from jax.experimental.pallas import tpu as pltpu
from jax.sharding import PartitionSpec as P

CELL_XY = 24
SLAB = 40
F32 = jnp.float32
BF16 = jnp.bfloat16

spacing = 0.5
soft_sq = 9.0
sigma_water = 3.1507
eps_water = 0.1521
k_dipole = 79.4
k_charge = 162.3
rho_bulk = 0.0334
pair_index = ((0, 0), (0, 1), (0, 2), (0, 3), (1, 1), (1, 2), (1, 3), (2, 2), (2, 3), (3, 3))

CUTOFF = spacing * CELL_XY
UNIT = 1.0 / sigma_water
P_SOFT = soft_sq * UNIT * UNIT
P_CUT = CUTOFF * CUTOFF * UNIT * UNIT
P_END = P_SOFT + P_CUT
KD = k_dipole / (4.0 * eps_water * sigma_water**3)
KQ = k_charge * UNIT * UNIT
SCALE_WW = 0.5 * 4.0 * eps_water / (P_CUT * P_CUT)
SCALE_SW = 1.0 / (P_CUT * P_CUT)
FAR = 1.0e4
ROWS = 64


def split3(value):
    first = value.astype(BF16).astype(F32)
    rest = value - first
    second = rest.astype(BF16).astype(F32)
    return first, second, (rest - second).astype(BF16).astype(F32)


def rows_of(parts, fill=0.0):
    lanes = parts[0].shape[1]
    missing = 8 - len(parts)
    if missing:
        parts = list(parts) + [jnp.full((missing, lanes), fill, F32)]
    return jnp.concatenate(parts, axis=0)


def sincos(angle):
    turns = jnp.floor(angle * 0.6366197723675814 + 0.5)
    rest = angle - turns * 1.5703125 - turns * 4.838267948966e-4
    square = rest * rest
    sine = rest + rest * square * (
        -1.6666654611e-1 + square * (8.3321608736e-3 - square * 1.9515295891e-4)
    )
    cosine = (
        1.0
        - 0.5 * square
        + square
        * square
        * (4.166664568298827e-2 + square * (-1.388731625493765e-3 + square * 2.443315711809948e-5))
    )
    quarter = turns.astype(jnp.int32) & 3
    odd = (quarter & 1) == 1
    sin_out = jnp.where(odd, cosine, sine)
    cos_out = jnp.where(odd, sine, cosine)
    sin_out = jnp.where(quarter >= 2, -sin_out, sin_out)
    cos_out = jnp.where((quarter == 1) | (quarter == 2), -cos_out, cos_out)
    return sin_out, cos_out


def prepare_kernel(
    place_ref, count_ref, sigma_ref, well_ref, charge_ref,
    voxel_ref, offset_ref, angle_ref, frac_ref, type_ref,
    feat_ref, side_ref, comp_ref,
    raw_ref, key_ref, sorted_ref,
):
    frames = voxel_ref.shape[0]
    lane = lax.broadcasted_iota(jnp.int32, (1, 128), 1)
    for i in range(2):
        for j in range(2):
            for f in range(frames):
                fc = (i * 2 + j) * frames + f
                voxel = voxel_ref[f, i, j : j + 1, :]
                raw_ref[fc, 0:1, :] = voxel.astype(F32)
                raw_ref[fc, 1:4, :] = offset_ref[f, i, j]
                raw_ref[fc, 4:7, :] = angle_ref[f, i, j]
                raw_ref[fc, 7:8, :] = jnp.where(lane < count_ref[f, i, j], 1.0, 0.0).astype(F32)
                key_ref[fc : fc + 1, :] = (voxel * 128 + lane).astype(F32)
    total = 4 * frames
    keys = key_ref[...]
    keys_t = keys.T
    rank_iota = lax.broadcasted_iota(jnp.int32, (128, 128), 0).astype(F32)
    for fc in range(total):
        before = jnp.where(keys_t[:, fc : fc + 1] < keys[fc : fc + 1, :], 1.0, 0.0)
        rank = jnp.sum(before, axis=0, keepdims=True)
        chosen = jnp.where(rank_iota == rank, 1.0, 0.0).astype(BF16)
        parts = jnp.concatenate(split3(raw_ref[fc]), axis=0).astype(BF16)
        moved = lax.dot_general(
            parts, chosen, (((1,), (1,)), ((), ())), preferred_element_type=F32
        )
        sorted_ref[:, fc, :] = moved[0:8] + moved[8:16] + moved[16:24]

    voxel = sorted_ref[0]
    cell_x = jnp.floor((voxel + 0.5) * (1.0 / (CELL_XY * SLAB)))
    in_plane = voxel - cell_x * (CELL_XY * SLAB)
    cell_y = jnp.floor((in_plane + 0.5) * (1.0 / SLAB))
    cell_z = in_plane - cell_y * SLAB
    row = lax.broadcasted_iota(jnp.int32, (total, 128), 0)
    own_x = (row // (2 * frames)).astype(F32)
    own_y = ((row // frames) % 2).astype(F32)
    x = (spacing * (cell_x + 0.5) + sorted_ref[1] + CUTOFF * (own_x - 1.0)) * UNIT
    y = (spacing * (cell_y + 0.5) + sorted_ref[2] + CUTOFF * (own_y - 1.0)) * UNIT
    z = (spacing * (cell_z + 0.5) + sorted_ref[3] - 0.5 * spacing * SLAB) * UNIT
    sin_b, cos_b = sincos(0.5 * sorted_ref[5])
    sin_p, cos_p = sincos(0.5 * (sorted_ref[4] + sorted_ref[6]))
    sin_m, cos_m = sincos(0.5 * (sorted_ref[4] - sorted_ref[6]))
    quat_w = cos_b * cos_p
    quat_x = -sin_b * sin_m
    quat_y = sin_b * cos_m
    quat_z = cos_b * sin_p
    features = (
        x, y, z,
        2.0 * (quat_x * quat_z + quat_w * quat_y),
        2.0 * (quat_y * quat_z - quat_w * quat_x),
        1.0 - 2.0 * (quat_x * quat_x + quat_y * quat_y),
        sorted_ref[7],
    )
    for number, value in enumerate(features):
        for cell in range(4):
            feat_ref[cell, 0:frames, number, :] = value[cell * frames : (cell + 1) * frames]
    share = CELL_XY * CELL_XY * SLAB // 32
    band = (lax.broadcasted_iota(jnp.int32, (total, 128), 1) // 4 * share).astype(F32)
    for number, value in enumerate((quat_w, quat_x, quat_y, quat_z, sorted_ref[7], voxel - band)):
        comp_ref[number] = value

    for i in range(2):
        for j in range(2):
            kind = type_ref[i, j : j + 1, :]
            sigma = jnp.zeros((1, 128), F32)
            well = jnp.zeros((1, 128), F32)
            charge = jnp.zeros((1, 128), F32)
            for t in range(sigma_ref.shape[0]):
                same = kind == t
                sigma = jnp.where(same, sigma_ref[t], sigma)
                well = jnp.where(same, well_ref[t], well)
                charge = jnp.where(same, charge_ref[t], charge)
            ratio = 0.5 * (1.0 + sigma * UNIT)
            cube = ratio * ratio * ratio
            sixth = cube * cube
            lower = (4.0 * eps_water**0.5) * jnp.sqrt(well) * sixth
            frac = frac_ref[i, j]
            atom_x = (frac[0:1] * CUTOFF + CUTOFF * (i - 1.0)) * UNIT
            atom_y = (frac[1:2] * CUTOFF + CUTOFF * (j - 1.0)) * UNIT
            atom_z = (frac[2:3] * (spacing * SLAB) - 0.5 * spacing * SLAB) * UNIT
            feat_ref[i * 2 + j, frames] = rows_of(
                [atom_x, atom_y, atom_z, lower, lower * sixth, charge, jnp.ones((1, 128), F32)]
            )
    for cell in range(4):
        for f in range(frames):
            feat_ref[cell, f, 7:8, :] = jnp.zeros((1, 128), F32)
    facing = 1 - place_ref[1]
    for i in range(2):
        side_ref[i] = feat_ref[i * 2 + facing]


def partner_rows(base):
    first, second, third = split3(base)
    number = lax.broadcasted_iota(jnp.int32, (8, 128), 0)
    ones = jnp.where(number < 3, 1.0, 0.0).astype(F32)
    stacked = jnp.concatenate(
        [first, first, first, second, second, third, ones, jnp.zeros((8, 128), F32)], axis=0
    )
    return stacked.T.astype(BF16)


def water_partner(value, shift, absent):
    x, y, z = value[0:1] + shift[0], value[1:2] + shift[1], value[2:3]
    mx, my, mz = value[3:4], value[4:5], value[5:6]
    n = x * x + y * y + z * z + FAR * ((1.0 - value[6:7]) + absent)
    e = mx * x + my * y + mz * z
    return partner_rows(jnp.concatenate([x, y, z, mx, my, mz, n, e], axis=0))


def solute_partner(value, shift, absent):
    x, y, z, charge = value[0:1] + shift[0], value[1:2] + shift[1], value[2:3], value[5:6]
    n = x * x + y * y + z * z + FAR * ((1.0 - value[6:7]) + absent)
    base = jnp.concatenate([x, y, z, charge * x, charge * y, charge * z, n, charge], axis=0)
    lower = jnp.broadcast_to(value[3:4], (128, 128)).T
    upper = jnp.broadcast_to(value[4:5], (128, 128)).T
    return partner_rows(base), lower, upper


def own_side(value):
    x, y, z = value[0:1], value[1:2], value[2:3]
    mx, my, mz = value[3:4], value[4:5], value[5:6]
    zero = jnp.zeros((1, 128), F32)
    one = jnp.ones((1, 128), F32)
    n = x * x + y * y + z * z + P_SOFT
    c = mx * x + my * y + mz * z
    kd3 = 3.0 * KD
    sides = (
        ([-2.0 * x, -2.0 * y, -2.0 * z, zero, zero, zero, one, zero], n),
        ([zero, zero, zero, KD * mx, KD * my, KD * mz, zero, zero], None),
        ([mx, my, mz, zero, zero, zero, zero, zero], -c),
        ([zero, zero, zero, -kd3 * x, -kd3 * y, -kd3 * z, zero, kd3 * one], None),
        ([zero, zero, zero, KQ * mx, KQ * my, KQ * mz, zero, -KQ * c], None),
    )
    out = []
    for rows, term in sides:
        first, second, third = split3(jnp.concatenate(rows, axis=0))
        if term is None:
            last = jnp.zeros((16, 128), F32)
        else:
            last = jnp.concatenate(list(split3(term)) + [jnp.zeros((13, 128), F32)], axis=0)
        out.append(
            jnp.concatenate([first, second, third, first, second, first, last], axis=0).astype(BF16)
        )
    return out


def fold(acc, value):
    for k in range(value.shape[0] // 8):
        acc = acc + value[8 * k : 8 * k + 8]
    return acc


CHUNK = 16


def water_pairs(acc, p, al, ao, ab):
    for k in range(p.shape[0] // CHUNK):
        part = slice(k * CHUNK, (k + 1) * CHUNK)
        pk = p[part]
        root = lax.rsqrt(pk)
        u = root * root
        u15 = u * root
        window = jnp.maximum(P_END - pk, 0.0)
        inner = u15 * (u15 * u15 - 1.0) + (al[part] - ao[part] * ab[part] * u)
        acc = fold(acc, u15 * inner * (window * window))
    return acc


def solute_pairs(acc, p, charge, lower, upper):
    for k in range(p.shape[0] // CHUNK):
        part = slice(k * CHUNK, (k + 1) * CHUNK)
        pk = p[part]
        root = lax.rsqrt(pk)
        u15 = root * root * root
        window = jnp.maximum(P_END - pk, 0.0)
        low = jnp.concatenate([lower[part]] * 2, axis=1)
        high = jnp.concatenate([upper[part]] * 2, axis=1)
        inner = u15 * (high * (u15 * u15) - low) + charge[part]
        acc = fold(acc, u15 * inner * (window * window))
    return acc


def dot(left, right):
    return jnp.dot(left, right, preferred_element_type=F32)


def inner_kernel(feat_ref, comp_ref, acc_ref, rec_ref, left_ref, own_ref, coef_ref):
    frames = feat_ref.shape[1] - 1
    for cell in range(4):
        rows, lower, upper = solute_partner(feat_ref[cell, frames], (0.0, 0.0), 0.0)
        left_ref[frames, cell] = rows
        coef_ref[cell, 0] = lower
        coef_ref[cell, 1] = upper
        for f in range(frames):
            left_ref[f, cell] = water_partner(feat_ref[cell, f], (0.0, 0.0), 0.0)
            for q, side in enumerate(own_side(feat_ref[cell, f])):
                own_ref[f, q, cell] = side

    @pl.loop(0, frames)
    def _(f):
        for i in range(2):
            sides = [
                jnp.concatenate([own_ref[f, q, 2 * i], own_ref[f, q, 2 * i + 1]], axis=1)
                for q in range(5)
            ]
            acc_w = jnp.zeros((8, 256), F32)
            acc_s = jnp.zeros((8, 256), F32)
            for cell in range(4):
                left = left_ref[f, cell]
                acc_w = water_pairs(acc_w, *[dot(left, sides[q]) for q in range(4)])
                left = left_ref[frames, cell]
                acc_s = solute_pairs(
                    acc_s, dot(left, sides[0]), dot(left, sides[4]), coef_ref[cell, 0], coef_ref[cell, 1]
                )
            acc_ref[f, i, 0] = acc_w
            acc_ref[f, i, 1] = acc_s

    filled = comp_ref[4]
    rows = {0: filled, 13: comp_ref[5]}
    for number, (a, b) in enumerate(pair_index):
        rows[3 + number] = comp_ref[a] * comp_ref[b] * filled
    rec_ref[...] = jnp.zeros_like(rec_ref)
    for number, value in rows.items():
        rec_ref[:, number, :] = value


def outer_kernel(
    place_ref, feat_ref, side_ref, low_ref, high_ref, first_ref, rec_in_ref, send_ref,
    left_ref, own_ref, coef_ref, acc_ref, rec_ref,
):
    frames = feat_ref.shape[1] - 1
    px = place_ref[0]
    py = place_ref[1]
    last = place_ref[2]
    facing = 1 - py
    width = 2.0 * CUTOFF * UNIT
    to_side = jnp.where(py == 0, width, -width).astype(F32)
    no_low = jnp.where(px == 0, 1.0, 0.0).astype(F32)
    no_high = jnp.where(px == last, 1.0, 0.0).astype(F32)
    halo = (
        [(low_ref, k, (-width, to_side if k == 2 else 0.0), no_low) for k in range(3)]
        + [(high_ref, k, (width, to_side if k == 2 else 0.0), no_high) for k in range(3)]
        + [(side_ref, k, (0.0, to_side), 0.0) for k in range(2)]
    )
    for cell, (ref, k, shift, absent) in enumerate(halo):
        rows, lower, upper = solute_partner(ref[k, frames], shift, absent)
        left_ref[frames, cell] = rows
        coef_ref[cell, 0] = lower
        coef_ref[cell, 1] = upper
        for f in range(frames):
            left_ref[f, cell] = water_partner(ref[k, f], shift, absent)
    for cell in range(4):
        for f in range(frames):
            for q, side in enumerate(own_side(feat_ref[cell, f])):
                own_ref[f, q, cell] = side
    acc_ref[...] = first_ref[...]

    @pl.loop(0, frames)
    def _(f):
        def unit(sides, cell, acc_w, acc_s):
            left = left_ref[f, cell]
            acc_w = water_pairs(acc_w, *[dot(left, sides[q]) for q in range(4)])
            left = left_ref[frames, cell]
            acc_s = solute_pairs(
                acc_s, dot(left, sides[0]), dot(left, sides[4]), coef_ref[cell, 0], coef_ref[cell, 1]
            )
            return acc_w, acc_s

        for i in range(2):
            sides = [
                jnp.concatenate([own_ref[f, q, 2 * i], own_ref[f, q, 2 * i + 1]], axis=1)
                for q in range(5)
            ]
            acc_w = acc_ref[f, i, 0]
            acc_s = acc_ref[f, i, 1]
            for k in range(2):
                acc_w, acc_s = unit(sides, 3 * i + k, acc_w, acc_s)
            acc_ref[f, i, 0] = acc_w
            acc_ref[f, i, 1] = acc_s
        sides = [
            jnp.concatenate([own_ref[f, q, facing], own_ref[f, q, 2 + facing]], axis=1)
            for q in range(5)
        ]
        acc_w = jnp.zeros((8, 256), F32)
        acc_s = jnp.zeros((8, 256), F32)
        for k in range(2):
            acc_w, acc_s = unit(sides, 6 + k, acc_w, acc_s)

        def both(source, q):
            return jnp.concatenate(
                [
                    dot(left_ref[source, 2], own_ref[f, q, facing]),
                    dot(left_ref[source, 5], own_ref[f, q, 2 + facing]),
                ],
                axis=1,
            )

        acc_w = water_pairs(acc_w, *[both(f, q) for q in range(4)])
        p = both(frames, 0)
        charge = both(frames, 4)
        for k in range(128 // CHUNK):
            part = slice(k * CHUNK, (k + 1) * CHUNK)
            pk = p[part]
            root = lax.rsqrt(pk)
            u15 = root * root * root
            window = jnp.maximum(P_END - pk, 0.0)
            low = jnp.concatenate([coef_ref[2, 0, part], coef_ref[5, 0, part]], axis=1)
            high = jnp.concatenate([coef_ref[2, 1, part], coef_ref[5, 1, part]], axis=1)
            inner = u15 * (high * (u15 * u15) - low) + charge[part]
            acc_s = fold(acc_s, u15 * inner * (window * window))
        upper_row = (facing == 1).astype(F32)
        for i in range(2):
            for number, acc in ((0, acc_w), (1, acc_s)):
                mine = acc[:, i * 128 : (i + 1) * 128]
                acc_ref[f, i, number] += jnp.concatenate(
                    [mine * (1.0 - upper_row), mine * upper_row], axis=1
                )

    rec_ref[...] = rec_in_ref[...]
    self_root = P_SOFT**-0.5
    self_u15 = self_root**3
    for i in range(2):
        for f in range(frames):
            water = jnp.sum(acc_ref[f, i, 0], axis=0, keepdims=True)
            solute = jnp.sum(acc_ref[f, i, 1], axis=0, keepdims=True)
            for j in range(2):
                value = feat_ref[2 * i + j, f]
                filled = value[6:7]
                moment = value[3:4] * value[3:4] + value[4:5] * value[4:5] + value[5:6] * value[5:6]
                own = (self_u15 * P_CUT * P_CUT) * (
                    self_u15 * (self_u15 * self_u15 - 1.0) + KD * moment
                )
                fc = (2 * i + j) * frames + f
                part = slice(j * 128, (j + 1) * 128)
                rec_ref[fc, 1:2, :] = filled * (SCALE_SW * solute[:, part])
                rec_ref[fc, 2:3, :] = filled * (SCALE_WW * (water[:, part] - own))
    for i in range(2):
        block = rec_ref[8 * i : 8 * i + 8].reshape(128, 128).T
        send_ref[:, 4 * i : 4 * i + 4, :] = block.reshape(32, 4, 128)


def bin_kernel(frame_total, got_ref, out_ref):
    share = out_ref.shape[-1]
    number = lax.broadcasted_iota(jnp.int32, (share, 128), 0).astype(F32)
    for i in range(2):
        block = got_ref[:, 4 * i : 4 * i + 4, :].reshape(128, 128).T
        for j in range(2):
            totals = jnp.zeros((48, share), F32)
            for f in range(4):
                start = (j * 4 + f) * 16
                record = block[start : start + 16]
                chosen = jnp.where(number == record[13:14], 1.0, 0.0).astype(BF16)
                parts = jnp.concatenate(split3(record), axis=0).astype(BF16)
                totals = totals + lax.dot_general(
                    parts, chosen, (((1,), (1,)), ((), ())), preferred_element_type=F32
                )
            summed = totals[0:16] + totals[16:32] + totals[32:48]
            counted = summed[0:1]
            out_ref[0:1, i, j, :] = counted * (1.0 / (frame_total * rho_bulk * spacing**3))
            out_ref[1:13, i, j, :] = summed[1:13] / jnp.maximum(counted, 1.0)


def vmem():
    return pl.BlockSpec(memory_space=pltpu.VMEM)


def smem():
    return pl.BlockSpec(memory_space=pltpu.SMEM)


PARAMS = pltpu.CompilerParams(vmem_limit_bytes=48 * 1024 * 1024)


def shards(
    water_voxel, water_offset, water_angles, water_count,
    solute_frac, solute_type, type_sigma, type_well, type_charge,
):
    frames = water_voxel.shape[0]
    cols = lax.axis_size("px")
    ranks = lax.axis_size("fr")
    place = jnp.stack(
        [lax.axis_index("px"), lax.axis_index("py"), jnp.int32(cols - 1)]
    ).astype(jnp.int32)
    total = 4 * frames
    feat, side_out, comp = pl.pallas_call(
        prepare_kernel,
        out_shape=(
            jax.ShapeDtypeStruct((4, frames + 1, 8, 128), F32),
            jax.ShapeDtypeStruct((2, frames + 1, 8, 128), F32),
            jax.ShapeDtypeStruct((6, total, 128), F32),
        ),
        in_specs=[smem()] * 5 + [vmem()] * 5,
        out_specs=(vmem(),) * 3,
        scratch_shapes=[
            pltpu.VMEM((total, 8, 128), F32),
            pltpu.VMEM((total, 128), F32),
            pltpu.VMEM((8, total, 128), F32),
        ],
        compiler_params=PARAMS,
        name="prepare",
    )(place, water_count, type_sigma, type_well, type_charge,
      water_voxel, water_offset, water_angles, solute_frac, solute_type)

    side = lax.ppermute(side_out, "py", [(0, 1), (1, 0)])
    up = [(k, (k + 1) % cols) for k in range(cols)]
    down = [(k, (k - 1) % cols) for k in range(cols)]
    low = lax.ppermute(jnp.concatenate([feat[2:4], side[1:2]], axis=0), "px", up)
    high = lax.ppermute(jnp.concatenate([feat[0:2], side[0:1]], axis=0), "px", down)

    acc, rec = pl.pallas_call(
        inner_kernel,
        out_shape=(
            jax.ShapeDtypeStruct((frames, 2, 2, 8, 256), F32),
            jax.ShapeDtypeStruct((total, 16, 128), F32),
        ),
        in_specs=[vmem()] * 2,
        out_specs=(vmem(),) * 2,
        scratch_shapes=[
            pltpu.VMEM((frames + 1, 4, 128, ROWS), BF16),
            pltpu.VMEM((frames, 5, 4, ROWS, 128), BF16),
            pltpu.VMEM((4, 2, 128, 128), F32),
        ],
        compiler_params=PARAMS,
        cost_estimate=pl.CostEstimate(flops=10**9, bytes_accessed=10**6, transcendentals=0),
        name="inner",
    )(feat, comp)

    send = pl.pallas_call(
        outer_kernel,
        out_shape=jax.ShapeDtypeStruct((ranks, 8, 128), F32),
        in_specs=[smem()] + [vmem()] * 6,
        out_specs=vmem(),
        scratch_shapes=[
            pltpu.VMEM((frames + 1, 8, 128, ROWS), BF16),
            pltpu.VMEM((frames, 5, 4, ROWS, 128), BF16),
            pltpu.VMEM((8, 2, 128, 128), F32),
            pltpu.VMEM((frames, 2, 2, 8, 256), F32),
            pltpu.VMEM((total, 16, 128), F32),
        ],
        compiler_params=PARAMS,
        name="outer",
    )(place, feat, side, low, high, acc, rec)

    got = lax.all_to_all(send, "fr", 0, 0, tiled=True)
    share = CELL_XY * CELL_XY * SLAB // ranks
    return pl.pallas_call(
        functools.partial(bin_kernel, frames * ranks),
        out_shape=jax.ShapeDtypeStruct((13, 2, 2, share), F32),
        in_specs=[vmem()],
        out_specs=vmem(),
        compiler_params=PARAMS,
        name="bin",
    )(got)


def solution(mesh):
    placed = (
        P("fr", "px", "py", None),
        P("fr", "px", "py", None, None),
        P("fr", "px", "py", None, None),
        P("fr", "px", "py"),
        P("px", "py", None, None),
        P("px", "py", None),
        P(),
        P(),
        P(),
    )
    return jax.shard_map(
        shards, mesh=mesh, in_specs=placed, out_specs=P(None, "px", "py", "fr"), check_vma=False
    )
```

```python
import functools

import jax
import jax.numpy as jnp
from jax import lax
from jax.experimental import pallas as pl
from jax.experimental.pallas import tpu as pltpu
from jax.sharding import PartitionSpec as P

CELL_XY = 24
SLAB = 40
F32 = jnp.float32
BF16 = jnp.bfloat16

spacing = 0.5
soft_sq = 9.0
sigma_water = 3.1507
eps_water = 0.1521
k_dipole = 79.4
k_charge = 162.3
rho_bulk = 0.0334
pair_index = ((0, 0), (0, 1), (0, 2), (0, 3), (1, 1), (1, 2), (1, 3), (2, 2), (2, 3), (3, 3))

CUTOFF = spacing * CELL_XY
UNIT = 1.0 / sigma_water
P_SOFT = soft_sq * UNIT * UNIT
P_CUT = CUTOFF * CUTOFF * UNIT * UNIT
P_END = P_SOFT + P_CUT
KD = k_dipole / (4.0 * eps_water * sigma_water**3)
KQ = k_charge * UNIT * UNIT
SCALE_WW = 0.5 * 4.0 * eps_water / (P_CUT * P_CUT)
SCALE_SW = 1.0 / (P_CUT * P_CUT)
FAR = 1.0e4
ROWS = 64


def split3(value):
    first = value.astype(BF16).astype(F32)
    rest = value - first
    second = rest.astype(BF16).astype(F32)
    return first, second, (rest - second).astype(BF16).astype(F32)


def rows_of(parts, fill=0.0):
    lanes = parts[0].shape[1]
    missing = 8 - len(parts)
    if missing:
        parts = list(parts) + [jnp.full((missing, lanes), fill, F32)]
    return jnp.concatenate(parts, axis=0)


def sincos(angle):
    turns = jnp.floor(angle * 0.6366197723675814 + 0.5)
    rest = angle - turns * 1.5703125 - turns * 4.838267948966e-4
    square = rest * rest
    sine = rest + rest * square * (
        -1.6666654611e-1 + square * (8.3321608736e-3 - square * 1.9515295891e-4)
    )
    cosine = (
        1.0
        - 0.5 * square
        + square
        * square
        * (4.166664568298827e-2 + square * (-1.388731625493765e-3 + square * 2.443315711809948e-5))
    )
    quarter = turns.astype(jnp.int32) & 3
    odd = (quarter & 1) == 1
    sin_out = jnp.where(odd, cosine, sine)
    cos_out = jnp.where(odd, sine, cosine)
    sin_out = jnp.where(quarter >= 2, -sin_out, sin_out)
    cos_out = jnp.where((quarter == 1) | (quarter == 2), -cos_out, cos_out)
    return sin_out, cos_out


def prepare_kernel(packed_ref, feat_ref, side_ref, comp_ref, raw_ref, key_ref, sorted_ref):
    frames = feat_ref.shape[1] - 1
    pairs = 2 * frames
    offset_at, angle_at, frac_at = pairs, 4 * pairs, 7 * pairs
    type_at, count_at, table_at = frac_at + 6, frac_at + 8, frac_at + 10
    lane = lax.broadcasted_iota(jnp.int32, (1, 128), 1).astype(F32)
    for i in range(2):
        for j in range(2):
            row = slice(j, j + 1)
            for f in range(frames):
                fc = (i * 2 + j) * frames + f
                voxel = packed_ref[f * 2 + i, row, :]
                raw_ref[fc, 0:1, :] = voxel
                for axis in range(3):
                    at = (f * 2 + i) * 3 + axis
                    raw_ref[fc, 1 + axis : 2 + axis, :] = packed_ref[offset_at + at, row, :]
                    raw_ref[fc, 4 + axis : 5 + axis, :] = packed_ref[angle_at + at, row, :]
                count = packed_ref[count_at + i, row, f : f + 1]
                raw_ref[fc, 7:8, :] = jnp.where(lane < count, 1.0, 0.0).astype(F32)
                key_ref[fc : fc + 1, :] = voxel * 128.0 + lane
    total = 4 * frames
    keys = key_ref[...]
    keys_t = keys.T
    rank_iota = lax.broadcasted_iota(jnp.int32, (128, 128), 0).astype(F32)
    for fc in range(total):
        before = jnp.where(keys_t[:, fc : fc + 1] < keys[fc : fc + 1, :], 1.0, 0.0)
        rank = jnp.sum(before, axis=0, keepdims=True)
        chosen = jnp.where(rank_iota == rank, 1.0, 0.0).astype(BF16)
        parts = jnp.concatenate(split3(raw_ref[fc]), axis=0).astype(BF16)
        moved = lax.dot_general(
            parts, chosen, (((1,), (1,)), ((), ())), preferred_element_type=F32
        )
        sorted_ref[:, fc, :] = moved[0:8] + moved[8:16] + moved[16:24]

    voxel = sorted_ref[0]
    cell_x = jnp.floor((voxel + 0.5) * (1.0 / (CELL_XY * SLAB)))
    in_plane = voxel - cell_x * (CELL_XY * SLAB)
    cell_y = jnp.floor((in_plane + 0.5) * (1.0 / SLAB))
    cell_z = in_plane - cell_y * SLAB
    row = lax.broadcasted_iota(jnp.int32, (total, 128), 0)
    own_x = (row // (2 * frames)).astype(F32)
    own_y = ((row // frames) % 2).astype(F32)
    x = (spacing * (cell_x + 0.5) + sorted_ref[1] + CUTOFF * (own_x - 1.0)) * UNIT
    y = (spacing * (cell_y + 0.5) + sorted_ref[2] + CUTOFF * (own_y - 1.0)) * UNIT
    z = (spacing * (cell_z + 0.5) + sorted_ref[3] - 0.5 * spacing * SLAB) * UNIT
    sin_b, cos_b = sincos(0.5 * sorted_ref[5])
    sin_p, cos_p = sincos(0.5 * (sorted_ref[4] + sorted_ref[6]))
    sin_m, cos_m = sincos(0.5 * (sorted_ref[4] - sorted_ref[6]))
    quat_w = cos_b * cos_p
    quat_x = -sin_b * sin_m
    quat_y = sin_b * cos_m
    quat_z = cos_b * sin_p
    features = (
        x, y, z,
        2.0 * (quat_x * quat_z + quat_w * quat_y),
        2.0 * (quat_y * quat_z - quat_w * quat_x),
        1.0 - 2.0 * (quat_x * quat_x + quat_y * quat_y),
        sorted_ref[7],
    )
    for number, value in enumerate(features):
        for cell in range(4):
            feat_ref[cell, 0:frames, number, :] = value[cell * frames : (cell + 1) * frames]
    share = CELL_XY * CELL_XY * SLAB // 32
    band = (lax.broadcasted_iota(jnp.int32, (total, 128), 1) // 4 * share).astype(F32)
    for number, value in enumerate((quat_w, quat_x, quat_y, quat_z, sorted_ref[7], voxel - band)):
        comp_ref[number] = value

    table = jnp.concatenate(
        [packed_ref[table_at + k, 0:1, :] for k in range(3)] + [jnp.zeros((5, 128), F32)], axis=0
    )
    tables = jnp.concatenate(split3(table), axis=0).astype(BF16)
    for i in range(2):
        for j in range(2):
            kind = packed_ref[type_at + i, j : j + 1, :]
            chosen = jnp.where(rank_iota == kind, 1.0, 0.0).astype(BF16)
            looked = jnp.dot(tables, chosen, preferred_element_type=F32)
            looked = looked[0:8] + looked[8:16] + looked[16:24]
            sigma, well, charge = looked[0:1], looked[1:2], looked[2:3]
            ratio = 0.5 * (1.0 + sigma * UNIT)
            cube = ratio * ratio * ratio
            sixth = cube * cube
            lower = (4.0 * eps_water**0.5) * jnp.sqrt(well) * sixth
            frac_x, frac_y, frac_z = (
                packed_ref[frac_at + i * 3 + axis, j : j + 1, :] for axis in range(3)
            )
            atom_x = (frac_x * CUTOFF + CUTOFF * (i - 1.0)) * UNIT
            atom_y = (frac_y * CUTOFF + CUTOFF * (j - 1.0)) * UNIT
            atom_z = (frac_z * (spacing * SLAB) - 0.5 * spacing * SLAB) * UNIT
            feat_ref[i * 2 + j, frames] = rows_of(
                [atom_x, atom_y, atom_z, lower, lower * sixth, charge, jnp.ones((1, 128), F32)]
            )
    for cell in range(4):
        for f in range(frames):
            feat_ref[cell, f, 7:8, :] = jnp.zeros((1, 128), F32)
    facing = 1 - lax.axis_index("py")
    for i in range(2):
        side_ref[i] = feat_ref[i * 2 + facing]


def partner_rows(base):
    first, second, third = split3(base)
    number = lax.broadcasted_iota(jnp.int32, (8, 128), 0)
    ones = jnp.where(number < 3, 1.0, 0.0).astype(F32)
    stacked = jnp.concatenate(
        [first, first, first, second, second, third, ones, jnp.zeros((8, 128), F32)], axis=0
    )
    return stacked.T.astype(BF16)


def water_partner(value, shift, absent):
    x, y, z = value[0:1] + shift[0], value[1:2] + shift[1], value[2:3]
    mx, my, mz = value[3:4], value[4:5], value[5:6]
    n = x * x + y * y + z * z + FAR * ((1.0 - value[6:7]) + absent)
    e = mx * x + my * y + mz * z
    return partner_rows(jnp.concatenate([x, y, z, mx, my, mz, n, e], axis=0))


def solute_partner(value, shift, absent):
    x, y, z, charge = value[0:1] + shift[0], value[1:2] + shift[1], value[2:3], value[5:6]
    n = x * x + y * y + z * z + FAR * ((1.0 - value[6:7]) + absent)
    base = jnp.concatenate([x, y, z, charge * x, charge * y, charge * z, n, charge], axis=0)
    lower = jnp.broadcast_to(value[3:4], (128, 128)).T
    upper = jnp.broadcast_to(value[4:5], (128, 128)).T
    return partner_rows(base), lower, upper


def own_side(value):
    x, y, z = value[0:1], value[1:2], value[2:3]
    mx, my, mz = value[3:4], value[4:5], value[5:6]
    zero = jnp.zeros((1, 128), F32)
    one = jnp.ones((1, 128), F32)
    n = x * x + y * y + z * z + P_SOFT
    c = mx * x + my * y + mz * z
    kd3 = 3.0 * KD
    sides = (
        ([-2.0 * x, -2.0 * y, -2.0 * z, zero, zero, zero, one, zero], n),
        ([zero, zero, zero, KD * mx, KD * my, KD * mz, zero, zero], None),
        ([mx, my, mz, zero, zero, zero, zero, zero], -c),
        ([zero, zero, zero, -kd3 * x, -kd3 * y, -kd3 * z, zero, kd3 * one], None),
        ([zero, zero, zero, KQ * mx, KQ * my, KQ * mz, zero, -KQ * c], None),
    )
    out = []
    for rows, term in sides:
        first, second, third = split3(jnp.concatenate(rows, axis=0))
        if term is None:
            last = jnp.zeros((16, 128), F32)
        else:
            last = jnp.concatenate(list(split3(term)) + [jnp.zeros((13, 128), F32)], axis=0)
        out.append(
            jnp.concatenate([first, second, third, first, second, first, last], axis=0).astype(BF16)
        )
    return out


def fold(acc, value):
    for k in range(value.shape[0] // 8):
        acc = acc + value[8 * k : 8 * k + 8]
    return acc


CHUNK = 16


def water_pairs(acc, p, al, ao, ab):
    for k in range(p.shape[0] // CHUNK):
        part = slice(k * CHUNK, (k + 1) * CHUNK)
        pk = p[part]
        root = lax.rsqrt(pk)
        u = root * root
        u15 = u * root
        window = jnp.maximum(P_END - pk, 0.0)
        inner = u15 * (u15 * u15 - 1.0) + (al[part] - ao[part] * ab[part] * u)
        acc = fold(acc, u15 * inner * (window * window))
    return acc


def solute_pairs(acc, p, charge, lower, upper):
    for k in range(p.shape[0] // CHUNK):
        part = slice(k * CHUNK, (k + 1) * CHUNK)
        pk = p[part]
        root = lax.rsqrt(pk)
        u15 = root * root * root
        window = jnp.maximum(P_END - pk, 0.0)
        low, high = lower[part], upper[part]
        if low.shape[1] != pk.shape[1]:
            low, high = jnp.concatenate([low] * 2, axis=1), jnp.concatenate([high] * 2, axis=1)
        inner = u15 * (high * (u15 * u15) - low) + charge[part]
        acc = fold(acc, u15 * inner * (window * window))
    return acc


def dot(left, right):
    return jnp.dot(left, right, preferred_element_type=F32)


def inner_kernel(feat_ref, comp_ref, acc_ref, rec_ref, own_ref, left_ref, coef_ref):
    frames = feat_ref.shape[1] - 1
    for cell in range(4):
        rows, lower, upper = solute_partner(feat_ref[cell, frames], (0.0, 0.0), 0.0)
        left_ref[frames, cell] = rows
        coef_ref[cell, 0] = lower
        coef_ref[cell, 1] = upper
        for f in range(frames):
            left_ref[f, cell] = water_partner(feat_ref[cell, f], (0.0, 0.0), 0.0)
            for q, side in enumerate(own_side(feat_ref[cell, f])):
                own_ref[f, q, cell] = side

    @pl.loop(0, frames)
    def _(f):
        for i in range(2):
            sides = [
                jnp.concatenate([own_ref[f, q, 2 * i], own_ref[f, q, 2 * i + 1]], axis=1)
                for q in range(5)
            ]
            acc_w = jnp.zeros((8, 256), F32)
            acc_s = jnp.zeros((8, 256), F32)
            for cell in range(4):
                left = left_ref[f, cell]
                acc_w = water_pairs(acc_w, *[dot(left, sides[q]) for q in range(4)])
                left = left_ref[frames, cell]
                acc_s = solute_pairs(
                    acc_s, dot(left, sides[0]), dot(left, sides[4]), coef_ref[cell, 0], coef_ref[cell, 1]
                )
            acc_ref[f, i, 0] = acc_w
            acc_ref[f, i, 1] = acc_s

    filled = comp_ref[4]
    rows = {0: filled, 13: comp_ref[5]}
    for number, (a, b) in enumerate(pair_index):
        rows[3 + number] = comp_ref[a] * comp_ref[b] * filled
    rec_ref[...] = jnp.zeros_like(rec_ref)
    for number, value in rows.items():
        rec_ref[:, number, :] = value


def side_kernel(side_ref, own_ref, acc_in_ref, acc_ref, left_ref, coef_ref):
    frames = side_ref.shape[1] - 1
    py = lax.axis_index("py")
    facing = 1 - py
    width = 2.0 * CUTOFF * UNIT
    to_side = jnp.where(py == 0, width, -width).astype(F32)
    for cell in range(2):
        rows, lower, upper = solute_partner(side_ref[cell, frames], (0.0, to_side), 0.0)
        left_ref[frames, cell] = rows
        coef_ref[cell, 0] = lower
        coef_ref[cell, 1] = upper
        for f in range(frames):
            left_ref[f, cell] = water_partner(side_ref[cell, f], (0.0, to_side), 0.0)
    upper_row = (facing == 1).astype(F32)

    @pl.loop(0, frames)
    def _(f):
        sides = [
            jnp.concatenate([own_ref[f, q, facing], own_ref[f, q, 2 + facing]], axis=1)
            for q in range(5)
        ]
        acc_w = jnp.zeros((8, 256), F32)
        acc_s = jnp.zeros((8, 256), F32)
        for cell in range(2):
            left = left_ref[f, cell]
            acc_w = water_pairs(acc_w, *[dot(left, sides[q]) for q in range(4)])
            left = left_ref[frames, cell]
            acc_s = solute_pairs(
                acc_s, dot(left, sides[0]), dot(left, sides[4]), coef_ref[cell, 0], coef_ref[cell, 1]
            )
        for i in range(2):
            for number, acc in ((0, acc_w), (1, acc_s)):
                mine = acc[:, i * 128 : (i + 1) * 128]
                acc_ref[f, i, number] = acc_in_ref[f, i, number] + jnp.concatenate(
                    [mine * (1.0 - upper_row), mine * upper_row], axis=1
                )


def outer_kernel(
    feat_ref, low_ref, high_ref, own_ref, acc_in_ref, rec_in_ref, send_ref,
    left_ref, coef_ref, acc_ref, rec_ref,
):
    frames = feat_ref.shape[1] - 1
    px = lax.axis_index("px")
    py = lax.axis_index("py")
    last = lax.axis_size("px") - 1
    facing = 1 - py
    width = 2.0 * CUTOFF * UNIT
    to_side = jnp.where(py == 0, width, -width).astype(F32)
    no_low = jnp.where(px == 0, 1.0, 0.0).astype(F32)
    no_high = jnp.where(px == last, 1.0, 0.0).astype(F32)
    halo = [(low_ref, k, (-width, to_side if k == 2 else 0.0), no_low) for k in range(3)] + [
        (high_ref, k, (width, to_side if k == 2 else 0.0), no_high) for k in range(3)
    ]
    for cell, (ref, k, shift, absent) in enumerate(halo):
        rows, lower, upper = solute_partner(ref[k, frames], shift, absent)
        left_ref[frames, cell] = rows
        coef_ref[cell, 0] = lower
        coef_ref[cell, 1] = upper
        for f in range(frames):
            left_ref[f, cell] = water_partner(ref[k, f], shift, absent)
    upper_row = (facing == 1).astype(F32)

    @pl.loop(0, frames)
    def _(f):
        def both(source, q):
            return jnp.concatenate(
                [
                    dot(left_ref[source, 2], own_ref[f, q, facing]),
                    dot(left_ref[source, 5], own_ref[f, q, 2 + facing]),
                ],
                axis=1,
            )

        zero = jnp.zeros((8, 256), F32)
        corner_w = water_pairs(zero, *[both(f, q) for q in range(4)])
        lower, upper = (
            jnp.concatenate([coef_ref[2, k], coef_ref[5, k]], axis=1) for k in range(2)
        )
        corner_s = solute_pairs(zero, both(frames, 0), both(frames, 4), lower, upper)
        for i in range(2):
            sides = [
                jnp.concatenate([own_ref[f, q, 2 * i], own_ref[f, q, 2 * i + 1]], axis=1)
                for q in range(5)
            ]
            start = []
            for number, acc in ((0, corner_w), (1, corner_s)):
                mine = acc[:, i * 128 : (i + 1) * 128]
                start.append(
                    acc_in_ref[f, i, number]
                    + jnp.concatenate([mine * (1.0 - upper_row), mine * upper_row], axis=1)
                )
            acc_w, acc_s = start
            for cell in (3 * i, 3 * i + 1):
                left = left_ref[f, cell]
                acc_w = water_pairs(acc_w, *[dot(left, sides[q]) for q in range(4)])
                left = left_ref[frames, cell]
                acc_s = solute_pairs(
                    acc_s, dot(left, sides[0]), dot(left, sides[4]), coef_ref[cell, 0], coef_ref[cell, 1]
                )
            acc_ref[f, i, 0] = acc_w
            acc_ref[f, i, 1] = acc_s

    rec_ref[...] = rec_in_ref[...]
    self_root = P_SOFT**-0.5
    self_u15 = self_root**3
    for i in range(2):
        for f in range(frames):
            water = jnp.sum(acc_ref[f, i, 0], axis=0, keepdims=True)
            solute = jnp.sum(acc_ref[f, i, 1], axis=0, keepdims=True)
            for j in range(2):
                value = feat_ref[2 * i + j, f]
                filled = value[6:7]
                moment = value[3:4] * value[3:4] + value[4:5] * value[4:5] + value[5:6] * value[5:6]
                own = (self_u15 * P_CUT * P_CUT) * (
                    self_u15 * (self_u15 * self_u15 - 1.0) + KD * moment
                )
                fc = (2 * i + j) * frames + f
                part = slice(j * 128, (j + 1) * 128)
                rec_ref[fc, 1:2, :] = filled * (SCALE_SW * solute[:, part])
                rec_ref[fc, 2:3, :] = filled * (SCALE_WW * (water[:, part] - own))
    for i in range(2):
        block = rec_ref[8 * i : 8 * i + 8].reshape(128, 128).T
        send_ref[:, 4 * i : 4 * i + 4, :] = block.reshape(32, 4, 128)


def bin_kernel(frame_total, got_ref, out_ref):
    share = out_ref.shape[-1]
    number = lax.broadcasted_iota(jnp.int32, (share, 128), 0).astype(F32)
    for i in range(2):
        block = got_ref[:, 4 * i : 4 * i + 4, :].reshape(128, 128).T
        for j in range(2):
            totals = jnp.zeros((48, share), F32)
            for f in range(4):
                start = (j * 4 + f) * 16
                record = block[start : start + 16]
                chosen = jnp.where(number == record[13:14], 1.0, 0.0).astype(BF16)
                parts = jnp.concatenate(split3(record), axis=0).astype(BF16)
                totals = totals + lax.dot_general(
                    parts, chosen, (((1,), (1,)), ((), ())), preferred_element_type=F32
                )
            summed = totals[0:16] + totals[16:32] + totals[32:48]
            counted = summed[0:1]
            out_ref[0:1, i, j, :] = counted * (1.0 / (frame_total * rho_bulk * spacing**3))
            out_ref[1:13, i, j, :] = summed[1:13] / jnp.maximum(counted, 1.0)


def vmem():
    return pl.BlockSpec(memory_space=pltpu.VMEM)


PARAMS = pltpu.CompilerParams(vmem_limit_bytes=24 * 1024 * 1024)


def shards(
    water_voxel, water_offset, water_angles, water_count,
    solute_frac, solute_type, type_sigma, type_well, type_charge,
):
    frames = water_voxel.shape[0]
    cols = lax.axis_size("px")
    ranks = lax.axis_size("fr")
    total = 4 * frames
    rows = (-1, 2, 128)
    pieces = (
        water_voxel.reshape(rows),
        jnp.transpose(water_offset, (0, 1, 3, 2, 4)).reshape(rows),
        jnp.transpose(water_angles, (0, 1, 3, 2, 4)).reshape(rows),
        jnp.transpose(solute_frac, (0, 2, 1, 3)).reshape(rows),
        solute_type.reshape(rows),
        jnp.transpose(water_count, (1, 2, 0)),
        type_sigma.reshape(1, 1, -1), type_well.reshape(1, 1, -1), type_charge.reshape(1, 1, -1),
    )
    deep = sum(piece.shape[0] for piece in pieces)
    sums = {F32: jnp.zeros((deep, 2, 128), F32), jnp.int32: jnp.zeros((deep, 2, 128), jnp.int32)}
    start = 0
    for piece in pieces:
        size = piece.shape
        kind = F32 if piece.dtype == F32 else jnp.int32
        sums[kind] = sums[kind] + lax.pad(
            piece, jnp.zeros((), kind),
            ((start, deep - start - size[0], 0), (0, 2 - size[1], 0), (0, 128 - size[2], 0)),
        )
        start += size[0]
    packed = sums[F32] + sums[jnp.int32].astype(F32)
    feat, side_out, comp = pl.pallas_call(
        prepare_kernel,
        out_shape=(
            jax.ShapeDtypeStruct((4, frames + 1, 8, 128), F32),
            jax.ShapeDtypeStruct((2, frames + 1, 8, 128), F32),
            jax.ShapeDtypeStruct((6, total, 128), F32),
        ),
        in_specs=[vmem()],
        out_specs=(vmem(),) * 3,
        scratch_shapes=[
            pltpu.VMEM((total, 8, 128), F32),
            pltpu.VMEM((total, 128), F32),
            pltpu.VMEM((8, total, 128), F32),
        ],
        compiler_params=PARAMS,
        name="prepare",
    )(packed)

    side = lax.ppermute(side_out, "py", [(0, 1), (1, 0)])

    acc_shape = jax.ShapeDtypeStruct((frames, 2, 2, 8, 256), F32)
    acc, rec, own = pl.pallas_call(
        inner_kernel,
        out_shape=(
            acc_shape,
            jax.ShapeDtypeStruct((total, 16, 128), F32),
            jax.ShapeDtypeStruct((frames, 5, 4, ROWS, 128), BF16),
        ),
        in_specs=[vmem()] * 2,
        out_specs=(vmem(),) * 3,
        scratch_shapes=[
            pltpu.VMEM((frames + 1, 4, 128, ROWS), BF16),
            pltpu.VMEM((4, 2, 128, 128), F32),
        ],
        compiler_params=PARAMS,
        cost_estimate=pl.CostEstimate(flops=10**9, bytes_accessed=10**6, transcendentals=0),
        name="inner",
    )(feat, comp)

    side, acc = lax.optimization_barrier((side, acc))
    up = [(k, (k + 1) % cols) for k in range(cols)]
    down = [(k, (k - 1) % cols) for k in range(cols)]
    low = lax.ppermute(jnp.concatenate([feat[2:4], side[1:2]], axis=0), "px", up)
    high = lax.ppermute(jnp.concatenate([feat[0:2], side[0:1]], axis=0), "px", down)
    acc = pl.pallas_call(
        side_kernel,
        out_shape=acc_shape,
        in_specs=[vmem()] * 3,
        out_specs=vmem(),
        scratch_shapes=[
            pltpu.VMEM((frames + 1, 2, 128, ROWS), BF16),
            pltpu.VMEM((2, 2, 128, 128), F32),
        ],
        compiler_params=PARAMS,
        cost_estimate=pl.CostEstimate(flops=10**9, bytes_accessed=10**6, transcendentals=0),
        name="side",
    )(side, own, acc)

    send = pl.pallas_call(
        outer_kernel,
        out_shape=jax.ShapeDtypeStruct((ranks, 8, 128), F32),
        in_specs=[vmem()] * 6,
        out_specs=vmem(),
        scratch_shapes=[
            pltpu.VMEM((frames + 1, 6, 128, ROWS), BF16),
            pltpu.VMEM((6, 2, 128, 128), F32),
            pltpu.VMEM((frames, 2, 2, 8, 256), F32),
            pltpu.VMEM((total, 16, 128), F32),
        ],
        compiler_params=PARAMS,
        name="outer",
    )(feat, low, high, own, acc, rec)

    got = lax.all_to_all(send, "fr", 0, 0, tiled=True)
    share = CELL_XY * CELL_XY * SLAB // ranks
    return pl.pallas_call(
        functools.partial(bin_kernel, frames * ranks),
        out_shape=jax.ShapeDtypeStruct((13, 2, 2, share), F32),
        in_specs=[vmem()],
        out_specs=vmem(),
        compiler_params=PARAMS,
        name="bin",
    )(got)


def solution(mesh):
    placed = (
        P("fr", "px", "py", None),
        P("fr", "px", "py", None, None),
        P("fr", "px", "py", None, None),
        P("fr", "px", "py"),
        P("px", "py", None, None),
        P("px", "py", None),
        P(),
        P(),
        P(),
    )
    return jax.shard_map(
        shards, mesh=mesh, in_specs=placed, out_specs=P(None, "px", "py", "fr"), check_vma=False
    )
```

```python
import functools

import jax
import jax.numpy as jnp
from jax import lax
from jax.experimental import pallas as pl
from jax.experimental.pallas import tpu as pltpu
from jax.sharding import PartitionSpec as P

CELL_XY = 24
SLAB = 40
F32 = jnp.float32
BF16 = jnp.bfloat16

spacing = 0.5
soft_sq = 9.0
sigma_water = 3.1507
eps_water = 0.1521
k_dipole = 79.4
k_charge = 162.3
rho_bulk = 0.0334
pair_index = ((0, 0), (0, 1), (0, 2), (0, 3), (1, 1), (1, 2), (1, 3), (2, 2), (2, 3), (3, 3))

CUTOFF = spacing * CELL_XY
UNIT = 1.0 / sigma_water
P_SOFT = soft_sq * UNIT * UNIT
P_CUT = CUTOFF * CUTOFF * UNIT * UNIT
P_END = P_SOFT + P_CUT
KD = k_dipole / (4.0 * eps_water * sigma_water**3)
KQ = k_charge * UNIT * UNIT
SCALE_WW = 0.5 * 4.0 * eps_water / (P_CUT * P_CUT)
SCALE_SW = 1.0 / (P_CUT * P_CUT)
FAR = 1.0e4
ROWS = 64


def split3(value):
    first = value.astype(BF16).astype(F32)
    rest = value - first
    second = rest.astype(BF16).astype(F32)
    return first, second, (rest - second).astype(BF16).astype(F32)


def rows_of(parts, fill=0.0):
    lanes = parts[0].shape[1]
    missing = 8 - len(parts)
    if missing:
        parts = list(parts) + [jnp.full((missing, lanes), fill, F32)]
    return jnp.concatenate(parts, axis=0)


def sincos(angle):
    turns = jnp.floor(angle * 0.6366197723675814 + 0.5)
    rest = angle - turns * 1.5703125 - turns * 4.838267948966e-4
    square = rest * rest
    sine = rest + rest * square * (
        -1.6666654611e-1 + square * (8.3321608736e-3 - square * 1.9515295891e-4)
    )
    cosine = (
        1.0
        - 0.5 * square
        + square
        * square
        * (4.166664568298827e-2 + square * (-1.388731625493765e-3 + square * 2.443315711809948e-5))
    )
    quarter = turns.astype(jnp.int32) & 3
    odd = (quarter & 1) == 1
    sin_out = jnp.where(odd, cosine, sine)
    cos_out = jnp.where(odd, sine, cosine)
    sin_out = jnp.where(quarter >= 2, -sin_out, sin_out)
    cos_out = jnp.where((quarter == 1) | (quarter == 2), -cos_out, cos_out)
    return sin_out, cos_out


def prepare_kernel(packed_ref, feat_ref, side_ref, comp_ref, raw_ref, key_ref, sorted_ref):
    frames = feat_ref.shape[1] - 1
    pairs = 2 * frames
    offset_at, angle_at, frac_at = pairs, 4 * pairs, 7 * pairs
    type_at, count_at, table_at = frac_at + 6, frac_at + 8, frac_at + 10
    lane = lax.broadcasted_iota(jnp.int32, (1, 128), 1).astype(F32)
    for i in range(2):
        for j in range(2):
            row = slice(j, j + 1)
            for f in range(frames):
                fc = (i * 2 + j) * frames + f
                voxel = packed_ref[f * 2 + i, row, :]
                raw_ref[fc, 0:1, :] = voxel
                for axis in range(3):
                    at = (f * 2 + i) * 3 + axis
                    raw_ref[fc, 1 + axis : 2 + axis, :] = packed_ref[offset_at + at, row, :]
                    raw_ref[fc, 4 + axis : 5 + axis, :] = packed_ref[angle_at + at, row, :]
                count = packed_ref[count_at + i, row, f : f + 1]
                raw_ref[fc, 7:8, :] = jnp.where(lane < count, 1.0, 0.0).astype(F32)
                key_ref[fc : fc + 1, :] = voxel * 128.0 + lane
    total = 4 * frames
    keys = key_ref[...]
    keys_t = keys.T
    rank_iota = lax.broadcasted_iota(jnp.int32, (128, 128), 0).astype(F32)
    for fc in range(total):
        before = jnp.where(keys_t[:, fc : fc + 1] < keys[fc : fc + 1, :], 1.0, 0.0)
        rank = jnp.sum(before, axis=0, keepdims=True)
        chosen = jnp.where(rank_iota == rank, 1.0, 0.0).astype(BF16)
        parts = jnp.concatenate(split3(raw_ref[fc]), axis=0).astype(BF16)
        moved = lax.dot_general(
            parts, chosen, (((1,), (1,)), ((), ())), preferred_element_type=F32
        )
        sorted_ref[:, fc, :] = moved[0:8] + moved[8:16] + moved[16:24]

    voxel = sorted_ref[0]
    cell_x = jnp.floor((voxel + 0.5) * (1.0 / (CELL_XY * SLAB)))
    in_plane = voxel - cell_x * (CELL_XY * SLAB)
    cell_y = jnp.floor((in_plane + 0.5) * (1.0 / SLAB))
    cell_z = in_plane - cell_y * SLAB
    row = lax.broadcasted_iota(jnp.int32, (total, 128), 0)
    own_x = (row // (2 * frames)).astype(F32)
    own_y = ((row // frames) % 2).astype(F32)
    x = (spacing * (cell_x + 0.5) + sorted_ref[1] + CUTOFF * (own_x - 1.0)) * UNIT
    y = (spacing * (cell_y + 0.5) + sorted_ref[2] + CUTOFF * (own_y - 1.0)) * UNIT
    z = (spacing * (cell_z + 0.5) + sorted_ref[3] - 0.5 * spacing * SLAB) * UNIT
    sin_b, cos_b = sincos(0.5 * sorted_ref[5])
    sin_p, cos_p = sincos(0.5 * (sorted_ref[4] + sorted_ref[6]))
    sin_m, cos_m = sincos(0.5 * (sorted_ref[4] - sorted_ref[6]))
    quat_w = cos_b * cos_p
    quat_x = -sin_b * sin_m
    quat_y = sin_b * cos_m
    quat_z = cos_b * sin_p
    features = (
        x, y, z,
        2.0 * (quat_x * quat_z + quat_w * quat_y),
        2.0 * (quat_y * quat_z - quat_w * quat_x),
        1.0 - 2.0 * (quat_x * quat_x + quat_y * quat_y),
        sorted_ref[7],
    )
    for number, value in enumerate(features):
        for cell in range(4):
            feat_ref[cell, 0:frames, number, :] = value[cell * frames : (cell + 1) * frames]
    share = CELL_XY * CELL_XY * SLAB // 32
    band = (lax.broadcasted_iota(jnp.int32, (total, 128), 1) // 4 * share).astype(F32)
    for number, value in enumerate((quat_w, quat_x, quat_y, quat_z, sorted_ref[7], voxel - band)):
        comp_ref[:, number, :] = value
    comp_ref[:, 6, :] = jnp.zeros((total, 128), F32)
    comp_ref[:, 7, :] = jnp.zeros((total, 128), F32)

    table = jnp.concatenate(
        [packed_ref[table_at + k, 0:1, :] for k in range(3)] + [jnp.zeros((5, 128), F32)], axis=0
    )
    tables = jnp.concatenate(split3(table), axis=0).astype(BF16)
    for i in range(2):
        for j in range(2):
            kind = packed_ref[type_at + i, j : j + 1, :]
            chosen = jnp.where(rank_iota == kind, 1.0, 0.0).astype(BF16)
            looked = jnp.dot(tables, chosen, preferred_element_type=F32)
            looked = looked[0:8] + looked[8:16] + looked[16:24]
            sigma, well, charge = looked[0:1], looked[1:2], looked[2:3]
            ratio = 0.5 * (1.0 + sigma * UNIT)
            cube = ratio * ratio * ratio
            sixth = cube * cube
            lower = (4.0 * eps_water**0.5) * jnp.sqrt(well) * sixth
            frac_x, frac_y, frac_z = (
                packed_ref[frac_at + i * 3 + axis, j : j + 1, :] for axis in range(3)
            )
            atom_x = (frac_x * CUTOFF + CUTOFF * (i - 1.0)) * UNIT
            atom_y = (frac_y * CUTOFF + CUTOFF * (j - 1.0)) * UNIT
            atom_z = (frac_z * (spacing * SLAB) - 0.5 * spacing * SLAB) * UNIT
            feat_ref[i * 2 + j, frames] = rows_of(
                [atom_x, atom_y, atom_z, lower, lower * sixth, charge, jnp.ones((1, 128), F32)]
            )
    for cell in range(4):
        for f in range(frames):
            feat_ref[cell, f, 7:8, :] = jnp.zeros((1, 128), F32)
    facing = 1 - lax.axis_index("py")
    for i in range(2):
        side_ref[i] = feat_ref[i * 2 + facing]


def partner_rows(base):
    first, second, third = split3(base)
    number = lax.broadcasted_iota(jnp.int32, (8, 128), 0)
    ones = jnp.where(number < 3, 1.0, 0.0).astype(F32)
    return jnp.concatenate(
        [first, first, first, second, second, third, ones, jnp.zeros((8, 128), F32)], axis=0
    )


def pair_rows(base, other):
    return jnp.concatenate([partner_rows(base), partner_rows(other)], axis=0).T.astype(BF16)


def water_partner(value, shift, absent):
    x, y, z = value[0:1] + shift[0], value[1:2] + shift[1], value[2:3]
    mx, my, mz = value[3:4], value[4:5], value[5:6]
    n = x * x + y * y + z * z + FAR * ((1.0 - value[6:7]) + absent)
    e = mx * x + my * y + mz * z
    return jnp.concatenate([x, y, z, mx, my, mz, n, e], axis=0)


def solute_partner(value, shift, absent):
    x, y, z, charge = value[0:1] + shift[0], value[1:2] + shift[1], value[2:3], value[5:6]
    n = x * x + y * y + z * z + FAR * ((1.0 - value[6:7]) + absent)
    return jnp.concatenate([x, y, z, charge * x, charge * y, charge * z, n, charge], axis=0)


def solute_levels(value):
    return (jnp.broadcast_to(value[k : k + 1], (128, 128)).T for k in (3, 4))


def own_side(value):
    x, y, z = value[0:1], value[1:2], value[2:3]
    mx, my, mz = value[3:4], value[4:5], value[5:6]
    zero = jnp.zeros((1, 128), F32)
    one = jnp.ones((1, 128), F32)
    n = x * x + y * y + z * z + P_SOFT + FAR * (1.0 - value[6:7])
    c = mx * x + my * y + mz * z
    kd3 = 3.0 * KD
    sides = (
        ([-2.0 * x, -2.0 * y, -2.0 * z, zero, zero, zero, one, zero], n),
        ([zero, zero, zero, KD * mx, KD * my, KD * mz, zero, zero], None),
        ([mx, my, mz, zero, zero, zero, zero, zero], -c),
        ([zero, zero, zero, -kd3 * x, -kd3 * y, -kd3 * z, zero, kd3 * one], None),
        ([zero, zero, zero, KQ * mx, KQ * my, KQ * mz, zero, -KQ * c], None),
    )
    out = []
    for rows, term in sides:
        first, second, third = split3(jnp.concatenate(rows, axis=0))
        if term is None:
            last = jnp.zeros((16, 128), F32)
        else:
            last = jnp.concatenate(list(split3(term)) + [jnp.zeros((13, 128), F32)], axis=0)
        out.append(
            jnp.concatenate([first, second, third, first, second, first, last], axis=0).astype(BF16)
        )
    return out


def fold(acc, value):
    for k in range(value.shape[0] // 8):
        acc = acc + value[8 * k : 8 * k + 8]
    return acc


CHUNK = 16


def water_energy(p, al, ao, ab):
    root = lax.rsqrt(p)
    u = root * root
    u15 = u * root
    window = jnp.maximum(P_END - p, 0.0)
    inner = u15 * (u15 * u15 - 1.0) + (al - ao * ab * u)
    return u15 * inner * (window * window)


def solute_energy(p, charge, lower, upper):
    root = lax.rsqrt(p)
    u15 = root * root * root
    window = jnp.maximum(P_END - p, 0.0)
    inner = u15 * (upper * (u15 * u15) - lower) + charge
    return u15 * inner * (window * window)


def chunks(rows):
    return [slice(k * CHUNK, (k + 1) * CHUNK) for k in range(rows // CHUNK)]


def water_pairs(acc, values):
    for part in chunks(values[0].shape[0]):
        acc = fold(acc, water_energy(*[value[part] for value in values]))
    return acc


def solute_pairs(acc, p, charge, lower, upper):
    for part in chunks(p.shape[0]):
        low, high = lower[part], upper[part]
        if low.shape[1] != p.shape[1]:
            low, high = jnp.concatenate([low] * 2, axis=1), jnp.concatenate([high] * 2, axis=1)
        acc = fold(acc, solute_energy(p[part], charge[part], low, high))
    return acc


def dot(left, right):
    return jnp.dot(left, right, preferred_element_type=F32)


def only(side, number):
    parts = [side, jnp.zeros_like(side)]
    return jnp.concatenate(parts if number == 0 else parts[::-1], axis=0)


def each(left, right):
    top = jnp.concatenate([left, jnp.zeros_like(right)], axis=1)
    bottom = jnp.concatenate([jnp.zeros_like(left), right], axis=1)
    return jnp.concatenate([top, bottom], axis=0)


def crossed(left, right):
    top = jnp.concatenate([jnp.zeros_like(left), right], axis=1)
    bottom = jnp.concatenate([left, jnp.zeros_like(right)], axis=1)
    return jnp.concatenate([top, bottom], axis=0)


def halves_of(column, f, feat_ref):
    first, second = feat_ref[2 * column, f], feat_ref[2 * column + 1, f]
    return (
        jnp.concatenate([first[:, :64], second[:, :64]], axis=1),
        jnp.concatenate([first[:, 64:], second[:, 64:]], axis=1),
    )


def inner_kernel(feat_ref, acc_ref, other_ref, own_ref, left_ref, sum_ref):
    frames = feat_ref.shape[1] - 1
    for i in range(2):
        for f in range(frames):
            left_ref[f, i] = pair_rows(
                water_partner(feat_ref[2 * i, f], (0.0, 0.0), 0.0),
                water_partner(feat_ref[2 * i + 1, f], (0.0, 0.0), 0.0),
            )
            lower, upper = (own_side(half) for half in halves_of(i, f, feat_ref))
            for q in range(5):
                own_ref[f, q, i] = jnp.concatenate([lower[q], upper[q]], axis=1)

    @pl.loop(0, frames)
    def _(f):
        for i in range(2):
            sides = [own_ref[f, q, i] for q in range(4)]
            acc = jnp.zeros((8, 256), F32)
            left = left_ref[f, i]
            for j in range(2):
                acc = water_pairs(acc, [dot(left, only(side, j)) for side in sides])
            if i == 0:
                near = left_ref[f, 1, 0:64]
                for j in range(2):
                    values = [dot(near, only(side, j)) for side in sides]
                    for part in chunks(64):
                        energy = water_energy(*[value[part] for value in values])
                        acc = fold(acc, energy)
                        sum_ref[f, j, part] = energy[:, :128] + energy[:, 128:]
                far = left_ref[f, 1, 64:128]
                values = [dot(far, each(side[:, 128:], side[:, 128:])) for side in sides]
                late = jnp.zeros((8, 256), F32)
                for part in chunks(64):
                    energy = water_energy(*[value[part] for value in values])
                    late = fold(late, energy)
                    rows = slice(64 + part.start, 64 + part.stop)
                    sum_ref[f, 0, rows] = energy[:, :128]
                    sum_ref[f, 1, rows] = energy[:, 128:]
                acc = acc + jnp.concatenate(
                    [jnp.zeros((8, 128), F32), late[:, :128] + late[:, 128:]], axis=1
                )
            acc_ref[f, i] = acc
        for j in range(2):
            other_ref[f, j] = fold(jnp.zeros((8, 128), F32), sum_ref[f, j].T)


def to_facing():
    return jnp.where(lax.axis_index("py") == 0, 1.0, -1.0).astype(F32) * (2.0 * CUTOFF * UNIT)


def side_kernel(
    feat_ref, side_ref, own_ref, acc_ref, wall_ref, face_ref,
    solute_ref, left_ref, coef_ref,
):
    frames = side_ref.shape[1] - 1
    facing = 1 - lax.axis_index("py")
    shift = (0.0, to_facing())
    for i in range(2):
        atoms = [feat_ref[2 * i + j, frames] for j in range(2)]
        solute_ref[i] = pair_rows(*[solute_partner(value, (0.0, 0.0), 0.0) for value in atoms])
        for j in range(2):
            coef_ref[2 * i + j, 0], coef_ref[2 * i + j, 1] = solute_levels(atoms[j])
    solute_ref[2] = pair_rows(*[solute_partner(side_ref[k, frames], shift, 0.0) for k in range(2)])
    for k in range(2):
        coef_ref[4 + k, 0], coef_ref[4 + k, 1] = solute_levels(side_ref[k, frames])
    for f in range(frames):
        left_ref[f] = pair_rows(*[water_partner(side_ref[k, f], shift, 0.0) for k in range(2)])
        first, second = own_side(feat_ref[facing, f]), own_side(feat_ref[2 + facing, f])
        for q in range(5):
            face_ref[f, q] = jnp.concatenate([first[q], second[q]], axis=1)

    @pl.loop(0, frames)
    def _(f):
        for i in range(2):
            sides = [own_ref[f, q, i] for q in (0, 4)]
            acc = jnp.zeros((8, 256), F32)
            for column in range(2):
                left = solute_ref[column]
                for j in range(2):
                    cell = 2 * column + j
                    acc = solute_pairs(
                        acc, *[dot(left, only(side, j)) for side in sides],
                        coef_ref[cell, 0], coef_ref[cell, 1],
                    )
            acc_ref[f, i] = acc
        faces = [face_ref[f, q] for q in range(5)]
        water = jnp.zeros((8, 256), F32)
        solute = jnp.zeros((8, 256), F32)
        for meet, order in ((each, (4, 5)), (crossed, (5, 4))):
            sides = [meet(face[:, :128], face[:, 128:]) for face in faces]
            water = water_pairs(water, [dot(left_ref[f], side) for side in sides[:4]])
            levels = [
                jnp.concatenate([coef_ref[order[0], k], coef_ref[order[1], k]], axis=1) for k in range(2)
            ]
            solute = solute_pairs(
                solute, *[dot(solute_ref[2], sides[q]) for q in (0, 4)], *levels
            )
        wall_ref[f, 0] = water
        wall_ref[f, 1] = solute


def outer_kernel(
    feat_ref, low_ref, high_ref, own_ref, face_ref, water_ref, other_ref, solute_in_ref, wall_in_ref,
    comp_ref, send_ref, left_ref, solute_ref, coef_ref, acc_ref, wall_ref, rec_ref,
):
    frames = feat_ref.shape[1] - 1
    px = lax.axis_index("px")
    width = 2.0 * CUTOFF * UNIT
    across = to_facing()
    no_low = jnp.where(px == 0, 1.0, 0.0).astype(F32)
    no_high = jnp.where(px == lax.axis_size("px") - 1, 1.0, 0.0).astype(F32)
    low = ((-width, 0.0), no_low)
    high = ((width, 0.0), no_high)
    pairs = (
        ((low_ref, 0, *low), (low_ref, 1, *low)),
        ((high_ref, 0, *high), (high_ref, 1, *high)),
        ((low_ref, 2, (-width, across), no_low), (high_ref, 2, (width, across), no_high)),
    )
    for number, pair in enumerate(pairs):
        solute_ref[number] = pair_rows(
            *[solute_partner(ref[k, frames], shift, absent) for ref, k, shift, absent in pair]
        )
        for place, (ref, k, _, _) in enumerate(pair):
            cell = 2 * number + place
            coef_ref[cell, 0], coef_ref[cell, 1] = solute_levels(ref[k, frames])
        for f in range(frames):
            left_ref[f, number] = pair_rows(
                *[water_partner(ref[k, f], shift, absent) for ref, k, shift, absent in pair]
            )

    @pl.loop(0, frames)
    def _(f):
        faces = [face_ref[f, q] for q in range(5)]
        sides = [each(face[:, :128], face[:, 128:]) for face in faces]
        wall_ref[f, 0] = water_pairs(
            wall_in_ref[f, 0], [dot(left_ref[f, 2], side) for side in sides[:4]]
        )
        levels = [jnp.concatenate([coef_ref[4, k], coef_ref[5, k]], axis=1) for k in range(2)]
        wall_ref[f, 1] = solute_pairs(
            wall_in_ref[f, 1], *[dot(solute_ref[2], sides[q]) for q in (0, 4)], *levels
        )
        for i in range(2):
            sides = [own_ref[f, q, i] for q in range(5)]
            full, part = (slice(64, 128), slice(0, 64)) if i == 0 else (slice(0, 64), slice(64, 128))
            lanes = slice(0, 128) if i == 0 else slice(128, 256)
            water = water_ref[f, i]
            for j in range(2):
                water = water_pairs(
                    water, [dot(left_ref[f, i, full], only(side, j)) for side in sides[:4]]
                )
            late = water_pairs(
                jnp.zeros((8, 256), F32),
                [dot(left_ref[f, i, part], each(side[:, lanes], side[:, lanes])) for side in sides[:4]],
            )
            late = [late[:, :128] + late[:, 128:], jnp.zeros((8, 128), F32)]
            acc_ref[f, i, 0] = water + jnp.concatenate(late if i == 0 else late[::-1], axis=1)
            solute = solute_in_ref[f, i]
            for j in range(2):
                cell = 2 * i + j
                solute = solute_pairs(
                    solute, *[dot(solute_ref[i], only(sides[q], j)) for q in (0, 4)],
                    coef_ref[cell, 0], coef_ref[cell, 1],
                )
            acc_ref[f, i, 1] = solute

    rec_ref[...] = comp_ref[...]
    self_root = P_SOFT**-0.5
    self_u15 = self_root**3
    facing = 1 - lax.axis_index("py")
    for f in range(frames):
        walls = [jnp.sum(wall_ref[f, k], axis=0, keepdims=True) for k in range(2)]
        for i in range(2):
            sums = [jnp.sum(acc_ref[f, i, k], axis=0, keepdims=True) for k in range(2)]
            for j in range(2):
                near = (facing == j).astype(F32)
                water, solute = (
                    jnp.concatenate([value[:, 64 * j : 64 * j + 64], value[:, 128 + 64 * j : 192 + 64 * j]], axis=1)
                    + near * wall[:, 128 * i : 128 * i + 128]
                    for value, wall in zip(sums, walls)
                )
                if i == 1:
                    water = water + jnp.sum(other_ref[f, j], axis=0, keepdims=True)
                value = feat_ref[2 * i + j, f]
                filled = value[6:7]
                moment = value[3:4] * value[3:4] + value[4:5] * value[4:5] + value[5:6] * value[5:6]
                own = (self_u15 * P_CUT * P_CUT) * (
                    self_u15 * (self_u15 * self_u15 - 1.0) + KD * moment
                )
                fc = (2 * i + j) * frames + f
                rec_ref[fc, 6:7, :] = filled * (SCALE_SW * solute)
                rec_ref[fc, 7:8, :] = filled * (SCALE_WW * (water - own))
    send_ref[...] = rec_ref[...].reshape(128, 128).T.reshape(send_ref.shape)


def bin_kernel(frame_total, got_ref, out_ref, field_ref, rec_ref):
    share = out_ref.shape[-1]
    number = lax.broadcasted_iota(jnp.int32, (share, 128), 0).astype(F32)
    field_ref[...] = got_ref[...].reshape(128, 128).T.reshape(field_ref.shape)
    filled = field_ref[:, 4, :]
    quaternion = [field_ref[:, k, :] for k in range(4)]
    rec_ref[:, 0, :] = filled
    rec_ref[:, 1, :] = field_ref[:, 6, :]
    rec_ref[:, 2, :] = field_ref[:, 7, :]
    for k, (a, b) in enumerate(pair_index):
        rec_ref[:, 3 + k, :] = quaternion[a] * quaternion[b] * filled
    for k in range(13, 16):
        rec_ref[:, k, :] = jnp.zeros_like(filled)
    for i in range(2):
        for j in range(2):
            totals = jnp.zeros((48, share), F32)
            for f in range(4):
                fc = (2 * i + j) * 4 + f
                chosen = jnp.where(number == field_ref[fc, 5:6, :], 1.0, 0.0).astype(BF16)
                parts = jnp.concatenate(split3(rec_ref[fc]), axis=0).astype(BF16)
                totals = totals + lax.dot_general(
                    parts, chosen, (((1,), (1,)), ((), ())), preferred_element_type=F32
                )
            summed = totals[0:16] + totals[16:32] + totals[32:48]
            counted = summed[0:1]
            out_ref[0:1, i, j, :] = counted * (1.0 / (frame_total * rho_bulk * spacing**3))
            out_ref[1:13, i, j, :] = summed[1:13] / jnp.maximum(counted, 1.0)


def vmem():
    return pl.BlockSpec(memory_space=pltpu.VMEM)


PARAMS = pltpu.CompilerParams(vmem_limit_bytes=24 * 1024 * 1024)


def shards(
    water_voxel, water_offset, water_angles, water_count,
    solute_frac, solute_type, type_sigma, type_well, type_charge,
):
    frames = water_voxel.shape[0]
    cols = lax.axis_size("px")
    ranks = lax.axis_size("fr")
    total = 4 * frames
    rows = (-1, 2, 128)
    pieces = (
        water_voxel.reshape(rows),
        jnp.transpose(water_offset, (0, 1, 3, 2, 4)).reshape(rows),
        jnp.transpose(water_angles, (0, 1, 3, 2, 4)).reshape(rows),
        jnp.transpose(solute_frac, (0, 2, 1, 3)).reshape(rows),
        solute_type.reshape(rows),
        jnp.transpose(water_count, (1, 2, 0)),
        type_sigma.reshape(1, 1, -1), type_well.reshape(1, 1, -1), type_charge.reshape(1, 1, -1),
    )
    deep = sum(piece.shape[0] for piece in pieces)
    sums = {F32: jnp.zeros((deep, 2, 128), F32), jnp.int32: jnp.zeros((deep, 2, 128), jnp.int32)}
    start = 0
    for piece in pieces:
        size = piece.shape
        kind = F32 if piece.dtype == F32 else jnp.int32
        sums[kind] = sums[kind] + lax.pad(
            piece, jnp.zeros((), kind),
            ((start, deep - start - size[0], 0), (0, 2 - size[1], 0), (0, 128 - size[2], 0)),
        )
        start += size[0]
    packed = sums[F32] + sums[jnp.int32].astype(F32)
    feat, side_out, comp = pl.pallas_call(
        prepare_kernel,
        out_shape=(
            jax.ShapeDtypeStruct((4, frames + 1, 8, 128), F32),
            jax.ShapeDtypeStruct((2, frames + 1, 8, 128), F32),
            jax.ShapeDtypeStruct((total, 8, 128), F32),
        ),
        in_specs=[vmem()],
        out_specs=(vmem(),) * 3,
        scratch_shapes=[
            pltpu.VMEM((total, 8, 128), F32),
            pltpu.VMEM((total, 128), F32),
            pltpu.VMEM((8, total, 128), F32),
        ],
        compiler_params=PARAMS,
        name="prepare",
    )(packed)

    side = lax.ppermute(side_out, "py", [(0, 1), (1, 0)])

    work = pl.CostEstimate(flops=10**9, bytes_accessed=10**6, transcendentals=0)
    column_shape = jax.ShapeDtypeStruct((frames, 2, 8, 256), F32)
    water, other, own = pl.pallas_call(
        inner_kernel,
        out_shape=(
            column_shape,
            jax.ShapeDtypeStruct((frames, 2, 8, 128), F32),
            jax.ShapeDtypeStruct((frames, 5, 2, ROWS, 256), BF16),
        ),
        in_specs=[vmem()],
        out_specs=(vmem(),) * 3,
        scratch_shapes=[
            pltpu.VMEM((frames, 2, 128, 2 * ROWS), BF16),
            pltpu.VMEM((frames, 2, 128, 128), F32),
        ],
        compiler_params=PARAMS,
        cost_estimate=work,
        name="inner",
    )(feat)

    side, water = lax.optimization_barrier((side, water))
    up = [(k, (k + 1) % cols) for k in range(cols)]
    down = [(k, (k - 1) % cols) for k in range(cols)]
    low = lax.ppermute(jnp.concatenate([feat[2:4], side[1:2]], axis=0), "px", up)
    high = lax.ppermute(jnp.concatenate([feat[0:2], side[0:1]], axis=0), "px", down)
    solute, wall, face = pl.pallas_call(
        side_kernel,
        out_shape=(
            column_shape,
            column_shape,
            jax.ShapeDtypeStruct((frames, 5, ROWS, 256), BF16),
        ),
        in_specs=[vmem()] * 3,
        out_specs=(vmem(),) * 3,
        scratch_shapes=[
            pltpu.VMEM((3, 128, 2 * ROWS), BF16),
            pltpu.VMEM((frames, 128, 2 * ROWS), BF16),
            pltpu.VMEM((6, 2, 128, 128), F32),
        ],
        compiler_params=PARAMS,
        cost_estimate=work,
        name="side",
    )(feat, side, own)

    send = pl.pallas_call(
        outer_kernel,
        out_shape=jax.ShapeDtypeStruct((ranks, 4, 128), F32),
        in_specs=[vmem()] * 10,
        out_specs=vmem(),
        scratch_shapes=[
            pltpu.VMEM((frames, 3, 128, 2 * ROWS), BF16),
            pltpu.VMEM((3, 128, 2 * ROWS), BF16),
            pltpu.VMEM((6, 2, 128, 128), F32),
            pltpu.VMEM((frames, 2, 2, 8, 256), F32),
            pltpu.VMEM((frames, 2, 8, 256), F32),
            pltpu.VMEM((total, 8, 128), F32),
        ],
        compiler_params=PARAMS,
        name="outer",
    )(feat, low, high, own, face, water, other, solute, wall, comp)

    got = lax.all_to_all(send, "fr", 0, 0, tiled=True)
    share = CELL_XY * CELL_XY * SLAB // ranks
    return pl.pallas_call(
        functools.partial(bin_kernel, frames * ranks),
        out_shape=jax.ShapeDtypeStruct((13, 2, 2, share), F32),
        in_specs=[vmem()],
        out_specs=vmem(),
        scratch_shapes=[pltpu.VMEM((total, 8, 128), F32), pltpu.VMEM((total, 16, 128), F32)],
        compiler_params=PARAMS,
        name="bin",
    )(got)


def solution(mesh):
    placed = (
        P("fr", "px", "py", None),
        P("fr", "px", "py", None, None),
        P("fr", "px", "py", None, None),
        P("fr", "px", "py"),
        P("px", "py", None, None),
        P("px", "py", None),
        P(),
        P(),
        P(),
    )
    return jax.shard_map(
        shards, mesh=mesh, in_specs=placed, out_specs=P(None, "px", "py", "fr"), check_vma=False
    )
```

```python
import functools

import jax
import jax.numpy as jnp
from jax import lax
from jax.experimental import pallas as pl
from jax.experimental.pallas import tpu as pltpu
from jax.sharding import PartitionSpec as P

CELL_XY = 24
SLAB = 40
F32 = jnp.float32
BF16 = jnp.bfloat16

spacing = 0.5
soft_sq = 9.0
sigma_water = 3.1507
eps_water = 0.1521
k_dipole = 79.4
k_charge = 162.3
rho_bulk = 0.0334
pair_index = ((0, 0), (0, 1), (0, 2), (0, 3), (1, 1), (1, 2), (1, 3), (2, 2), (2, 3), (3, 3))

CUTOFF = spacing * CELL_XY
UNIT = 1.0 / sigma_water
P_SOFT = soft_sq * UNIT * UNIT
P_CUT = CUTOFF * CUTOFF * UNIT * UNIT
P_END = P_SOFT + P_CUT
KD = k_dipole / (4.0 * eps_water * sigma_water**3)
KQ = k_charge * UNIT * UNIT
SCALE_WW = 0.5 * 4.0 * eps_water / (P_CUT * P_CUT)
SCALE_SW = 1.0 / (P_CUT * P_CUT)
FAR = 1.0e4
ROWS = 64


def split3(value):
    first = value.astype(BF16).astype(F32)
    rest = value - first
    second = rest.astype(BF16).astype(F32)
    return first, second, (rest - second).astype(BF16).astype(F32)


def rows_of(parts, fill=0.0):
    lanes = parts[0].shape[1]
    missing = 8 - len(parts)
    if missing:
        parts = list(parts) + [jnp.full((missing, lanes), fill, F32)]
    return jnp.concatenate(parts, axis=0)


def sincos(angle):
    turns = jnp.floor(angle * 0.6366197723675814 + 0.5)
    rest = angle - turns * 1.5703125 - turns * 4.838267948966e-4
    square = rest * rest
    sine = rest + rest * square * (
        -1.6666654611e-1 + square * (8.3321608736e-3 - square * 1.9515295891e-4)
    )
    cosine = (
        1.0
        - 0.5 * square
        + square
        * square
        * (4.166664568298827e-2 + square * (-1.388731625493765e-3 + square * 2.443315711809948e-5))
    )
    quarter = turns.astype(jnp.int32) & 3
    odd = (quarter & 1) == 1
    sin_out = jnp.where(odd, cosine, sine)
    cos_out = jnp.where(odd, sine, cosine)
    sin_out = jnp.where(quarter >= 2, -sin_out, sin_out)
    cos_out = jnp.where((quarter == 1) | (quarter == 2), -cos_out, cos_out)
    return sin_out, cos_out


def prepare_kernel(packed_ref, feat_ref, side_ref, comp_ref, raw_ref, key_ref, sorted_ref):
    frames = feat_ref.shape[1] - 1
    pairs = 2 * frames
    offset_at, angle_at, frac_at = pairs, 4 * pairs, 7 * pairs
    type_at, count_at, table_at = frac_at + 6, frac_at + 8, frac_at + 10
    lane = lax.broadcasted_iota(jnp.int32, (1, 128), 1).astype(F32)
    for i in range(2):
        for j in range(2):
            row = slice(j, j + 1)
            for f in range(frames):
                fc = (i * 2 + j) * frames + f
                voxel = packed_ref[f * 2 + i, row, :]
                raw_ref[fc, 0:1, :] = voxel
                for axis in range(3):
                    at = (f * 2 + i) * 3 + axis
                    raw_ref[fc, 1 + axis : 2 + axis, :] = packed_ref[offset_at + at, row, :]
                    raw_ref[fc, 4 + axis : 5 + axis, :] = packed_ref[angle_at + at, row, :]
                count = packed_ref[count_at + i, row, f : f + 1]
                raw_ref[fc, 7:8, :] = jnp.where(lane < count, 1.0, 0.0).astype(F32)
                key_ref[fc : fc + 1, :] = voxel * 128.0 + lane
    total = 4 * frames
    keys = key_ref[...]
    keys_t = keys.T
    rank_iota = lax.broadcasted_iota(jnp.int32, (128, 128), 0).astype(F32)
    for fc in range(total):
        before = jnp.where(keys_t[:, fc : fc + 1] < keys[fc : fc + 1, :], 1.0, 0.0)
        rank = jnp.sum(before, axis=0, keepdims=True)
        chosen = jnp.where(rank_iota == rank, 1.0, 0.0).astype(BF16)
        parts = jnp.concatenate(split3(raw_ref[fc]), axis=0).astype(BF16)
        moved = lax.dot_general(
            parts, chosen, (((1,), (1,)), ((), ())), preferred_element_type=F32
        )
        sorted_ref[:, fc, :] = moved[0:8] + moved[8:16] + moved[16:24]

    voxel = sorted_ref[0]
    cell_x = jnp.floor((voxel + 0.5) * (1.0 / (CELL_XY * SLAB)))
    in_plane = voxel - cell_x * (CELL_XY * SLAB)
    cell_y = jnp.floor((in_plane + 0.5) * (1.0 / SLAB))
    cell_z = in_plane - cell_y * SLAB
    row = lax.broadcasted_iota(jnp.int32, (total, 128), 0)
    own_x = (row // (2 * frames)).astype(F32)
    own_y = ((row // frames) % 2).astype(F32)
    x = (spacing * (cell_x + 0.5) + sorted_ref[1] + CUTOFF * (own_x - 1.0)) * UNIT
    y = (spacing * (cell_y + 0.5) + sorted_ref[2] + CUTOFF * (own_y - 1.0)) * UNIT
    z = (spacing * (cell_z + 0.5) + sorted_ref[3] - 0.5 * spacing * SLAB) * UNIT
    sin_b, cos_b = sincos(0.5 * sorted_ref[5])
    sin_p, cos_p = sincos(0.5 * (sorted_ref[4] + sorted_ref[6]))
    sin_m, cos_m = sincos(0.5 * (sorted_ref[4] - sorted_ref[6]))
    quat_w = cos_b * cos_p
    quat_x = -sin_b * sin_m
    quat_y = sin_b * cos_m
    quat_z = cos_b * sin_p
    features = (
        x, y, z,
        2.0 * (quat_x * quat_z + quat_w * quat_y),
        2.0 * (quat_y * quat_z - quat_w * quat_x),
        1.0 - 2.0 * (quat_x * quat_x + quat_y * quat_y),
        sorted_ref[7],
    )
    for number, value in enumerate(features):
        for cell in range(4):
            feat_ref[cell, 0:frames, number, :] = value[cell * frames : (cell + 1) * frames]
    share = CELL_XY * CELL_XY * SLAB // 32
    band = (lax.broadcasted_iota(jnp.int32, (total, 128), 1) // 4 * share).astype(F32)
    for number, value in enumerate((quat_w, quat_x, quat_y, quat_z, sorted_ref[7], voxel - band)):
        comp_ref[:, number, :] = value
    comp_ref[:, 6, :] = jnp.zeros((total, 128), F32)
    comp_ref[:, 7, :] = jnp.zeros((total, 128), F32)

    table = jnp.concatenate(
        [packed_ref[table_at + k, 0:1, :] for k in range(3)] + [jnp.zeros((5, 128), F32)], axis=0
    )
    tables = jnp.concatenate(split3(table), axis=0).astype(BF16)
    for i in range(2):
        for j in range(2):
            kind = packed_ref[type_at + i, j : j + 1, :]
            chosen = jnp.where(rank_iota == kind, 1.0, 0.0).astype(BF16)
            looked = jnp.dot(tables, chosen, preferred_element_type=F32)
            looked = looked[0:8] + looked[8:16] + looked[16:24]
            sigma, well, charge = looked[0:1], looked[1:2], looked[2:3]
            ratio = 0.5 * (1.0 + sigma * UNIT)
            cube = ratio * ratio * ratio
            sixth = cube * cube
            lower = (4.0 * eps_water**0.5) * jnp.sqrt(well) * sixth
            frac_x, frac_y, frac_z = (
                packed_ref[frac_at + i * 3 + axis, j : j + 1, :] for axis in range(3)
            )
            atom_x = (frac_x * CUTOFF + CUTOFF * (i - 1.0)) * UNIT
            atom_y = (frac_y * CUTOFF + CUTOFF * (j - 1.0)) * UNIT
            atom_z = (frac_z * (spacing * SLAB) - 0.5 * spacing * SLAB) * UNIT
            feat_ref[i * 2 + j, frames] = rows_of(
                [atom_x, atom_y, atom_z, lower, lower * sixth, charge, jnp.ones((1, 128), F32)]
            )
    for cell in range(4):
        for f in range(frames):
            feat_ref[cell, f, 7:8, :] = jnp.zeros((1, 128), F32)
    facing = 1 - lax.axis_index("py")
    for i in range(2):
        side_ref[i] = feat_ref[i * 2 + facing]


def partner_rows(base):
    first, second, third = split3(base)
    number = lax.broadcasted_iota(jnp.int32, (8, 128), 0)
    ones = jnp.where(number < 3, 1.0, 0.0).astype(F32)
    return jnp.concatenate(
        [first, first, first, second, second, third, ones, jnp.zeros((8, 128), F32)], axis=0
    )


def pair_rows(base, other):
    return jnp.concatenate([partner_rows(base), partner_rows(other)], axis=0).T.astype(BF16)


def water_partner(value, shift, absent):
    x, y, z = value[0:1] + shift[0], value[1:2] + shift[1], value[2:3]
    mx, my, mz = value[3:4], value[4:5], value[5:6]
    n = x * x + y * y + z * z + FAR * ((1.0 - value[6:7]) + absent)
    e = mx * x + my * y + mz * z
    return jnp.concatenate([x, y, z, mx, my, mz, n, e], axis=0)


def solute_partner(value, shift, absent):
    x, y, z, charge = value[0:1] + shift[0], value[1:2] + shift[1], value[2:3], value[5:6]
    n = x * x + y * y + z * z + FAR * ((1.0 - value[6:7]) + absent)
    return jnp.concatenate([x, y, z, charge * x, charge * y, charge * z, n, charge], axis=0)


def solute_levels(value):
    return (jnp.broadcast_to(value[k : k + 1], (128, 128)).T for k in (3, 4))


def own_side(value):
    x, y, z = value[0:1], value[1:2], value[2:3]
    mx, my, mz = value[3:4], value[4:5], value[5:6]
    zero = jnp.zeros((1, 128), F32)
    one = jnp.ones((1, 128), F32)
    n = x * x + y * y + z * z + P_SOFT + FAR * (1.0 - value[6:7])
    c = mx * x + my * y + mz * z
    kd3 = 3.0 * KD
    sides = (
        ([-2.0 * x, -2.0 * y, -2.0 * z, zero, zero, zero, one, zero], n),
        ([zero, zero, zero, KD * mx, KD * my, KD * mz, zero, zero], None),
        ([mx, my, mz, zero, zero, zero, zero, zero], -c),
        ([zero, zero, zero, -kd3 * x, -kd3 * y, -kd3 * z, zero, kd3 * one], None),
        ([zero, zero, zero, KQ * mx, KQ * my, KQ * mz, zero, -KQ * c], None),
    )
    out = []
    for rows, term in sides:
        first, second, third = split3(jnp.concatenate(rows, axis=0))
        if term is None:
            last = jnp.zeros((16, 128), F32)
        else:
            last = jnp.concatenate(list(split3(term)) + [jnp.zeros((13, 128), F32)], axis=0)
        out.append(
            jnp.concatenate([first, second, third, first, second, first, last], axis=0).astype(BF16)
        )
    return out


def fold(acc, value):
    for k in range(value.shape[0] // 8):
        acc = acc + value[8 * k : 8 * k + 8]
    return acc


CHUNK = 16


def water_energy(p, al, ao, ab):
    root = lax.rsqrt(p)
    u = root * root
    u15 = u * root
    window = jnp.maximum(P_END - p, 0.0)
    inner = u15 * (u15 * u15 - 1.0) + (al - ao * ab * u)
    return u15 * inner * (window * window)


def solute_energy(p, charge, lower, upper):
    root = lax.rsqrt(p)
    u15 = root * root * root
    window = jnp.maximum(P_END - p, 0.0)
    inner = u15 * (upper * (u15 * u15) - lower) + charge
    return u15 * inner * (window * window)


def chunks(rows):
    return [slice(k * CHUNK, (k + 1) * CHUNK) for k in range(rows // CHUNK)]


def water_pairs(acc, values):
    for part in chunks(values[0].shape[0]):
        acc = fold(acc, water_energy(*[value[part] for value in values]))
    return acc


def solute_pairs(acc, p, charge, lower, upper):
    for part in chunks(p.shape[0]):
        low, high = lower[part], upper[part]
        if low.shape[1] != p.shape[1]:
            low, high = jnp.concatenate([low] * 2, axis=1), jnp.concatenate([high] * 2, axis=1)
        acc = fold(acc, solute_energy(p[part], charge[part], low, high))
    return acc


def dot(left, right):
    return jnp.dot(left, right, preferred_element_type=F32)


def only(side, number):
    parts = [side, jnp.zeros_like(side)]
    return jnp.concatenate(parts if number == 0 else parts[::-1], axis=0)


def each(left, right):
    top = jnp.concatenate([left, jnp.zeros_like(right)], axis=1)
    bottom = jnp.concatenate([jnp.zeros_like(left), right], axis=1)
    return jnp.concatenate([top, bottom], axis=0)


def crossed(left, right):
    top = jnp.concatenate([jnp.zeros_like(left), right], axis=1)
    bottom = jnp.concatenate([left, jnp.zeros_like(right)], axis=1)
    return jnp.concatenate([top, bottom], axis=0)


def halves_of(column, f, feat_ref):
    first, second = feat_ref[2 * column, f], feat_ref[2 * column + 1, f]
    return (
        jnp.concatenate([first[:, :64], second[:, :64]], axis=1),
        jnp.concatenate([first[:, 64:], second[:, 64:]], axis=1),
    )


def inner_kernel(feat_ref, acc_ref, other_ref, own_ref, left_ref, sum_ref):
    frames = feat_ref.shape[1] - 1
    for i in range(2):
        for f in range(frames):
            left_ref[f, i] = pair_rows(
                water_partner(feat_ref[2 * i, f], (0.0, 0.0), 0.0),
                water_partner(feat_ref[2 * i + 1, f], (0.0, 0.0), 0.0),
            )
            lower, upper = (own_side(half) for half in halves_of(i, f, feat_ref))
            for q in range(5):
                own_ref[f, q, i] = jnp.concatenate([lower[q], upper[q]], axis=1)

    @pl.loop(0, frames)
    def _(f):
        for i in range(2):
            sides = [own_ref[f, q, i] for q in range(4)]
            acc = jnp.zeros((8, 256), F32)
            left = left_ref[f, i]
            for j in range(2):
                acc = water_pairs(acc, [dot(left, only(side, j)) for side in sides])
            if i == 0:
                near = left_ref[f, 1, 0:64]
                for j in range(2):
                    values = [dot(near, only(side, j)) for side in sides]
                    for part in chunks(64):
                        energy = water_energy(*[value[part] for value in values])
                        acc = fold(acc, energy)
                        sum_ref[f, j, part] = energy[:, :128] + energy[:, 128:]
                far = left_ref[f, 1, 64:128]
                values = [dot(far, each(side[:, 128:], side[:, 128:])) for side in sides]
                late = jnp.zeros((8, 256), F32)
                for part in chunks(64):
                    energy = water_energy(*[value[part] for value in values])
                    late = fold(late, energy)
                    rows = slice(64 + part.start, 64 + part.stop)
                    sum_ref[f, 0, rows] = energy[:, :128]
                    sum_ref[f, 1, rows] = energy[:, 128:]
                acc = acc + jnp.concatenate(
                    [jnp.zeros((8, 128), F32), late[:, :128] + late[:, 128:]], axis=1
                )
            acc_ref[f, i] = acc
        for j in range(2):
            other_ref[f, j] = fold(jnp.zeros((8, 128), F32), sum_ref[f, j].T)


def to_facing():
    return jnp.where(lax.axis_index("py") == 0, 1.0, -1.0).astype(F32) * (2.0 * CUTOFF * UNIT)


def side_kernel(
    feat_ref, side_ref, own_ref, acc_ref, wall_ref, face_ref,
    solute_ref, left_ref, coef_ref,
):
    frames = side_ref.shape[1] - 1
    facing = 1 - lax.axis_index("py")
    shift = (0.0, to_facing())
    for i in range(2):
        atoms = [feat_ref[2 * i + j, frames] for j in range(2)]
        solute_ref[i] = pair_rows(*[solute_partner(value, (0.0, 0.0), 0.0) for value in atoms])
        for j in range(2):
            coef_ref[2 * i + j, 0], coef_ref[2 * i + j, 1] = solute_levels(atoms[j])
    solute_ref[2] = pair_rows(*[solute_partner(side_ref[k, frames], shift, 0.0) for k in range(2)])
    for k in range(2):
        coef_ref[4 + k, 0], coef_ref[4 + k, 1] = solute_levels(side_ref[k, frames])
    for f in range(frames):
        left_ref[f] = pair_rows(*[water_partner(side_ref[k, f], shift, 0.0) for k in range(2)])
        first, second = own_side(feat_ref[facing, f]), own_side(feat_ref[2 + facing, f])
        for q in range(5):
            face_ref[f, q] = jnp.concatenate([first[q], second[q]], axis=1)

    @pl.loop(0, frames)
    def _(f):
        for i in range(2):
            sides = [own_ref[f, q, i] for q in (0, 4)]
            acc = jnp.zeros((8, 256), F32)
            for column in range(2):
                left = solute_ref[column]
                for j in range(2):
                    cell = 2 * column + j
                    acc = solute_pairs(
                        acc, *[dot(left, only(side, j)) for side in sides],
                        coef_ref[cell, 0], coef_ref[cell, 1],
                    )
            acc_ref[f, i] = acc
        faces = [face_ref[f, q] for q in range(5)]
        water = jnp.zeros((8, 256), F32)
        solute = jnp.zeros((8, 256), F32)
        for meet, order in ((each, (4, 5)), (crossed, (5, 4))):
            sides = [meet(face[:, :128], face[:, 128:]) for face in faces]
            water = water_pairs(water, [dot(left_ref[f], side) for side in sides[:4]])
            levels = [
                jnp.concatenate([coef_ref[order[0], k], coef_ref[order[1], k]], axis=1) for k in range(2)
            ]
            solute = solute_pairs(
                solute, *[dot(solute_ref[2], sides[q]) for q in (0, 4)], *levels
            )
        wall_ref[f, 0] = water
        wall_ref[f, 1] = solute


def outer_kernel(
    feat_ref, low_ref, high_ref, own_ref, face_ref, water_ref, other_ref, solute_in_ref, wall_in_ref,
    comp_ref, send_ref, left_ref, solute_ref, coef_ref, acc_ref, wall_ref, rec_ref,
):
    frames = feat_ref.shape[1] - 1
    px = lax.axis_index("px")
    width = 2.0 * CUTOFF * UNIT
    across = to_facing()
    no_low = jnp.where(px == 0, 1.0, 0.0).astype(F32)
    no_high = jnp.where(px == lax.axis_size("px") - 1, 1.0, 0.0).astype(F32)
    low = ((-width, 0.0), no_low)
    high = ((width, 0.0), no_high)
    pairs = (
        ((low_ref, 0, *low), (low_ref, 1, *low)),
        ((high_ref, 0, *high), (high_ref, 1, *high)),
        ((low_ref, 2, (-width, across), no_low), (high_ref, 2, (width, across), no_high)),
    )
    for number, pair in enumerate(pairs):
        solute_ref[number] = pair_rows(
            *[solute_partner(ref[k, frames], shift, absent) for ref, k, shift, absent in pair]
        )
        for place, (ref, k, _, _) in enumerate(pair):
            cell = 2 * number + place
            coef_ref[cell, 0], coef_ref[cell, 1] = solute_levels(ref[k, frames])
        for f in range(frames):
            left_ref[f, number] = pair_rows(
                *[water_partner(ref[k, f], shift, absent) for ref, k, shift, absent in pair]
            )

    @pl.loop(0, frames)
    def _(f):
        faces = [face_ref[f, q] for q in range(5)]
        sides = [each(face[:, :128], face[:, 128:]) for face in faces]
        wall_ref[f, 0] = water_pairs(
            wall_in_ref[f, 0], [dot(left_ref[f, 2], side) for side in sides[:4]]
        )
        levels = [jnp.concatenate([coef_ref[4, k], coef_ref[5, k]], axis=1) for k in range(2)]
        wall_ref[f, 1] = solute_pairs(
            wall_in_ref[f, 1], *[dot(solute_ref[2], sides[q]) for q in (0, 4)], *levels
        )
        for i in range(2):
            sides = [own_ref[f, q, i] for q in range(5)]
            full, part = (slice(64, 128), slice(0, 64)) if i == 0 else (slice(0, 64), slice(64, 128))
            lanes = slice(0, 128) if i == 0 else slice(128, 256)
            water = water_ref[f, i]
            for j in range(2):
                water = water_pairs(
                    water, [dot(left_ref[f, i, full], only(side, j)) for side in sides[:4]]
                )
            late = water_pairs(
                jnp.zeros((8, 256), F32),
                [dot(left_ref[f, i, part], each(side[:, lanes], side[:, lanes])) for side in sides[:4]],
            )
            late = [late[:, :128] + late[:, 128:], jnp.zeros((8, 128), F32)]
            acc_ref[f, i, 0] = water + jnp.concatenate(late if i == 0 else late[::-1], axis=1)
            solute = solute_in_ref[f, i]
            for j in range(2):
                cell = 2 * i + j
                solute = solute_pairs(
                    solute, *[dot(solute_ref[i], only(sides[q], j)) for q in (0, 4)],
                    coef_ref[cell, 0], coef_ref[cell, 1],
                )
            acc_ref[f, i, 1] = solute

    rec_ref[...] = comp_ref[...]
    self_root = P_SOFT**-0.5
    self_u15 = self_root**3
    facing = 1 - lax.axis_index("py")
    for f in range(frames):
        walls = [jnp.sum(wall_ref[f, k], axis=0, keepdims=True) for k in range(2)]
        for i in range(2):
            sums = [jnp.sum(acc_ref[f, i, k], axis=0, keepdims=True) for k in range(2)]
            for j in range(2):
                near = (facing == j).astype(F32)
                water, solute = (
                    jnp.concatenate([value[:, 64 * j : 64 * j + 64], value[:, 128 + 64 * j : 192 + 64 * j]], axis=1)
                    + near * wall[:, 128 * i : 128 * i + 128]
                    for value, wall in zip(sums, walls)
                )
                if i == 1:
                    water = water + jnp.sum(other_ref[f, j], axis=0, keepdims=True)
                value = feat_ref[2 * i + j, f]
                filled = value[6:7]
                moment = value[3:4] * value[3:4] + value[4:5] * value[4:5] + value[5:6] * value[5:6]
                own = (self_u15 * P_CUT * P_CUT) * (
                    self_u15 * (self_u15 * self_u15 - 1.0) + KD * moment
                )
                fc = (2 * i + j) * frames + f
                rec_ref[fc, 6:7, :] = filled * (SCALE_SW * solute)
                rec_ref[fc, 7:8, :] = filled * (SCALE_WW * (water - own))
    send_ref[...] = rec_ref[...].reshape(128, 128).T.reshape(send_ref.shape)


def bin_kernel(frame_total, got_ref, out_ref, field_ref, rec_ref):
    share = out_ref.shape[-1]
    groups = -(-share // 128)
    number = lax.broadcasted_iota(jnp.int32, (128, 128), 0).astype(F32)
    field_ref[...] = got_ref[...].reshape(128, 128).T.reshape(field_ref.shape)
    filled = field_ref[:, 4, :]
    quaternion = [field_ref[:, k, :] for k in range(4)]
    rec_ref[:, 0, :] = filled
    rec_ref[:, 1, :] = field_ref[:, 6, :]
    rec_ref[:, 2, :] = field_ref[:, 7, :]
    for k, (a, b) in enumerate(pair_index):
        rec_ref[:, 3 + k, :] = quaternion[a] * quaternion[b] * filled
    for k in range(13, 16):
        rec_ref[:, k, :] = jnp.zeros_like(filled)
    for i in range(2):
        for j in range(2):
            totals = jnp.zeros((48 * groups, 128), F32)
            for f in range(4):
                fc = (2 * i + j) * 4 + f
                voxel = field_ref[fc, 5:6, :]
                group = jnp.floor((voxel + 0.5) * (1.0 / 128.0))
                chosen = jnp.where(number == voxel - 128.0 * group, 1.0, 0.0).astype(BF16)
                parts = jnp.concatenate(split3(rec_ref[fc]), axis=0)
                parts = jnp.concatenate(
                    [jnp.where(group == k, parts, 0.0) for k in range(groups)], axis=0
                ).astype(BF16)
                totals = totals + lax.dot_general(
                    parts, chosen, (((1,), (1,)), ((), ())), preferred_element_type=F32
                )
            for k in range(groups):
                lanes = min(128, share - 128 * k)
                part = totals[48 * k : 48 * k + 48]
                summed = (part[0:16] + part[16:32] + part[32:48])[:, :lanes]
                counted = summed[0:1]
                span = slice(128 * k, 128 * k + lanes)
                out_ref[0:1, i, j, span] = counted * (1.0 / (frame_total * rho_bulk * spacing**3))
                out_ref[1:13, i, j, span] = summed[1:13] / jnp.maximum(counted, 1.0)


def vmem():
    return pl.BlockSpec(memory_space=pltpu.VMEM)


PARAMS = pltpu.CompilerParams(vmem_limit_bytes=24 * 1024 * 1024)


def shards(
    water_voxel, water_offset, water_angles, water_count,
    solute_frac, solute_type, type_sigma, type_well, type_charge,
):
    frames = water_voxel.shape[0]
    cols = lax.axis_size("px")
    ranks = lax.axis_size("fr")
    total = 4 * frames
    rows = (-1, 2, 128)
    pieces = (
        water_voxel.reshape(rows),
        jnp.transpose(water_offset, (0, 1, 3, 2, 4)).reshape(rows),
        jnp.transpose(water_angles, (0, 1, 3, 2, 4)).reshape(rows),
        jnp.transpose(solute_frac, (0, 2, 1, 3)).reshape(rows),
        solute_type.reshape(rows),
        jnp.transpose(water_count, (1, 2, 0)),
        type_sigma.reshape(1, 1, -1), type_well.reshape(1, 1, -1), type_charge.reshape(1, 1, -1),
    )
    deep = sum(piece.shape[0] for piece in pieces)
    sums = {F32: jnp.zeros((deep, 2, 128), F32), jnp.int32: jnp.zeros((deep, 2, 128), jnp.int32)}
    start = 0
    for piece in pieces:
        size = piece.shape
        kind = F32 if piece.dtype == F32 else jnp.int32
        sums[kind] = sums[kind] + lax.pad(
            piece, jnp.zeros((), kind),
            ((start, deep - start - size[0], 0), (0, 2 - size[1], 0), (0, 128 - size[2], 0)),
        )
        start += size[0]
    packed = sums[F32] + sums[jnp.int32].astype(F32)
    feat, side_out, comp = pl.pallas_call(
        prepare_kernel,
        out_shape=(
            jax.ShapeDtypeStruct((4, frames + 1, 8, 128), F32),
            jax.ShapeDtypeStruct((2, frames + 1, 8, 128), F32),
            jax.ShapeDtypeStruct((total, 8, 128), F32),
        ),
        in_specs=[vmem()],
        out_specs=(vmem(),) * 3,
        scratch_shapes=[
            pltpu.VMEM((total, 8, 128), F32),
            pltpu.VMEM((total, 128), F32),
            pltpu.VMEM((8, total, 128), F32),
        ],
        compiler_params=PARAMS,
        name="prepare",
    )(packed)

    side = lax.ppermute(side_out, "py", [(0, 1), (1, 0)])

    work = pl.CostEstimate(flops=10**9, bytes_accessed=10**6, transcendentals=0)
    column_shape = jax.ShapeDtypeStruct((frames, 2, 8, 256), F32)
    water, other, own = pl.pallas_call(
        inner_kernel,
        out_shape=(
            column_shape,
            jax.ShapeDtypeStruct((frames, 2, 8, 128), F32),
            jax.ShapeDtypeStruct((frames, 5, 2, ROWS, 256), BF16),
        ),
        in_specs=[vmem()],
        out_specs=(vmem(),) * 3,
        scratch_shapes=[
            pltpu.VMEM((frames, 2, 128, 2 * ROWS), BF16),
            pltpu.VMEM((frames, 2, 128, 128), F32),
        ],
        compiler_params=PARAMS,
        cost_estimate=work,
        name="inner",
    )(feat)

    side, water = lax.optimization_barrier((side, water))
    up = [(k, (k + 1) % cols) for k in range(cols)]
    down = [(k, (k - 1) % cols) for k in range(cols)]
    low = lax.ppermute(jnp.concatenate([feat[2:4], side[1:2]], axis=0), "px", up)
    high = lax.ppermute(jnp.concatenate([feat[0:2], side[0:1]], axis=0), "px", down)
    solute, wall, face = pl.pallas_call(
        side_kernel,
        out_shape=(
            column_shape,
            column_shape,
            jax.ShapeDtypeStruct((frames, 5, ROWS, 256), BF16),
        ),
        in_specs=[vmem()] * 3,
        out_specs=(vmem(),) * 3,
        scratch_shapes=[
            pltpu.VMEM((3, 128, 2 * ROWS), BF16),
            pltpu.VMEM((frames, 128, 2 * ROWS), BF16),
            pltpu.VMEM((6, 2, 128, 128), F32),
        ],
        compiler_params=PARAMS,
        cost_estimate=work,
        name="side",
    )(feat, side, own)

    send = pl.pallas_call(
        outer_kernel,
        out_shape=jax.ShapeDtypeStruct((ranks, 4, 128), F32),
        in_specs=[vmem()] * 10,
        out_specs=vmem(),
        scratch_shapes=[
            pltpu.VMEM((frames, 3, 128, 2 * ROWS), BF16),
            pltpu.VMEM((3, 128, 2 * ROWS), BF16),
            pltpu.VMEM((6, 2, 128, 128), F32),
            pltpu.VMEM((frames, 2, 2, 8, 256), F32),
            pltpu.VMEM((frames, 2, 8, 256), F32),
            pltpu.VMEM((total, 8, 128), F32),
        ],
        compiler_params=PARAMS,
        name="outer",
    )(feat, low, high, own, face, water, other, solute, wall, comp)

    got = lax.all_to_all(send, "fr", 0, 0, tiled=True)
    share = CELL_XY * CELL_XY * SLAB // ranks
    return pl.pallas_call(
        functools.partial(bin_kernel, frames * ranks),
        out_shape=jax.ShapeDtypeStruct((13, 2, 2, share), F32),
        in_specs=[vmem()],
        out_specs=vmem(),
        scratch_shapes=[pltpu.VMEM((total, 8, 128), F32), pltpu.VMEM((total, 16, 128), F32)],
        compiler_params=PARAMS,
        name="bin",
    )(got)


def solution(mesh):
    placed = (
        P("fr", "px", "py", None),
        P("fr", "px", "py", None, None),
        P("fr", "px", "py", None, None),
        P("fr", "px", "py"),
        P("px", "py", None, None),
        P("px", "py", None),
        P(),
        P(),
        P(),
    )
    return jax.shard_map(
        shards, mesh=mesh, in_specs=placed, out_specs=P(None, "px", "py", "fr"), check_vma=False
    )
```

```python
import functools

import jax
import jax.numpy as jnp
from jax import lax
from jax.experimental import pallas as pl
from jax.experimental.pallas import tpu as pltpu
from jax.sharding import PartitionSpec as P

CELL_XY = 24
SLAB = 40
F32 = jnp.float32
BF16 = jnp.bfloat16

spacing = 0.5
soft_sq = 9.0
sigma_water = 3.1507
eps_water = 0.1521
k_dipole = 79.4
k_charge = 162.3
rho_bulk = 0.0334
pair_index = ((0, 0), (0, 1), (0, 2), (0, 3), (1, 1), (1, 2), (1, 3), (2, 2), (2, 3), (3, 3))

CUTOFF = spacing * CELL_XY
UNIT = 1.0 / sigma_water
P_SOFT = soft_sq * UNIT * UNIT
P_CUT = CUTOFF * CUTOFF * UNIT * UNIT
P_END = P_SOFT + P_CUT
KD = k_dipole / (4.0 * eps_water * sigma_water**3)
KQ = k_charge * UNIT * UNIT
SCALE_WW = 0.5 * 4.0 * eps_water / (P_CUT * P_CUT)
SCALE_SW = 1.0 / (P_CUT * P_CUT)
FAR = 1.0e4
MONO = 96
P_ROWS, Q_ROWS, M_ROWS = slice(0, 64), slice(64, 128), slice(128, 224)
OWN_ROWS, HELD_ROWS = 224, 320
ROWS = 64


def split3(value):
    first = value.astype(BF16).astype(F32)
    rest = value - first
    second = rest.astype(BF16).astype(F32)
    return first, second, (rest - second).astype(BF16).astype(F32)


def rows_of(parts, fill=0.0):
    lanes = parts[0].shape[1]
    missing = 8 - len(parts)
    if missing:
        parts = list(parts) + [jnp.full((missing, lanes), fill, F32)]
    return jnp.concatenate(parts, axis=0)


def sincos(angle):
    turns = jnp.floor(angle * 0.6366197723675814 + 0.5)
    rest = angle - turns * 1.5703125 - turns * 4.838267948966e-4
    square = rest * rest
    sine = rest + rest * square * (
        -1.6666654611e-1 + square * (8.3321608736e-3 - square * 1.9515295891e-4)
    )
    cosine = (
        1.0
        - 0.5 * square
        + square
        * square
        * (4.166664568298827e-2 + square * (-1.388731625493765e-3 + square * 2.443315711809948e-5))
    )
    quarter = turns.astype(jnp.int32) & 3
    odd = (quarter & 1) == 1
    sin_out = jnp.where(odd, cosine, sine)
    cos_out = jnp.where(odd, sine, cosine)
    sin_out = jnp.where(quarter >= 2, -sin_out, sin_out)
    cos_out = jnp.where((quarter == 1) | (quarter == 2), -cos_out, cos_out)
    return sin_out, cos_out


def prepare_kernel(packed_ref, feat_ref, side_ref, comp_ref, raw_ref, key_ref, sorted_ref):
    frames = feat_ref.shape[1] - 1
    pairs = 2 * frames
    offset_at, angle_at, frac_at = pairs, 4 * pairs, 7 * pairs
    type_at, count_at, table_at = frac_at + 6, frac_at + 8, frac_at + 10
    lane = lax.broadcasted_iota(jnp.int32, (1, 128), 1).astype(F32)
    for i in range(2):
        for j in range(2):
            row = slice(j, j + 1)
            for f in range(frames):
                fc = (i * 2 + j) * frames + f
                voxel = packed_ref[f * 2 + i, row, :]
                raw_ref[fc, 0:1, :] = voxel
                for axis in range(3):
                    at = (f * 2 + i) * 3 + axis
                    raw_ref[fc, 1 + axis : 2 + axis, :] = packed_ref[offset_at + at, row, :]
                    raw_ref[fc, 4 + axis : 5 + axis, :] = packed_ref[angle_at + at, row, :]
                count = packed_ref[count_at + i, row, f : f + 1]
                raw_ref[fc, 7:8, :] = jnp.where(lane < count, 1.0, 0.0).astype(F32)
                key_ref[fc : fc + 1, :] = voxel * 128.0 + lane
    total = 4 * frames
    keys = key_ref[...]
    keys_t = keys.T
    rank_iota = lax.broadcasted_iota(jnp.int32, (128, 128), 0).astype(F32)
    for fc in range(total):
        before = jnp.where(keys_t[:, fc : fc + 1] < keys[fc : fc + 1, :], 1.0, 0.0)
        rank = jnp.sum(before, axis=0, keepdims=True)
        chosen = jnp.where(rank_iota == rank, 1.0, 0.0).astype(BF16)
        parts = jnp.concatenate(split3(raw_ref[fc]), axis=0).astype(BF16)
        moved = lax.dot_general(
            parts, chosen, (((1,), (1,)), ((), ())), preferred_element_type=F32
        )
        sorted_ref[:, fc, :] = moved[0:8] + moved[8:16] + moved[16:24]

    voxel = sorted_ref[0]
    cell_x = jnp.floor((voxel + 0.5) * (1.0 / (CELL_XY * SLAB)))
    in_plane = voxel - cell_x * (CELL_XY * SLAB)
    cell_y = jnp.floor((in_plane + 0.5) * (1.0 / SLAB))
    cell_z = in_plane - cell_y * SLAB
    row = lax.broadcasted_iota(jnp.int32, (total, 128), 0)
    own_x = (row // (2 * frames)).astype(F32)
    own_y = ((row // frames) % 2).astype(F32)
    x = (spacing * (cell_x + 0.5) + sorted_ref[1] + CUTOFF * (own_x - 1.0)) * UNIT
    y = (spacing * (cell_y + 0.5) + sorted_ref[2] + CUTOFF * (own_y - 1.0)) * UNIT
    z = (spacing * (cell_z + 0.5) + sorted_ref[3] - 0.5 * spacing * SLAB) * UNIT
    sin_b, cos_b = sincos(0.5 * sorted_ref[5])
    sin_p, cos_p = sincos(0.5 * (sorted_ref[4] + sorted_ref[6]))
    sin_m, cos_m = sincos(0.5 * (sorted_ref[4] - sorted_ref[6]))
    quat_w = cos_b * cos_p
    quat_x = -sin_b * sin_m
    quat_y = sin_b * cos_m
    quat_z = cos_b * sin_p
    features = (
        x, y, z,
        2.0 * (quat_x * quat_z + quat_w * quat_y),
        2.0 * (quat_y * quat_z - quat_w * quat_x),
        1.0 - 2.0 * (quat_x * quat_x + quat_y * quat_y),
        sorted_ref[7],
    )
    for number, value in enumerate(features):
        for cell in range(4):
            feat_ref[cell, 0:frames, number, :] = value[cell * frames : (cell + 1) * frames]
    share = CELL_XY * CELL_XY * SLAB // 32
    band = (lax.broadcasted_iota(jnp.int32, (total, 128), 1) // 4 * share).astype(F32)
    for number, value in enumerate((quat_w, quat_x, quat_y, quat_z, sorted_ref[7], voxel - band)):
        comp_ref[:, number, :] = value
    comp_ref[:, 6, :] = jnp.zeros((total, 128), F32)
    comp_ref[:, 7, :] = jnp.zeros((total, 128), F32)

    table = jnp.concatenate(
        [packed_ref[table_at + k, 0:1, :] for k in range(3)] + [jnp.zeros((5, 128), F32)], axis=0
    )
    tables = jnp.concatenate(split3(table), axis=0).astype(BF16)
    for i in range(2):
        for j in range(2):
            kind = packed_ref[type_at + i, j : j + 1, :]
            chosen = jnp.where(rank_iota == kind, 1.0, 0.0).astype(BF16)
            looked = jnp.dot(tables, chosen, preferred_element_type=F32)
            looked = looked[0:8] + looked[8:16] + looked[16:24]
            sigma, well, charge = looked[0:1], looked[1:2], looked[2:3]
            ratio = 0.5 * (1.0 + sigma * UNIT)
            cube = ratio * ratio * ratio
            sixth = cube * cube
            lower = (4.0 * eps_water**0.5) * jnp.sqrt(well) * sixth
            frac_x, frac_y, frac_z = (
                packed_ref[frac_at + i * 3 + axis, j : j + 1, :] for axis in range(3)
            )
            atom_x = (frac_x * CUTOFF + CUTOFF * (i - 1.0)) * UNIT
            atom_y = (frac_y * CUTOFF + CUTOFF * (j - 1.0)) * UNIT
            atom_z = (frac_z * (spacing * SLAB) - 0.5 * spacing * SLAB) * UNIT
            feat_ref[i * 2 + j, frames] = rows_of(
                [atom_x, atom_y, atom_z, lower, lower * sixth, charge, jnp.ones((1, 128), F32)]
            )
    for cell in range(4):
        for f in range(frames):
            feat_ref[cell, f, 7:8, :] = jnp.zeros((1, 128), F32)
    facing = 1 - lax.axis_index("py")
    for i in range(2):
        side_ref[i] = feat_ref[i * 2 + facing]


def partner_rows(base):
    first, second, third = split3(base)
    number = lax.broadcasted_iota(jnp.int32, (8, 128), 0)
    ones = jnp.where(number < 3, 1.0, 0.0).astype(F32)
    return jnp.concatenate(
        [first, first, first, second, second, third, ones, jnp.zeros((8, 128), F32)], axis=0
    )


def pair_rows(base, other):
    return jnp.concatenate([partner_rows(base), partner_rows(other)], axis=0).astype(BF16).T


def moment_rows(base, other):
    parts = []
    for value in (base, other):
        first, second, third = split3(value)
        parts += [first, first, first, second, second, third]
    return jnp.concatenate(parts, axis=0).astype(BF16).T


def moved_water(value, shift):
    x, y, z = value[0:1] + shift[0], value[1:2] + shift[1], value[2:3]
    return (x, y, z), (value[3:4], value[4:5], value[5:6])


def water_partner(value, shift, absent):
    (x, y, z), _ = moved_water(value, shift)
    n = x * x + y * y + z * z + FAR * ((1.0 - value[6:7]) + absent)
    zero = jnp.zeros((3, 128), F32)
    return jnp.concatenate([x, y, z, zero, n, zero[0:1]], axis=0)


def moment_partner(value, shift):
    place, moment = moved_water(value, shift)
    n = place[0] * place[0] + place[1] * place[1] + place[2] * place[2]
    e = moment[0] * place[0] + moment[1] * place[1] + moment[2] * place[2]
    rows = [moment[a] * n - 3.0 * place[a] * e for a in range(3)] + list(moment)
    rows += [3.0 * place[a] * moment[b] - 2.0 * moment[a] * place[b] for a in range(3) for b in range(3)]
    return jnp.concatenate(rows + [3.0 * e], axis=0)


def own_moments(value):
    place = (value[0:1], value[1:2], value[2:3])
    moment = (value[3:4], value[4:5], value[5:6])
    n = place[0] * place[0] + place[1] * place[1] + place[2] * place[2] + P_SOFT
    c = moment[0] * place[0] + moment[1] * place[1] + moment[2] * place[2]
    rows = list(moment) + [moment[a] * n - 3.0 * c * place[a] for a in range(3)]
    rows += [moment[a] * place[b] for a in range(3) for b in range(3)]
    first, second, third = split3(KD * jnp.concatenate(rows + [c], axis=0))
    return jnp.concatenate([first, second, third, first, second, first], axis=0).astype(BF16)


def solute_partner(value, shift, absent):
    x, y, z, charge = value[0:1] + shift[0], value[1:2] + shift[1], value[2:3], value[5:6]
    n = x * x + y * y + z * z + FAR * ((1.0 - value[6:7]) + absent)
    return jnp.concatenate([x, y, z, charge * x, charge * y, charge * z, n, charge], axis=0)


def solute_levels(value):
    return (jnp.broadcast_to(value[k : k + 1], (128, 128)).T for k in (3, 4))


def own_side(value):
    x, y, z = value[0:1], value[1:2], value[2:3]
    mx, my, mz = value[3:4], value[4:5], value[5:6]
    zero = jnp.zeros((1, 128), F32)
    one = jnp.ones((1, 128), F32)
    n = x * x + y * y + z * z + P_SOFT + FAR * (1.0 - value[6:7])
    c = mx * x + my * y + mz * z
    sides = (
        ([-2.0 * x, -2.0 * y, -2.0 * z, zero, zero, zero, one, zero], n),
        ([zero, zero, zero, KQ * mx, KQ * my, KQ * mz, zero, -KQ * c], None),
    )
    out = []
    for rows, term in sides:
        first, second, third = split3(jnp.concatenate(rows, axis=0))
        if term is None:
            last = jnp.zeros((16, 128), F32)
        else:
            last = jnp.concatenate(list(split3(term)) + [jnp.zeros((13, 128), F32)], axis=0)
        out += [first, second, third, first, second, first, last]
    return jnp.concatenate([jnp.concatenate(out, axis=0).astype(BF16), own_moments(value)], axis=0)


def run_frames(frames, set_up, frame):
    set_up(0)
    for f in range(frames):
        if f + 1 < frames:
            set_up(f + 1)
        frame(f)


def fold(acc, value):
    for k in range(value.shape[0] // 8):
        acc = acc + value[8 * k : 8 * k + 8]
    return acc


CHUNK = 16


def water_energy(p, moments):
    root = lax.rsqrt(p)
    u = root * root
    u15 = u * root
    window = jnp.maximum(P_END - p, 0.0)
    inner = u15 * (u15 * u15 - 1.0) + moments * u
    return u15 * inner * (window * window)


def solute_energy(p, charge, lower, upper):
    root = lax.rsqrt(p)
    u15 = root * root * root
    window = jnp.maximum(P_END - p, 0.0)
    inner = u15 * (upper * (u15 * u15) - lower) + charge
    return u15 * inner * (window * window)


def chunks(rows):
    return [slice(k * CHUNK, (k + 1) * CHUNK) for k in range(rows // CHUNK)]


def water_pairs(acc, values):
    for part in chunks(values[0].shape[0]):
        acc = fold(acc, water_energy(*[value[part] for value in values]))
    return acc


def solute_pairs(acc, p, charge, lower, upper):
    for part in chunks(p.shape[0]):
        low, high = lower[part], upper[part]
        if low.shape[1] != p.shape[1]:
            low, high = jnp.concatenate([low] * 2, axis=1), jnp.concatenate([high] * 2, axis=1)
        acc = fold(acc, solute_energy(p[part], charge[part], low, high))
    return acc


def dot(left, right):
    return jnp.dot(left, right, preferred_element_type=F32)


def only(side, number):
    parts = [side, jnp.zeros_like(side)]
    return jnp.concatenate(parts if number == 0 else parts[::-1], axis=0)


def each(left, right):
    top = jnp.concatenate([left, jnp.zeros_like(right)], axis=1)
    bottom = jnp.concatenate([jnp.zeros_like(left), right], axis=1)
    return jnp.concatenate([top, bottom], axis=0)


def crossed(left, right):
    top = jnp.concatenate([jnp.zeros_like(left), right], axis=1)
    bottom = jnp.concatenate([left, jnp.zeros_like(right)], axis=1)
    return jnp.concatenate([top, bottom], axis=0)


def halves_of(column, f, feat_ref):
    first, second = feat_ref[2 * column, f], feat_ref[2 * column + 1, f]
    return (
        jnp.concatenate([first[:, :64], second[:, :64]], axis=1),
        jnp.concatenate([first[:, 64:], second[:, 64:]], axis=1),
    )


def inner_kernel(feat_ref, acc_ref, other_ref, own_ref, left_ref, mono_ref, sum_ref):
    frames = feat_ref.shape[1] - 1
    def set_up(f):
        for i in range(2):
            left_ref[f, i] = pair_rows(
                *[water_partner(feat_ref[2 * i + j, f], (0.0, 0.0), 0.0) for j in range(2)]
            )
            mono_ref[f, i] = moment_rows(
                *[moment_partner(feat_ref[2 * i + j, f], (0.0, 0.0)) for j in range(2)]
            )
            own_ref[f, i, 0:OWN_ROWS] = jnp.concatenate(
                [own_side(half) for half in halves_of(i, f, feat_ref)], axis=1
            )

    def frame(f):
        for i in range(2):
            sides = (own_ref[f, i, P_ROWS], own_ref[f, i, M_ROWS])
            acc = jnp.zeros((8, 256), F32)
            lefts = (left_ref[f, i], mono_ref[f, i])
            for j in range(2):
                acc = water_pairs(acc, [dot(left, only(side, j)) for left, side in zip(lefts, sides)])
            if i == 0:
                near = (left_ref[f, 1, 0:64], mono_ref[f, 1, 0:64])
                for j in range(2):
                    values = [dot(left, only(side, j)) for left, side in zip(near, sides)]
                    for part in chunks(64):
                        energy = water_energy(*[value[part] for value in values])
                        acc = fold(acc, energy)
                        sum_ref[f, j, part] = energy[:, :128] + energy[:, 128:]
                far = (left_ref[f, 1, 64:128], mono_ref[f, 1, 64:128])
                values = [
                    dot(left, each(side[:, 128:], side[:, 128:])) for left, side in zip(far, sides)
                ]
                late = jnp.zeros((8, 256), F32)
                for part in chunks(64):
                    energy = water_energy(*[value[part] for value in values])
                    late = fold(late, energy)
                    rows = slice(64 + part.start, 64 + part.stop)
                    sum_ref[f, 0, rows] = energy[:, :128]
                    sum_ref[f, 1, rows] = energy[:, 128:]
                acc = acc + jnp.concatenate(
                    [jnp.zeros((8, 128), F32), late[:, :128] + late[:, 128:]], axis=1
                )
            acc_ref[f, i] = acc
        for j in range(2):
            other_ref[f, j] = fold(jnp.zeros((8, 128), F32), sum_ref[f, j].T)

    run_frames(frames, set_up, frame)


def to_facing():
    return jnp.where(lax.axis_index("py") == 0, 1.0, -1.0).astype(F32) * (2.0 * CUTOFF * UNIT)


def side_kernel(
    feat_ref, side_ref, own_ref, acc_ref, wall_ref, face_ref,
    solute_ref, left_ref, mono_ref, coef_ref,
):
    frames = side_ref.shape[1] - 1
    facing = 1 - lax.axis_index("py")
    shift = (0.0, to_facing())
    for i in range(2):
        atoms = [feat_ref[2 * i + j, frames] for j in range(2)]
        solute_ref[i] = pair_rows(*[solute_partner(value, (0.0, 0.0), 0.0) for value in atoms])
        for j in range(2):
            coef_ref[2 * i + j, 0], coef_ref[2 * i + j, 1] = solute_levels(atoms[j])
    solute_ref[2] = pair_rows(*[solute_partner(side_ref[k, frames], shift, 0.0) for k in range(2)])
    for k in range(2):
        coef_ref[4 + k, 0], coef_ref[4 + k, 1] = solute_levels(side_ref[k, frames])
    def set_up(f):
        left_ref[f] = pair_rows(*[water_partner(side_ref[k, f], shift, 0.0) for k in range(2)])
        mono_ref[f] = moment_rows(*[moment_partner(side_ref[k, f], shift) for k in range(2)])
        face_ref[f, 0:OWN_ROWS] = jnp.concatenate(
            [own_side(feat_ref[facing, f]), own_side(feat_ref[2 + facing, f])], axis=1
        )

    def frame(f):
        for i in range(2):
            sides = [own_ref[f, i, P_ROWS], own_ref[f, i, Q_ROWS]]
            acc = jnp.zeros((8, 256), F32)
            for column in range(2):
                left = solute_ref[column]
                for j in range(2):
                    cell = 2 * column + j
                    acc = solute_pairs(
                        acc, *[dot(left, only(side, j)) for side in sides],
                        coef_ref[cell, 0], coef_ref[cell, 1],
                    )
            acc_ref[f, i] = acc
        faces = [face_ref[f, rows] for rows in (P_ROWS, Q_ROWS, M_ROWS)]
        water = jnp.zeros((8, 256), F32)
        solute = jnp.zeros((8, 256), F32)
        for meet, order in ((each, (4, 5)), (crossed, (5, 4))):
            sides = [meet(face[:, :128], face[:, 128:]) for face in faces]
            water = water_pairs(water, [dot(left_ref[f], sides[0]), dot(mono_ref[f], sides[2])])
            levels = [
                jnp.concatenate([coef_ref[order[0], k], coef_ref[order[1], k]], axis=1) for k in range(2)
            ]
            solute = solute_pairs(
                solute, *[dot(solute_ref[2], sides[q]) for q in range(2)], *levels
            )
        wall_ref[f, 0] = water
        wall_ref[f, 1] = solute

    run_frames(frames, set_up, frame)


def outer_kernel(
    feat_ref, low_ref, high_ref, own_ref, face_ref, water_ref, other_ref, solute_in_ref, wall_in_ref,
    comp_ref, send_ref, left_ref, mono_ref, solute_ref, coef_ref, acc_ref, wall_ref, rec_ref,
):
    frames = feat_ref.shape[1] - 1
    px = lax.axis_index("px")
    width = 2.0 * CUTOFF * UNIT
    across = to_facing()
    no_low = jnp.where(px == 0, 1.0, 0.0).astype(F32)
    no_high = jnp.where(px == lax.axis_size("px") - 1, 1.0, 0.0).astype(F32)
    low = ((-width, 0.0), no_low)
    high = ((width, 0.0), no_high)
    pairs = (
        ((low_ref, 0, *low), (low_ref, 1, *low)),
        ((high_ref, 0, *high), (high_ref, 1, *high)),
        ((low_ref, 2, (-width, across), no_low), (high_ref, 2, (width, across), no_high)),
    )
    for number, pair in enumerate(pairs):
        solute_ref[number] = pair_rows(
            *[solute_partner(ref[k, frames], shift, absent) for ref, k, shift, absent in pair]
        )
        for place, (ref, k, _, _) in enumerate(pair):
            cell = 2 * number + place
            coef_ref[cell, 0], coef_ref[cell, 1] = solute_levels(ref[k, frames])

    def set_up(f):
        for number, pair in enumerate(pairs):
            left_ref[f, number] = pair_rows(
                *[water_partner(ref[k, f], shift, absent) for ref, k, shift, absent in pair]
            )
            mono_ref[f, number] = moment_rows(
                *[moment_partner(ref[k, f], shift) for ref, k, shift, _ in pair]
            )

    def frame(f):
        faces = [face_ref[f, rows] for rows in (P_ROWS, Q_ROWS, M_ROWS)]
        sides = [each(face[:, :128], face[:, 128:]) for face in faces]
        wall_ref[f, 0] = water_pairs(
            wall_in_ref[f, 0], [dot(left_ref[f, 2], sides[0]), dot(mono_ref[f, 2], sides[2])]
        )
        levels = [jnp.concatenate([coef_ref[4, k], coef_ref[5, k]], axis=1) for k in range(2)]
        wall_ref[f, 1] = solute_pairs(
            wall_in_ref[f, 1], *[dot(solute_ref[2], sides[q]) for q in range(2)], *levels
        )
        for i in range(2):
            sides = [own_ref[f, i, rows] for rows in (P_ROWS, Q_ROWS, M_ROWS)]
            full, part = (slice(64, 128), slice(0, 64)) if i == 0 else (slice(0, 64), slice(64, 128))
            lanes = slice(0, 128) if i == 0 else slice(128, 256)
            water = water_ref[f, i]
            for j in range(2):
                water = water_pairs(
                    water,
                    [
                        dot(left_ref[f, i, full], only(sides[0], j)),
                        dot(mono_ref[f, i, full], only(sides[2], j)),
                    ],
                )
            late = water_pairs(
                jnp.zeros((8, 256), F32),
                [
                    dot(left_ref[f, i, part], each(sides[0][:, lanes], sides[0][:, lanes])),
                    dot(mono_ref[f, i, part], each(sides[2][:, lanes], sides[2][:, lanes])),
                ],
            )
            late = [late[:, :128] + late[:, 128:], jnp.zeros((8, 128), F32)]
            acc_ref[f, i, 0] = water + jnp.concatenate(late if i == 0 else late[::-1], axis=1)
            solute = solute_in_ref[f, i]
            for j in range(2):
                cell = 2 * i + j
                solute = solute_pairs(
                    solute, *[dot(solute_ref[i], only(sides[q], j)) for q in range(2)],
                    coef_ref[cell, 0], coef_ref[cell, 1],
                )
            acc_ref[f, i, 1] = solute

    run_frames(frames, set_up, frame)
    rec_ref[...] = comp_ref[...]
    self_root = P_SOFT**-0.5
    self_u15 = self_root**3
    facing = 1 - lax.axis_index("py")
    for f in range(frames):
        walls = [jnp.sum(wall_ref[f, k], axis=0, keepdims=True) for k in range(2)]
        for i in range(2):
            sums = [jnp.sum(acc_ref[f, i, k], axis=0, keepdims=True) for k in range(2)]
            for j in range(2):
                near = (facing == j).astype(F32)
                water, solute = (
                    jnp.concatenate([value[:, 64 * j : 64 * j + 64], value[:, 128 + 64 * j : 192 + 64 * j]], axis=1)
                    + near * wall[:, 128 * i : 128 * i + 128]
                    for value, wall in zip(sums, walls)
                )
                if i == 1:
                    water = water + jnp.sum(other_ref[f, j], axis=0, keepdims=True)
                value = feat_ref[2 * i + j, f]
                filled = value[6:7]
                moment = value[3:4] * value[3:4] + value[4:5] * value[4:5] + value[5:6] * value[5:6]
                own = (self_u15 * P_CUT * P_CUT) * (
                    self_u15 * (self_u15 * self_u15 - 1.0) + KD * moment
                )
                fc = (2 * i + j) * frames + f
                rec_ref[fc, 6:7, :] = filled * (SCALE_SW * solute)
                rec_ref[fc, 7:8, :] = filled * (SCALE_WW * (water - own))
    send_ref[...] = rec_ref[...].reshape(128, 128).T.reshape(send_ref.shape)


def bin_kernel(frame_total, got_ref, out_ref, field_ref, rec_ref):
    share = out_ref.shape[-1]
    groups = -(-share // 128)
    number = lax.broadcasted_iota(jnp.int32, (128, 128), 0).astype(F32)
    field_ref[...] = got_ref[...].reshape(128, 128).T.reshape(field_ref.shape)
    filled = field_ref[:, 4, :]
    quaternion = [field_ref[:, k, :] for k in range(4)]
    rec_ref[:, 0, :] = filled
    rec_ref[:, 1, :] = field_ref[:, 6, :]
    rec_ref[:, 2, :] = field_ref[:, 7, :]
    for k, (a, b) in enumerate(pair_index):
        rec_ref[:, 3 + k, :] = quaternion[a] * quaternion[b] * filled
    for k in range(13, 16):
        rec_ref[:, k, :] = jnp.zeros_like(filled)
    for i in range(2):
        for j in range(2):
            totals = jnp.zeros((48 * groups, 128), F32)
            for f in range(4):
                fc = (2 * i + j) * 4 + f
                voxel = field_ref[fc, 5:6, :]
                group = jnp.floor((voxel + 0.5) * (1.0 / 128.0))
                chosen = jnp.where(number == voxel - 128.0 * group, 1.0, 0.0).astype(BF16)
                parts = jnp.concatenate(split3(rec_ref[fc]), axis=0)
                parts = jnp.concatenate(
                    [jnp.where(group == k, parts, 0.0) for k in range(groups)], axis=0
                ).astype(BF16)
                totals = totals + lax.dot_general(
                    parts, chosen, (((1,), (1,)), ((), ())), preferred_element_type=F32
                )
            for k in range(groups):
                lanes = min(128, share - 128 * k)
                part = totals[48 * k : 48 * k + 48]
                summed = (part[0:16] + part[16:32] + part[32:48])[:, :lanes]
                counted = summed[0:1]
                span = slice(128 * k, 128 * k + lanes)
                out_ref[0:1, i, j, span] = counted * (1.0 / (frame_total * rho_bulk * spacing**3))
                out_ref[1:13, i, j, span] = summed[1:13] / jnp.maximum(counted, 1.0)


def vmem():
    return pl.BlockSpec(memory_space=pltpu.VMEM)


PARAMS = pltpu.CompilerParams(vmem_limit_bytes=24 * 1024 * 1024)


def shards(
    water_voxel, water_offset, water_angles, water_count,
    solute_frac, solute_type, type_sigma, type_well, type_charge,
):
    frames = water_voxel.shape[0]
    cols = lax.axis_size("px")
    ranks = lax.axis_size("fr")
    total = 4 * frames
    rows = (-1, 2, 128)
    pieces = (
        water_voxel.reshape(rows),
        jnp.transpose(water_offset, (0, 1, 3, 2, 4)).reshape(rows),
        jnp.transpose(water_angles, (0, 1, 3, 2, 4)).reshape(rows),
        jnp.transpose(solute_frac, (0, 2, 1, 3)).reshape(rows),
        solute_type.reshape(rows),
        jnp.transpose(water_count, (1, 2, 0)),
        type_sigma.reshape(1, 1, -1), type_well.reshape(1, 1, -1), type_charge.reshape(1, 1, -1),
    )
    deep = sum(piece.shape[0] for piece in pieces)
    sums = {F32: jnp.zeros((deep, 2, 128), F32), jnp.int32: jnp.zeros((deep, 2, 128), jnp.int32)}
    start = 0
    for piece in pieces:
        size = piece.shape
        kind = F32 if piece.dtype == F32 else jnp.int32
        sums[kind] = sums[kind] + lax.pad(
            piece, jnp.zeros((), kind),
            ((start, deep - start - size[0], 0), (0, 2 - size[1], 0), (0, 128 - size[2], 0)),
        )
        start += size[0]
    packed = sums[F32] + sums[jnp.int32].astype(F32)
    feat, side_out, comp = pl.pallas_call(
        prepare_kernel,
        out_shape=(
            jax.ShapeDtypeStruct((4, frames + 1, 8, 128), F32),
            jax.ShapeDtypeStruct((2, frames + 1, 8, 128), F32),
            jax.ShapeDtypeStruct((total, 8, 128), F32),
        ),
        in_specs=[vmem()],
        out_specs=(vmem(),) * 3,
        scratch_shapes=[
            pltpu.VMEM((total, 8, 128), F32),
            pltpu.VMEM((total, 128), F32),
            pltpu.VMEM((8, total, 128), F32),
        ],
        compiler_params=PARAMS,
        name="prepare",
    )(packed)

    side = lax.ppermute(side_out, "py", [(0, 1), (1, 0)])

    work = pl.CostEstimate(flops=10**9, bytes_accessed=10**6, transcendentals=0)
    column_shape = jax.ShapeDtypeStruct((frames, 2, 8, 256), F32)
    water, other, own = pl.pallas_call(
        inner_kernel,
        out_shape=(
            column_shape,
            jax.ShapeDtypeStruct((frames, 2, 8, 128), F32),
            jax.ShapeDtypeStruct((frames, 2, HELD_ROWS, 256), BF16),
        ),
        in_specs=[vmem()],
        out_specs=(vmem(),) * 3,
        scratch_shapes=[
            pltpu.VMEM((frames, 2, 128, 2 * ROWS), BF16),
            pltpu.VMEM((frames, 2, 128, 2 * MONO), BF16),
            pltpu.VMEM((frames, 2, 128, 128), F32),
        ],
        compiler_params=PARAMS,
        cost_estimate=work,
        name="inner",
    )(feat)

    side, water = lax.optimization_barrier((side, water))
    up = [(k, (k + 1) % cols) for k in range(cols)]
    down = [(k, (k - 1) % cols) for k in range(cols)]
    low = lax.ppermute(jnp.concatenate([feat[2:4], side[1:2]], axis=0), "px", up)
    high = lax.ppermute(jnp.concatenate([feat[0:2], side[0:1]], axis=0), "px", down)
    solute, wall, face = pl.pallas_call(
        side_kernel,
        out_shape=(
            column_shape,
            column_shape,
            jax.ShapeDtypeStruct((frames, HELD_ROWS, 256), BF16),
        ),
        in_specs=[vmem()] * 3,
        out_specs=(vmem(),) * 3,
        scratch_shapes=[
            pltpu.VMEM((3, 128, 2 * ROWS), BF16),
            pltpu.VMEM((frames, 128, 2 * ROWS), BF16),
            pltpu.VMEM((frames, 128, 2 * MONO), BF16),
            pltpu.VMEM((6, 2, 128, 128), F32),
        ],
        compiler_params=PARAMS,
        cost_estimate=work,
        name="side",
    )(feat, side, own)

    send = pl.pallas_call(
        outer_kernel,
        out_shape=jax.ShapeDtypeStruct((ranks, 4, 128), F32),
        in_specs=[vmem()] * 10,
        out_specs=vmem(),
        scratch_shapes=[
            pltpu.VMEM((frames, 3, 128, 2 * ROWS), BF16),
            pltpu.VMEM((frames, 3, 128, 2 * MONO), BF16),
            pltpu.VMEM((3, 128, 2 * ROWS), BF16),
            pltpu.VMEM((6, 2, 128, 128), F32),
            pltpu.VMEM((frames, 2, 2, 8, 256), F32),
            pltpu.VMEM((frames, 2, 8, 256), F32),
            pltpu.VMEM((total, 8, 128), F32),
        ],
        compiler_params=PARAMS,
        name="outer",
    )(feat, low, high, own, face, water, other, solute, wall, comp)

    got = lax.all_to_all(send, "fr", 0, 0, tiled=True)
    share = CELL_XY * CELL_XY * SLAB // ranks
    return pl.pallas_call(
        functools.partial(bin_kernel, frames * ranks),
        out_shape=jax.ShapeDtypeStruct((13, 2, 2, share), F32),
        in_specs=[vmem()],
        out_specs=vmem(),
        scratch_shapes=[pltpu.VMEM((total, 8, 128), F32), pltpu.VMEM((total, 16, 128), F32)],
        compiler_params=PARAMS,
        name="bin",
    )(got)


def solution(mesh):
    placed = (
        P("fr", "px", "py", None),
        P("fr", "px", "py", None, None),
        P("fr", "px", "py", None, None),
        P("fr", "px", "py"),
        P("px", "py", None, None),
        P("px", "py", None),
        P(),
        P(),
        P(),
    )
    return jax.shard_map(
        shards, mesh=mesh, in_specs=placed, out_specs=P(None, "px", "py", "fr"), check_vma=False
    )
```

```python
import functools

import jax
import jax.numpy as jnp
from jax import lax
from jax.experimental import pallas as pl
from jax.experimental.pallas import tpu as pltpu
from jax.sharding import PartitionSpec as P

CELL_XY = 24
SLAB = 40
F32 = jnp.float32
BF16 = jnp.bfloat16

spacing = 0.5
soft_sq = 9.0
sigma_water = 3.1507
eps_water = 0.1521
k_dipole = 79.4
k_charge = 162.3
rho_bulk = 0.0334
pair_index = ((0, 0), (0, 1), (0, 2), (0, 3), (1, 1), (1, 2), (1, 3), (2, 2), (2, 3), (3, 3))

CUTOFF = spacing * CELL_XY
UNIT = 1.0 / sigma_water
P_SOFT = soft_sq * UNIT * UNIT
P_CUT = CUTOFF * CUTOFF * UNIT * UNIT
P_END = P_SOFT + P_CUT
KD = k_dipole / (4.0 * eps_water * sigma_water**3)
KQ = k_charge * UNIT * UNIT
SCALE_WW = 0.5 * 4.0 * eps_water / (P_CUT * P_CUT)
SCALE_SW = 1.0 / (P_CUT * P_CUT)
FAR = 1.0e4
MONO = 96
P_ROWS, Q_ROWS, M_ROWS = slice(0, 64), slice(64, 128), slice(128, 224)
OWN_ROWS, HELD_ROWS = 224, 320
ROWS = 64


def split3(value):
    first = value.astype(BF16).astype(F32)
    rest = value - first
    second = rest.astype(BF16).astype(F32)
    return first, second, (rest - second).astype(BF16).astype(F32)


def rows_of(parts, fill=0.0):
    lanes = parts[0].shape[1]
    missing = 8 - len(parts)
    if missing:
        parts = list(parts) + [jnp.full((missing, lanes), fill, F32)]
    return jnp.concatenate(parts, axis=0)


def sincos(angle):
    turns = jnp.floor(angle * 0.6366197723675814 + 0.5)
    rest = angle - turns * 1.5703125 - turns * 4.838267948966e-4
    square = rest * rest
    sine = rest + rest * square * (
        -1.6666654611e-1 + square * (8.3321608736e-3 - square * 1.9515295891e-4)
    )
    cosine = (
        1.0
        - 0.5 * square
        + square
        * square
        * (4.166664568298827e-2 + square * (-1.388731625493765e-3 + square * 2.443315711809948e-5))
    )
    quarter = turns.astype(jnp.int32) & 3
    odd = (quarter & 1) == 1
    sin_out = jnp.where(odd, cosine, sine)
    cos_out = jnp.where(odd, sine, cosine)
    sin_out = jnp.where(quarter >= 2, -sin_out, sin_out)
    cos_out = jnp.where((quarter == 1) | (quarter == 2), -cos_out, cos_out)
    return sin_out, cos_out


def prepare_kernel(packed_ref, feat_ref, side_ref, comp_ref, raw_ref, key_ref, sorted_ref):
    frames = feat_ref.shape[1] - 1
    pairs = 2 * frames
    offset_at, angle_at, frac_at = pairs, 4 * pairs, 7 * pairs
    type_at, count_at, table_at = frac_at + 6, frac_at + 8, frac_at + 10
    lane = lax.broadcasted_iota(jnp.int32, (1, 128), 1).astype(F32)
    for i in range(2):
        for j in range(2):
            row = slice(j, j + 1)
            for f in range(frames):
                fc = (i * 2 + j) * frames + f
                voxel = packed_ref[f * 2 + i, row, :]
                raw_ref[fc, 0:1, :] = voxel
                for axis in range(3):
                    at = (f * 2 + i) * 3 + axis
                    raw_ref[fc, 1 + axis : 2 + axis, :] = packed_ref[offset_at + at, row, :]
                    raw_ref[fc, 4 + axis : 5 + axis, :] = packed_ref[angle_at + at, row, :]
                count = packed_ref[count_at + i, row, f : f + 1]
                raw_ref[fc, 7:8, :] = jnp.where(lane < count, 1.0, 0.0).astype(F32)
                key_ref[fc : fc + 1, :] = voxel * 128.0 + lane
    total = 4 * frames
    keys = key_ref[...]
    keys_t = keys.T
    rank_iota = lax.broadcasted_iota(jnp.int32, (128, 128), 0).astype(F32)
    for fc in range(total):
        before = jnp.where(keys_t[:, fc : fc + 1] < keys[fc : fc + 1, :], 1.0, 0.0)
        rank = jnp.sum(before, axis=0, keepdims=True)
        chosen = jnp.where(rank_iota == rank, 1.0, 0.0).astype(BF16)
        parts = jnp.concatenate(split3(raw_ref[fc]), axis=0).astype(BF16)
        moved = lax.dot_general(
            parts, chosen, (((1,), (1,)), ((), ())), preferred_element_type=F32
        )
        sorted_ref[:, fc, :] = moved[0:8] + moved[8:16] + moved[16:24]

    voxel = sorted_ref[0]
    cell_x = jnp.floor((voxel + 0.5) * (1.0 / (CELL_XY * SLAB)))
    in_plane = voxel - cell_x * (CELL_XY * SLAB)
    cell_y = jnp.floor((in_plane + 0.5) * (1.0 / SLAB))
    cell_z = in_plane - cell_y * SLAB
    row = lax.broadcasted_iota(jnp.int32, (total, 128), 0)
    own_x = (row // (2 * frames)).astype(F32)
    own_y = ((row // frames) % 2).astype(F32)
    x = (spacing * (cell_x + 0.5) + sorted_ref[1] + CUTOFF * (own_x - 1.0)) * UNIT
    y = (spacing * (cell_y + 0.5) + sorted_ref[2] + CUTOFF * (own_y - 1.0)) * UNIT
    z = (spacing * (cell_z + 0.5) + sorted_ref[3] - 0.5 * spacing * SLAB) * UNIT
    sin_b, cos_b = sincos(0.5 * sorted_ref[5])
    sin_p, cos_p = sincos(0.5 * (sorted_ref[4] + sorted_ref[6]))
    sin_m, cos_m = sincos(0.5 * (sorted_ref[4] - sorted_ref[6]))
    quat_w = cos_b * cos_p
    quat_x = -sin_b * sin_m
    quat_y = sin_b * cos_m
    quat_z = cos_b * sin_p
    features = (
        x, y, z,
        2.0 * (quat_x * quat_z + quat_w * quat_y),
        2.0 * (quat_y * quat_z - quat_w * quat_x),
        1.0 - 2.0 * (quat_x * quat_x + quat_y * quat_y),
        sorted_ref[7],
    )
    for number, value in enumerate(features):
        for cell in range(4):
            feat_ref[cell, 0:frames, number, :] = value[cell * frames : (cell + 1) * frames]
    share = CELL_XY * CELL_XY * SLAB // 32
    band = (lax.broadcasted_iota(jnp.int32, (total, 128), 1) // 4 * share).astype(F32)
    for number, value in enumerate((quat_w, quat_x, quat_y, quat_z, sorted_ref[7], voxel - band)):
        comp_ref[:, number, :] = value
    comp_ref[:, 6, :] = jnp.zeros((total, 128), F32)
    comp_ref[:, 7, :] = jnp.zeros((total, 128), F32)

    table = jnp.concatenate(
        [packed_ref[table_at + k, 0:1, :] for k in range(3)] + [jnp.zeros((5, 128), F32)], axis=0
    )
    tables = jnp.concatenate(split3(table), axis=0).astype(BF16)
    for i in range(2):
        for j in range(2):
            kind = packed_ref[type_at + i, j : j + 1, :]
            chosen = jnp.where(rank_iota == kind, 1.0, 0.0).astype(BF16)
            looked = jnp.dot(tables, chosen, preferred_element_type=F32)
            looked = looked[0:8] + looked[8:16] + looked[16:24]
            sigma, well, charge = looked[0:1], looked[1:2], looked[2:3]
            ratio = 0.5 * (1.0 + sigma * UNIT)
            cube = ratio * ratio * ratio
            sixth = cube * cube
            lower = (4.0 * eps_water**0.5) * jnp.sqrt(well) * sixth
            frac_x, frac_y, frac_z = (
                packed_ref[frac_at + i * 3 + axis, j : j + 1, :] for axis in range(3)
            )
            atom_x = (frac_x * CUTOFF + CUTOFF * (i - 1.0)) * UNIT
            atom_y = (frac_y * CUTOFF + CUTOFF * (j - 1.0)) * UNIT
            atom_z = (frac_z * (spacing * SLAB) - 0.5 * spacing * SLAB) * UNIT
            feat_ref[i * 2 + j, frames] = rows_of(
                [atom_x, atom_y, atom_z, lower, lower * sixth, charge, jnp.ones((1, 128), F32)]
            )
    for cell in range(4):
        for f in range(frames):
            feat_ref[cell, f, 7:8, :] = jnp.zeros((1, 128), F32)
    facing = 1 - lax.axis_index("py")
    for i in range(2):
        side_ref[i] = feat_ref[i * 2 + facing]


def partner_rows(base):
    first, second, third = split3(base)
    number = lax.broadcasted_iota(jnp.int32, (8, 128), 0)
    ones = jnp.where(number < 3, 1.0, 0.0).astype(F32)
    return jnp.concatenate(
        [first, first, first, second, second, third, ones, jnp.zeros((8, 128), F32)], axis=0
    )


def pair_rows(base, other):
    return jnp.concatenate([partner_rows(base), partner_rows(other)], axis=0).astype(BF16).T


def moment_rows(base, other):
    parts = []
    for value in (base, other):
        first, second, third = split3(value)
        parts += [first, first, first, second, second, third]
    return jnp.concatenate(parts, axis=0).astype(BF16).T


def moved_water(value, shift):
    x, y, z = value[0:1] + shift[0], value[1:2] + shift[1], value[2:3]
    return (x, y, z), (value[3:4], value[4:5], value[5:6])


def water_partner(value, shift, absent):
    (x, y, z), _ = moved_water(value, shift)
    n = x * x + y * y + z * z + FAR * ((1.0 - value[6:7]) + absent)
    zero = jnp.zeros((3, 128), F32)
    return jnp.concatenate([x, y, z, zero, n, zero[0:1]], axis=0)


def moment_partner(value, shift):
    place, moment = moved_water(value, shift)
    n = place[0] * place[0] + place[1] * place[1] + place[2] * place[2]
    e = moment[0] * place[0] + moment[1] * place[1] + moment[2] * place[2]
    rows = [moment[a] * n - 3.0 * place[a] * e for a in range(3)] + list(moment)
    rows += [3.0 * place[a] * moment[b] - 2.0 * moment[a] * place[b] for a in range(3) for b in range(3)]
    return jnp.concatenate(rows + [3.0 * e], axis=0)


def own_moments(value):
    place = (value[0:1], value[1:2], value[2:3])
    moment = (value[3:4], value[4:5], value[5:6])
    n = place[0] * place[0] + place[1] * place[1] + place[2] * place[2] + P_SOFT
    c = moment[0] * place[0] + moment[1] * place[1] + moment[2] * place[2]
    rows = list(moment) + [moment[a] * n - 3.0 * c * place[a] for a in range(3)]
    rows += [moment[a] * place[b] for a in range(3) for b in range(3)]
    first, second, third = split3(KD * jnp.concatenate(rows + [c], axis=0))
    return jnp.concatenate([first, second, third, first, second, first], axis=0).astype(BF16)


def solute_partner(value, shift, absent):
    x, y, z, charge = value[0:1] + shift[0], value[1:2] + shift[1], value[2:3], value[5:6]
    n = x * x + y * y + z * z + FAR * ((1.0 - value[6:7]) + absent)
    return jnp.concatenate([x, y, z, charge * x, charge * y, charge * z, n, charge], axis=0)


def solute_levels(value):
    return (jnp.broadcast_to(value[k : k + 1], (128, 128)).T for k in (3, 4))


def own_side(value):
    x, y, z = value[0:1], value[1:2], value[2:3]
    mx, my, mz = value[3:4], value[4:5], value[5:6]
    zero = jnp.zeros((1, 128), F32)
    one = jnp.ones((1, 128), F32)
    n = x * x + y * y + z * z + P_SOFT + FAR * (1.0 - value[6:7])
    c = mx * x + my * y + mz * z
    sides = (
        ([-2.0 * x, -2.0 * y, -2.0 * z, zero, zero, zero, one, zero], n),
        ([zero, zero, zero, KQ * mx, KQ * my, KQ * mz, zero, -KQ * c], None),
    )
    out = []
    for rows, term in sides:
        first, second, third = split3(jnp.concatenate(rows, axis=0))
        if term is None:
            last = jnp.zeros((16, 128), F32)
        else:
            last = jnp.concatenate(list(split3(term)) + [jnp.zeros((13, 128), F32)], axis=0)
        out += [first, second, third, first, second, first, last]
    return jnp.concatenate([jnp.concatenate(out, axis=0).astype(BF16), own_moments(value)], axis=0)


def run_frames(frames, set_up, frame):
    set_up(0)
    for f in range(frames):
        if f + 1 < frames:
            set_up(f + 1)
        frame(f)


def fold(acc, value):
    for k in range(value.shape[0] // 8):
        acc = acc + value[8 * k : 8 * k + 8]
    return acc


CHUNK = 16


def water_energy(p, moments):
    root = lax.rsqrt(p)
    u = root * root
    u15 = u * root
    window = jnp.maximum(P_END - p, 0.0)
    inner = u15 * (u15 * u15 - 1.0) + moments * u
    return u15 * inner * (window * window)


def solute_energy(p, charge, lower, upper):
    root = lax.rsqrt(p)
    u15 = root * root * root
    window = jnp.maximum(P_END - p, 0.0)
    inner = u15 * (upper * (u15 * u15) - lower) + charge
    return u15 * inner * (window * window)


def chunks(rows):
    return [slice(k * CHUNK, (k + 1) * CHUNK) for k in range(rows // CHUNK)]


def water_pairs(acc, values):
    for part in chunks(values[0].shape[0]):
        acc = fold(acc, water_energy(*[value[part] for value in values]))
    return acc


def solute_pairs(acc, p, charge, lower, upper):
    for part in chunks(p.shape[0]):
        low, high = lower[part], upper[part]
        if low.shape[1] != p.shape[1]:
            low, high = jnp.concatenate([low] * 2, axis=1), jnp.concatenate([high] * 2, axis=1)
        acc = fold(acc, solute_energy(p[part], charge[part], low, high))
    return acc


def dot(left, right):
    return jnp.dot(left, right, preferred_element_type=F32)


def only(side, number):
    parts = [side, jnp.zeros_like(side)]
    return jnp.concatenate(parts if number == 0 else parts[::-1], axis=0)


def each(left, right):
    top = jnp.concatenate([left, jnp.zeros_like(right)], axis=1)
    bottom = jnp.concatenate([jnp.zeros_like(left), right], axis=1)
    return jnp.concatenate([top, bottom], axis=0)


def crossed(left, right):
    top = jnp.concatenate([jnp.zeros_like(left), right], axis=1)
    bottom = jnp.concatenate([left, jnp.zeros_like(right)], axis=1)
    return jnp.concatenate([top, bottom], axis=0)


def halves_of(column, f, feat_ref):
    first, second = feat_ref[2 * column, f], feat_ref[2 * column + 1, f]
    return (
        jnp.concatenate([first[:, :64], second[:, :64]], axis=1),
        jnp.concatenate([first[:, 64:], second[:, 64:]], axis=1),
    )


def inner_kernel(feat_ref, acc_ref, other_ref, own_ref, left_ref, mono_ref, sum_ref):
    frames = feat_ref.shape[1] - 1
    def set_up(f):
        for i in range(2):
            left_ref[f, i] = pair_rows(
                *[water_partner(feat_ref[2 * i + j, f], (0.0, 0.0), 0.0) for j in range(2)]
            )
            mono_ref[f, i] = moment_rows(
                *[moment_partner(feat_ref[2 * i + j, f], (0.0, 0.0)) for j in range(2)]
            )
            own_ref[f, i, 0:OWN_ROWS] = jnp.concatenate(
                [own_side(half) for half in halves_of(i, f, feat_ref)], axis=1
            )

    def frame(f):
        for i in range(2):
            sides = (own_ref[f, i, P_ROWS], own_ref[f, i, M_ROWS])
            acc = jnp.zeros((8, 256), F32)
            lefts = (left_ref[f, i], mono_ref[f, i])
            for j in range(2):
                acc = water_pairs(acc, [dot(left, only(side, j)) for left, side in zip(lefts, sides)])
            if i == 0:
                near = (left_ref[f, 1, 0:64], mono_ref[f, 1, 0:64])
                for j in range(2):
                    values = [dot(left, only(side, j)) for left, side in zip(near, sides)]
                    for part in chunks(64):
                        energy = water_energy(*[value[part] for value in values])
                        acc = fold(acc, energy)
                        sum_ref[f, j, part] = energy[:, :128] + energy[:, 128:]
                far = (left_ref[f, 1, 64:128], mono_ref[f, 1, 64:128])
                values = [
                    dot(left, each(side[:, 128:], side[:, 128:])) for left, side in zip(far, sides)
                ]
                late = jnp.zeros((8, 256), F32)
                for part in chunks(64):
                    energy = water_energy(*[value[part] for value in values])
                    late = fold(late, energy)
                    rows = slice(64 + part.start, 64 + part.stop)
                    sum_ref[f, 0, rows] = energy[:, :128]
                    sum_ref[f, 1, rows] = energy[:, 128:]
                acc = acc + jnp.concatenate(
                    [jnp.zeros((8, 128), F32), late[:, :128] + late[:, 128:]], axis=1
                )
            acc_ref[f, i] = acc
        for j in range(2):
            other_ref[f, j] = fold(jnp.zeros((8, 128), F32), sum_ref[f, j].T)

    run_frames(frames, set_up, frame)


def to_facing():
    return jnp.where(lax.axis_index("py") == 0, 1.0, -1.0).astype(F32) * (2.0 * CUTOFF * UNIT)


def set_solutes(pairs, frames, solute_ref, coef_ref, start):
    for number, pair in enumerate(pairs, start):
        solute_ref[number] = pair_rows(
            *[solute_partner(ref[k, frames], shift, absent) for ref, k, shift, absent in pair]
        )
        for place, (ref, k, _, _) in enumerate(pair):
            cell = 2 * number + place
            coef_ref[cell, 0], coef_ref[cell, 1] = solute_levels(ref[k, frames])


def set_waters(pairs, f, left_ref, mono_ref):
    for number, pair in enumerate(pairs):
        left_ref[f, number] = pair_rows(
            *[water_partner(ref[k, f], shift, absent) for ref, k, shift, absent in pair]
        )
        mono_ref[f, number] = moment_rows(
            *[moment_partner(ref[k, f], shift) for ref, k, shift, _ in pair]
        )


def ends():
    px = lax.axis_index("px")
    no_low = jnp.where(px == 0, 1.0, 0.0).astype(F32)
    no_high = jnp.where(px == lax.axis_size("px") - 1, 1.0, 0.0).astype(F32)
    width = 2.0 * CUTOFF * UNIT
    return (-width, no_low), (width, no_high)


def column_kernel(
    feat_ref, low_ref, high_ref, own_ref, water_ref, acc_ref, left_ref, mono_ref, solute_ref, coef_ref,
):
    frames = feat_ref.shape[1] - 1
    (low_x, no_low), (high_x, no_high) = ends()
    pairs = (
        tuple((low_ref, j, (low_x, 0.0), no_low) for j in range(2)),
        tuple((high_ref, j, (high_x, 0.0), no_high) for j in range(2)),
    )
    own_pairs = [[(feat_ref, 2 * i + j, (0.0, 0.0), 0.0) for j in range(2)] for i in range(2)]
    set_solutes(own_pairs, frames, solute_ref, coef_ref, 0)
    set_solutes(pairs, frames, solute_ref, coef_ref, 2)

    def set_up(f):
        set_waters(pairs, f, left_ref, mono_ref)

    def frame(f):
        for i in range(2):
            sides = [own_ref[f, i, rows] for rows in (P_ROWS, Q_ROWS, M_ROWS)]
            solute = jnp.zeros((8, 256), F32)
            for column in (0, 1, 2 + i):
                left = solute_ref[column]
                for j in range(2):
                    cell = 2 * column + j
                    solute = solute_pairs(
                        solute, *[dot(left, only(sides[q], j)) for q in range(2)],
                        coef_ref[cell, 0], coef_ref[cell, 1],
                    )
            acc_ref[f, i, 1] = solute
            full, part = (slice(64, 128), slice(0, 64)) if i == 0 else (slice(0, 64), slice(64, 128))
            lanes = slice(0, 128) if i == 0 else slice(128, 256)
            water = water_ref[f, i]
            for j in range(2):
                water = water_pairs(
                    water,
                    [
                        dot(left_ref[f, i, full], only(sides[0], j)),
                        dot(mono_ref[f, i, full], only(sides[2], j)),
                    ],
                )
            late = water_pairs(
                jnp.zeros((8, 256), F32),
                [
                    dot(left_ref[f, i, part], each(sides[0][:, lanes], sides[0][:, lanes])),
                    dot(mono_ref[f, i, part], each(sides[2][:, lanes], sides[2][:, lanes])),
                ],
            )
            late = [late[:, :128] + late[:, 128:], jnp.zeros((8, 128), F32)]
            acc_ref[f, i, 0] = water + jnp.concatenate(late if i == 0 else late[::-1], axis=1)

    run_frames(frames, set_up, frame)


def facing_kernel(
    feat_ref, side_ref, acc_ref, other_ref, comp_ref, send_ref,
    left_ref, mono_ref, solute_ref, coef_ref, face_ref, wall_ref, rec_ref,
):
    frames = feat_ref.shape[1] - 1
    facing = 1 - lax.axis_index("py")
    across = to_facing()
    (low_x, no_low), (high_x, no_high) = ends()
    pairs = (
        tuple((side_ref, k, (0.0, across), 0.0) for k in range(2)),
        ((side_ref, 2, (low_x, across), no_low), (side_ref, 3, (high_x, across), no_high)),
    )
    set_solutes(pairs, frames, solute_ref, coef_ref, 0)

    def set_up(f):
        set_waters(pairs, f, left_ref, mono_ref)
        face_ref[f] = jnp.concatenate(
            [own_side(feat_ref[facing, f]), own_side(feat_ref[2 + facing, f])], axis=1
        )

    def frame(f):
        faces = [face_ref[f, rows] for rows in (P_ROWS, Q_ROWS, M_ROWS)]
        water = jnp.zeros((8, 256), F32)
        solute = jnp.zeros((8, 256), F32)
        for meet, number, order in ((each, 0, (0, 1)), (crossed, 0, (1, 0)), (each, 1, (2, 3))):
            sides = [meet(face[:, :128], face[:, 128:]) for face in faces]
            water = water_pairs(
                water, [dot(left_ref[f, number], sides[0]), dot(mono_ref[f, number], sides[2])]
            )
            levels = [
                jnp.concatenate([coef_ref[order[0], k], coef_ref[order[1], k]], axis=1) for k in range(2)
            ]
            solute = solute_pairs(
                solute, *[dot(solute_ref[number], sides[q]) for q in range(2)], *levels
            )
        wall_ref[f, 0] = water
        wall_ref[f, 1] = solute

    run_frames(frames, set_up, frame)
    rec_ref[...] = comp_ref[...]
    self_root = P_SOFT**-0.5
    self_u15 = self_root**3
    for f in range(frames):
        walls = [jnp.sum(wall_ref[f, k], axis=0, keepdims=True) for k in range(2)]
        for i in range(2):
            sums = [jnp.sum(acc_ref[f, i, k], axis=0, keepdims=True) for k in range(2)]
            for j in range(2):
                near = (facing == j).astype(F32)
                water, solute = (
                    jnp.concatenate([value[:, 64 * j : 64 * j + 64], value[:, 128 + 64 * j : 192 + 64 * j]], axis=1)
                    + near * wall[:, 128 * i : 128 * i + 128]
                    for value, wall in zip(sums, walls)
                )
                if i == 1:
                    water = water + jnp.sum(other_ref[f, j], axis=0, keepdims=True)
                value = feat_ref[2 * i + j, f]
                filled = value[6:7]
                moment = value[3:4] * value[3:4] + value[4:5] * value[4:5] + value[5:6] * value[5:6]
                own = (self_u15 * P_CUT * P_CUT) * (
                    self_u15 * (self_u15 * self_u15 - 1.0) + KD * moment
                )
                fc = (2 * i + j) * frames + f
                rec_ref[fc, 6:7, :] = filled * (SCALE_SW * solute)
                rec_ref[fc, 7:8, :] = filled * (SCALE_WW * (water - own))
    send_ref[...] = rec_ref[...].reshape(128, 128).T.reshape(send_ref.shape)


def bin_kernel(frame_total, got_ref, out_ref, field_ref, rec_ref):
    share = out_ref.shape[-1]
    groups = -(-share // 128)
    number = lax.broadcasted_iota(jnp.int32, (128, 128), 0).astype(F32)
    field_ref[...] = got_ref[...].reshape(128, 128).T.reshape(field_ref.shape)
    filled = field_ref[:, 4, :]
    quaternion = [field_ref[:, k, :] for k in range(4)]
    rec_ref[:, 0, :] = filled
    rec_ref[:, 1, :] = field_ref[:, 6, :]
    rec_ref[:, 2, :] = field_ref[:, 7, :]
    for k, (a, b) in enumerate(pair_index):
        rec_ref[:, 3 + k, :] = quaternion[a] * quaternion[b] * filled
    for k in range(13, 16):
        rec_ref[:, k, :] = jnp.zeros_like(filled)
    for i in range(2):
        for j in range(2):
            totals = jnp.zeros((48 * groups, 128), F32)
            for f in range(4):
                fc = (2 * i + j) * 4 + f
                voxel = field_ref[fc, 5:6, :]
                group = jnp.floor((voxel + 0.5) * (1.0 / 128.0))
                chosen = jnp.where(number == voxel - 128.0 * group, 1.0, 0.0).astype(BF16)
                parts = jnp.concatenate(split3(rec_ref[fc]), axis=0)
                parts = jnp.concatenate(
                    [jnp.where(group == k, parts, 0.0) for k in range(groups)], axis=0
                ).astype(BF16)
                totals = totals + lax.dot_general(
                    parts, chosen, (((1,), (1,)), ((), ())), preferred_element_type=F32
                )
            for k in range(groups):
                lanes = min(128, share - 128 * k)
                part = totals[48 * k : 48 * k + 48]
                summed = (part[0:16] + part[16:32] + part[32:48])[:, :lanes]
                counted = summed[0:1]
                span = slice(128 * k, 128 * k + lanes)
                out_ref[0:1, i, j, span] = counted * (1.0 / (frame_total * rho_bulk * spacing**3))
                out_ref[1:13, i, j, span] = summed[1:13] / jnp.maximum(counted, 1.0)


def vmem():
    return pl.BlockSpec(memory_space=pltpu.VMEM)


PARAMS = pltpu.CompilerParams(vmem_limit_bytes=24 * 1024 * 1024)


def shards(
    water_voxel, water_offset, water_angles, water_count,
    solute_frac, solute_type, type_sigma, type_well, type_charge,
):
    frames = water_voxel.shape[0]
    cols = lax.axis_size("px")
    ranks = lax.axis_size("fr")
    total = 4 * frames
    rows = (-1, 2, 128)
    pieces = (
        water_voxel.reshape(rows),
        jnp.transpose(water_offset, (0, 1, 3, 2, 4)).reshape(rows),
        jnp.transpose(water_angles, (0, 1, 3, 2, 4)).reshape(rows),
        jnp.transpose(solute_frac, (0, 2, 1, 3)).reshape(rows),
        solute_type.reshape(rows),
        jnp.transpose(water_count, (1, 2, 0)),
        type_sigma.reshape(1, 1, -1), type_well.reshape(1, 1, -1), type_charge.reshape(1, 1, -1),
    )
    deep = sum(piece.shape[0] for piece in pieces)
    sums = {F32: jnp.zeros((deep, 2, 128), F32), jnp.int32: jnp.zeros((deep, 2, 128), jnp.int32)}
    start = 0
    for piece in pieces:
        size = piece.shape
        kind = F32 if piece.dtype == F32 else jnp.int32
        sums[kind] = sums[kind] + lax.pad(
            piece, jnp.zeros((), kind),
            ((start, deep - start - size[0], 0), (0, 2 - size[1], 0), (0, 128 - size[2], 0)),
        )
        start += size[0]
    packed = sums[F32] + sums[jnp.int32].astype(F32)
    feat, side_out, comp = pl.pallas_call(
        prepare_kernel,
        out_shape=(
            jax.ShapeDtypeStruct((4, frames + 1, 8, 128), F32),
            jax.ShapeDtypeStruct((2, frames + 1, 8, 128), F32),
            jax.ShapeDtypeStruct((total, 8, 128), F32),
        ),
        in_specs=[vmem()],
        out_specs=(vmem(),) * 3,
        scratch_shapes=[
            pltpu.VMEM((total, 8, 128), F32),
            pltpu.VMEM((total, 128), F32),
            pltpu.VMEM((8, total, 128), F32),
        ],
        compiler_params=PARAMS,
        name="prepare",
    )(packed)

    up = [(k, (k + 1) % cols) for k in range(cols)]
    down = [(k, (k - 1) % cols) for k in range(cols)]
    low = lax.ppermute(feat[2:4], "px", up)
    high = lax.ppermute(feat[0:2], "px", down)

    work = pl.CostEstimate(flops=10**9, bytes_accessed=10**6, transcendentals=0)
    column_shape = jax.ShapeDtypeStruct((frames, 2, 8, 256), F32)
    water, other, own = pl.pallas_call(
        inner_kernel,
        out_shape=(
            column_shape,
            jax.ShapeDtypeStruct((frames, 2, 8, 128), F32),
            jax.ShapeDtypeStruct((frames, 2, HELD_ROWS, 256), BF16),
        ),
        in_specs=[vmem()],
        out_specs=(vmem(),) * 3,
        scratch_shapes=[
            pltpu.VMEM((frames, 2, 128, 2 * ROWS), BF16),
            pltpu.VMEM((frames, 2, 128, 2 * MONO), BF16),
            pltpu.VMEM((frames, 2, 128, 128), F32),
        ],
        compiler_params=PARAMS,
        cost_estimate=work,
        name="inner",
    )(feat)

    low, high, water = lax.optimization_barrier((low, high, water))
    facing = 1 - lax.axis_index("py")
    beyond = [lax.dynamic_slice_in_dim(column, facing, 1, axis=0) for column in (low, high)]
    side = lax.ppermute(jnp.concatenate([side_out, *beyond], axis=0), "py", [(0, 1), (1, 0)])
    acc = pl.pallas_call(
        column_kernel,
        out_shape=jax.ShapeDtypeStruct((frames, 2, 2, 8, 256), F32),
        in_specs=[vmem()] * 5,
        out_specs=vmem(),
        scratch_shapes=[
            pltpu.VMEM((frames, 2, 128, 2 * ROWS), BF16),
            pltpu.VMEM((frames, 2, 128, 2 * MONO), BF16),
            pltpu.VMEM((4, 128, 2 * ROWS), BF16),
            pltpu.VMEM((8, 2, 128, 128), F32),
        ],
        compiler_params=PARAMS,
        cost_estimate=work,
        name="columns",
    )(feat, low, high, own, water)

    send = pl.pallas_call(
        facing_kernel,
        out_shape=jax.ShapeDtypeStruct((ranks, 4, 128), F32),
        in_specs=[vmem()] * 5,
        out_specs=vmem(),
        scratch_shapes=[
            pltpu.VMEM((frames, 2, 128, 2 * ROWS), BF16),
            pltpu.VMEM((frames, 2, 128, 2 * MONO), BF16),
            pltpu.VMEM((2, 128, 2 * ROWS), BF16),
            pltpu.VMEM((4, 2, 128, 128), F32),
            pltpu.VMEM((frames, OWN_ROWS, 256), BF16),
            pltpu.VMEM((frames, 2, 8, 256), F32),
            pltpu.VMEM((total, 8, 128), F32),
        ],
        compiler_params=PARAMS,
        name="facing",
    )(feat, side, acc, other, comp)

    got = lax.all_to_all(send, "fr", 0, 0, tiled=True)
    share = CELL_XY * CELL_XY * SLAB // ranks
    return pl.pallas_call(
        functools.partial(bin_kernel, frames * ranks),
        out_shape=jax.ShapeDtypeStruct((13, 2, 2, share), F32),
        in_specs=[vmem()],
        out_specs=vmem(),
        scratch_shapes=[pltpu.VMEM((total, 8, 128), F32), pltpu.VMEM((total, 16, 128), F32)],
        compiler_params=PARAMS,
        name="bin",
    )(got)


def solution(mesh):
    placed = (
        P("fr", "px", "py", None),
        P("fr", "px", "py", None, None),
        P("fr", "px", "py", None, None),
        P("fr", "px", "py"),
        P("px", "py", None, None),
        P("px", "py", None),
        P(),
        P(),
        P(),
    )
    return jax.shard_map(
        shards, mesh=mesh, in_specs=placed, out_specs=P(None, "px", "py", "fr"), check_vma=False
    )
```

```python
import functools

import jax
import jax.numpy as jnp
from jax import lax
from jax.experimental import pallas as pl
from jax.experimental.pallas import tpu as pltpu
from jax.sharding import PartitionSpec as P

CELL_XY = 24
SLAB = 40
F32 = jnp.float32
BF16 = jnp.bfloat16

spacing = 0.5
soft_sq = 9.0
sigma_water = 3.1507
eps_water = 0.1521
k_dipole = 79.4
k_charge = 162.3
rho_bulk = 0.0334
pair_index = ((0, 0), (0, 1), (0, 2), (0, 3), (1, 1), (1, 2), (1, 3), (2, 2), (2, 3), (3, 3))

CUTOFF = spacing * CELL_XY
UNIT = 1.0 / sigma_water
P_SOFT = soft_sq * UNIT * UNIT
P_CUT = CUTOFF * CUTOFF * UNIT * UNIT
P_END = P_SOFT + P_CUT
KD = k_dipole / (4.0 * eps_water * sigma_water**3)
KQ = k_charge * UNIT * UNIT
SCALE_WW = 0.5 * 4.0 * eps_water / (P_CUT * P_CUT)
SCALE_SW = 1.0 / (P_CUT * P_CUT)
FAR = 1.0e4
MONO = 96
P_ROWS, Q_ROWS, M_ROWS = slice(0, 64), slice(64, 128), slice(128, 224)
OWN_ROWS, HELD_ROWS = 224, 320
ROWS = 64


def split3(value):
    first = value.astype(BF16).astype(F32)
    rest = value - first
    second = rest.astype(BF16).astype(F32)
    return first, second, (rest - second).astype(BF16).astype(F32)


def rows_of(parts, fill=0.0):
    lanes = parts[0].shape[1]
    missing = 8 - len(parts)
    if missing:
        parts = list(parts) + [jnp.full((missing, lanes), fill, F32)]
    return jnp.concatenate(parts, axis=0)


def sincos(angle):
    turns = jnp.floor(angle * 0.6366197723675814 + 0.5)
    rest = angle - turns * 1.5703125 - turns * 4.838267948966e-4
    square = rest * rest
    sine = rest + rest * square * (
        -1.6666654611e-1 + square * (8.3321608736e-3 - square * 1.9515295891e-4)
    )
    cosine = (
        1.0
        - 0.5 * square
        + square
        * square
        * (4.166664568298827e-2 + square * (-1.388731625493765e-3 + square * 2.443315711809948e-5))
    )
    quarter = turns.astype(jnp.int32) & 3
    odd = (quarter & 1) == 1
    sin_out = jnp.where(odd, cosine, sine)
    cos_out = jnp.where(odd, sine, cosine)
    sin_out = jnp.where(quarter >= 2, -sin_out, sin_out)
    cos_out = jnp.where((quarter == 1) | (quarter == 2), -cos_out, cos_out)
    return sin_out, cos_out


def prepare_kernel(packed_ref, feat_ref, side_ref, comp_ref, raw_ref, key_ref, sorted_ref):
    frames = feat_ref.shape[1] - 1
    pairs = 2 * frames
    offset_at, angle_at, frac_at = pairs, 4 * pairs, 7 * pairs
    type_at, count_at, table_at = frac_at + 6, frac_at + 8, frac_at + 10
    lane = lax.broadcasted_iota(jnp.int32, (1, 128), 1).astype(F32)
    for i in range(2):
        for j in range(2):
            row = slice(j, j + 1)
            for f in range(frames):
                fc = (i * 2 + j) * frames + f
                voxel = packed_ref[f * 2 + i, row, :]
                raw_ref[fc, 0:1, :] = voxel
                for axis in range(3):
                    at = (f * 2 + i) * 3 + axis
                    raw_ref[fc, 1 + axis : 2 + axis, :] = packed_ref[offset_at + at, row, :]
                    raw_ref[fc, 4 + axis : 5 + axis, :] = packed_ref[angle_at + at, row, :]
                count = packed_ref[count_at + i, row, f : f + 1]
                raw_ref[fc, 7:8, :] = jnp.where(lane < count, 1.0, 0.0).astype(F32)
                key_ref[fc : fc + 1, :] = voxel * 128.0 + lane
    total = 4 * frames
    keys = key_ref[...]
    keys_t = keys.T
    rank_iota = lax.broadcasted_iota(jnp.int32, (128, 128), 0).astype(F32)
    for fc in range(total):
        before = jnp.where(keys_t[:, fc : fc + 1] < keys[fc : fc + 1, :], 1.0, 0.0)
        rank = jnp.sum(before, axis=0, keepdims=True)
        chosen = jnp.where(rank_iota == rank, 1.0, 0.0).astype(BF16)
        parts = jnp.concatenate(split3(raw_ref[fc]), axis=0).astype(BF16)
        moved = lax.dot_general(
            parts, chosen, (((1,), (1,)), ((), ())), preferred_element_type=F32
        )
        sorted_ref[:, fc, :] = moved[0:8] + moved[8:16] + moved[16:24]

    voxel = sorted_ref[0]
    cell_x = jnp.floor((voxel + 0.5) * (1.0 / (CELL_XY * SLAB)))
    in_plane = voxel - cell_x * (CELL_XY * SLAB)
    cell_y = jnp.floor((in_plane + 0.5) * (1.0 / SLAB))
    cell_z = in_plane - cell_y * SLAB
    row = lax.broadcasted_iota(jnp.int32, (total, 128), 0)
    own_x = (row // (2 * frames)).astype(F32)
    own_y = ((row // frames) % 2).astype(F32)
    x = (spacing * (cell_x + 0.5) + sorted_ref[1] + CUTOFF * (own_x - 1.0)) * UNIT
    y = (spacing * (cell_y + 0.5) + sorted_ref[2] + CUTOFF * (own_y - 1.0)) * UNIT
    z = (spacing * (cell_z + 0.5) + sorted_ref[3] - 0.5 * spacing * SLAB) * UNIT
    sin_b, cos_b = sincos(0.5 * sorted_ref[5])
    sin_p, cos_p = sincos(0.5 * (sorted_ref[4] + sorted_ref[6]))
    sin_m, cos_m = sincos(0.5 * (sorted_ref[4] - sorted_ref[6]))
    quat_w = cos_b * cos_p
    quat_x = -sin_b * sin_m
    quat_y = sin_b * cos_m
    quat_z = cos_b * sin_p
    features = (
        x, y, z,
        2.0 * (quat_x * quat_z + quat_w * quat_y),
        2.0 * (quat_y * quat_z - quat_w * quat_x),
        1.0 - 2.0 * (quat_x * quat_x + quat_y * quat_y),
        sorted_ref[7],
    )
    for number, value in enumerate(features):
        for cell in range(4):
            feat_ref[cell, 0:frames, number, :] = value[cell * frames : (cell + 1) * frames]
    share = CELL_XY * CELL_XY * SLAB // 32
    band = (lax.broadcasted_iota(jnp.int32, (total, 128), 1) // 4 * share).astype(F32)
    for number, value in enumerate((quat_w, quat_x, quat_y, quat_z, sorted_ref[7], voxel - band)):
        comp_ref[:, number, :] = value
    comp_ref[:, 6, :] = jnp.zeros((total, 128), F32)
    comp_ref[:, 7, :] = jnp.zeros((total, 128), F32)

    table = jnp.concatenate(
        [packed_ref[table_at + k, 0:1, :] for k in range(3)] + [jnp.zeros((5, 128), F32)], axis=0
    )
    tables = jnp.concatenate(split3(table), axis=0).astype(BF16)
    for i in range(2):
        for j in range(2):
            kind = packed_ref[type_at + i, j : j + 1, :]
            chosen = jnp.where(rank_iota == kind, 1.0, 0.0).astype(BF16)
            looked = jnp.dot(tables, chosen, preferred_element_type=F32)
            looked = looked[0:8] + looked[8:16] + looked[16:24]
            sigma, well, charge = looked[0:1], looked[1:2], looked[2:3]
            ratio = 0.5 * (1.0 + sigma * UNIT)
            cube = ratio * ratio * ratio
            sixth = cube * cube
            lower = (4.0 * eps_water**0.5) * jnp.sqrt(well) * sixth
            frac_x, frac_y, frac_z = (
                packed_ref[frac_at + i * 3 + axis, j : j + 1, :] for axis in range(3)
            )
            atom_x = (frac_x * CUTOFF + CUTOFF * (i - 1.0)) * UNIT
            atom_y = (frac_y * CUTOFF + CUTOFF * (j - 1.0)) * UNIT
            atom_z = (frac_z * (spacing * SLAB) - 0.5 * spacing * SLAB) * UNIT
            feat_ref[i * 2 + j, frames] = rows_of(
                [atom_x, atom_y, atom_z, lower, lower * sixth, charge, jnp.ones((1, 128), F32)]
            )
    for cell in range(4):
        for f in range(frames):
            feat_ref[cell, f, 7:8, :] = jnp.zeros((1, 128), F32)
    facing = 1 - lax.axis_index("py")
    for i in range(2):
        side_ref[i] = feat_ref[i * 2 + facing]


def partner_rows(base):
    first, second, third = split3(base)
    number = lax.broadcasted_iota(jnp.int32, (8, 128), 0)
    ones = jnp.where(number < 3, 1.0, 0.0).astype(F32)
    return jnp.concatenate(
        [first, first, first, second, second, third, ones, jnp.zeros((8, 128), F32)], axis=0
    )


def pair_rows(base, other):
    return jnp.concatenate([partner_rows(base), partner_rows(other)], axis=0).astype(BF16).T


def moment_rows(base, other):
    parts = []
    for value in (base, other):
        first, second, third = split3(value)
        parts += [first, first, first, second, second, third]
    return jnp.concatenate(parts, axis=0).astype(BF16).T


def moved_water(value, shift):
    x, y, z = value[0:1] + shift[0], value[1:2] + shift[1], value[2:3]
    return (x, y, z), (value[3:4], value[4:5], value[5:6])


def water_partner(value, shift, absent):
    (x, y, z), _ = moved_water(value, shift)
    n = x * x + y * y + z * z + FAR * ((1.0 - value[6:7]) + absent)
    zero = jnp.zeros((3, 128), F32)
    return jnp.concatenate([x, y, z, zero, n, zero[0:1]], axis=0)


def moment_partner(value, shift):
    place, moment = moved_water(value, shift)
    n = place[0] * place[0] + place[1] * place[1] + place[2] * place[2]
    e = moment[0] * place[0] + moment[1] * place[1] + moment[2] * place[2]
    rows = [moment[a] * n - 3.0 * place[a] * e for a in range(3)] + list(moment)
    rows += [3.0 * place[a] * moment[b] - 2.0 * moment[a] * place[b] for a in range(3) for b in range(3)]
    return jnp.concatenate(rows + [3.0 * e], axis=0)


def own_moments(value):
    place = (value[0:1], value[1:2], value[2:3])
    moment = (value[3:4], value[4:5], value[5:6])
    n = place[0] * place[0] + place[1] * place[1] + place[2] * place[2] + P_SOFT
    c = moment[0] * place[0] + moment[1] * place[1] + moment[2] * place[2]
    rows = list(moment) + [moment[a] * n - 3.0 * c * place[a] for a in range(3)]
    rows += [moment[a] * place[b] for a in range(3) for b in range(3)]
    first, second, third = split3(KD * jnp.concatenate(rows + [c], axis=0))
    return jnp.concatenate([first, second, third, first, second, first], axis=0).astype(BF16)


def solute_partner(value, shift, absent):
    x, y, z, charge = value[0:1] + shift[0], value[1:2] + shift[1], value[2:3], value[5:6]
    n = x * x + y * y + z * z + FAR * ((1.0 - value[6:7]) + absent)
    return jnp.concatenate([x, y, z, charge * x, charge * y, charge * z, n, charge], axis=0)


def solute_levels(value):
    return (jnp.broadcast_to(value[k : k + 1], (128, 128)).T for k in (3, 4))


def own_side(value):
    x, y, z = value[0:1], value[1:2], value[2:3]
    mx, my, mz = value[3:4], value[4:5], value[5:6]
    zero = jnp.zeros((1, 128), F32)
    one = jnp.ones((1, 128), F32)
    n = x * x + y * y + z * z + P_SOFT + FAR * (1.0 - value[6:7])
    c = mx * x + my * y + mz * z
    sides = (
        ([-2.0 * x, -2.0 * y, -2.0 * z, zero, zero, zero, one, zero], n),
        ([zero, zero, zero, KQ * mx, KQ * my, KQ * mz, zero, -KQ * c], None),
    )
    out = []
    for rows, term in sides:
        first, second, third = split3(jnp.concatenate(rows, axis=0))
        if term is None:
            last = jnp.zeros((16, 128), F32)
        else:
            last = jnp.concatenate(list(split3(term)) + [jnp.zeros((13, 128), F32)], axis=0)
        out += [first, second, third, first, second, first, last]
    return jnp.concatenate([jnp.concatenate(out, axis=0).astype(BF16), own_moments(value)], axis=0)


def run_frames(frames, set_up, frame):
    set_up(0)
    for f in range(frames):
        if f + 1 < frames:
            set_up(f + 1)
        frame(f)


def fold(acc, value):
    for k in range(value.shape[0] // 8):
        acc = acc + value[8 * k : 8 * k + 8]
    return acc


CHUNK = 16


def water_energy(p, moments):
    root = lax.rsqrt(p)
    u = root * root
    u15 = u * root
    window = jnp.maximum(P_END - p, 0.0)
    inner = u15 * (u15 * u15 - 1.0) + moments * u
    return u15 * inner * (window * window)


def solute_energy(p, charge, lower, upper):
    root = lax.rsqrt(p)
    u15 = root * root * root
    window = jnp.maximum(P_END - p, 0.0)
    inner = u15 * (upper * (u15 * u15) - lower) + charge
    return u15 * inner * (window * window)


def chunks(rows):
    return [slice(k * CHUNK, (k + 1) * CHUNK) for k in range(rows // CHUNK)]


def water_pairs(acc, values):
    for part in chunks(values[0].shape[0]):
        acc = fold(acc, water_energy(*[value[part] for value in values]))
    return acc


def solute_pairs(acc, p, charge, lower, upper):
    for part in chunks(p.shape[0]):
        low, high = lower[part], upper[part]
        if low.shape[1] != p.shape[1]:
            low, high = jnp.concatenate([low] * 2, axis=1), jnp.concatenate([high] * 2, axis=1)
        acc = fold(acc, solute_energy(p[part], charge[part], low, high))
    return acc


def dot(left, right):
    return jnp.dot(left, right, preferred_element_type=F32)


def only(side, number):
    parts = [side, jnp.zeros_like(side)]
    return jnp.concatenate(parts if number == 0 else parts[::-1], axis=0)


def each(left, right):
    top = jnp.concatenate([left, jnp.zeros_like(right)], axis=1)
    bottom = jnp.concatenate([jnp.zeros_like(left), right], axis=1)
    return jnp.concatenate([top, bottom], axis=0)


def crossed(left, right):
    top = jnp.concatenate([jnp.zeros_like(left), right], axis=1)
    bottom = jnp.concatenate([left, jnp.zeros_like(right)], axis=1)
    return jnp.concatenate([top, bottom], axis=0)


def halves_of(column, f, feat_ref):
    first, second = feat_ref[2 * column, f], feat_ref[2 * column + 1, f]
    return (
        jnp.concatenate([first[:, :64], second[:, :64]], axis=1),
        jnp.concatenate([first[:, 64:], second[:, 64:]], axis=1),
    )


def atom_pairs(acc, columns, own_ref, f, i, solute_ref, coef_ref):
    for column in columns:
        left = solute_ref[column]
        for j in range(2):
            cell = 2 * column + j
            acc = solute_pairs(
                acc, *[dot(left, only(own_ref[f, i, rows], j)) for rows in (P_ROWS, Q_ROWS)],
                coef_ref[cell, 0], coef_ref[cell, 1],
            )
    return acc


def inner_kernel(
    feat_ref, acc_ref, other_ref, own_ref, atoms_ref, left_ref, mono_ref, sum_ref, solute_ref, coef_ref,
):
    frames = feat_ref.shape[1] - 1
    own_pairs = [[(feat_ref, 2 * i + j, (0.0, 0.0), 0.0) for j in range(2)] for i in range(2)]
    set_solutes(own_pairs, frames, solute_ref, coef_ref, 0)

    def set_up(f):
        for i in range(2):
            left_ref[f, i] = pair_rows(
                *[water_partner(feat_ref[2 * i + j, f], (0.0, 0.0), 0.0) for j in range(2)]
            )
            mono_ref[f, i] = moment_rows(
                *[moment_partner(feat_ref[2 * i + j, f], (0.0, 0.0)) for j in range(2)]
            )
            own_ref[f, i, 0:OWN_ROWS] = jnp.concatenate(
                [own_side(half) for half in halves_of(i, f, feat_ref)], axis=1
            )

    def frame(f):
        atoms_ref[f] = atom_pairs(jnp.zeros((8, 256), F32), (0, 1), own_ref, f, 0, solute_ref, coef_ref)
        for i in range(2):
            sides = (own_ref[f, i, P_ROWS], own_ref[f, i, M_ROWS])
            acc = jnp.zeros((8, 256), F32)
            lefts = (left_ref[f, i], mono_ref[f, i])
            for j in range(2):
                acc = water_pairs(acc, [dot(left, only(side, j)) for left, side in zip(lefts, sides)])
            if i == 0:
                near = (left_ref[f, 1, 0:64], mono_ref[f, 1, 0:64])
                for j in range(2):
                    values = [dot(left, only(side, j)) for left, side in zip(near, sides)]
                    for part in chunks(64):
                        energy = water_energy(*[value[part] for value in values])
                        acc = fold(acc, energy)
                        sum_ref[f, j, part] = energy[:, :128] + energy[:, 128:]
                far = (left_ref[f, 1, 64:128], mono_ref[f, 1, 64:128])
                values = [
                    dot(left, each(side[:, 128:], side[:, 128:])) for left, side in zip(far, sides)
                ]
                late = jnp.zeros((8, 256), F32)
                for part in chunks(64):
                    energy = water_energy(*[value[part] for value in values])
                    late = fold(late, energy)
                    rows = slice(64 + part.start, 64 + part.stop)
                    sum_ref[f, 0, rows] = energy[:, :128]
                    sum_ref[f, 1, rows] = energy[:, 128:]
                acc = acc + jnp.concatenate(
                    [jnp.zeros((8, 128), F32), late[:, :128] + late[:, 128:]], axis=1
                )
            acc_ref[f, i] = acc
        for j in range(2):
            other_ref[f, j] = fold(jnp.zeros((8, 128), F32), sum_ref[f, j].T)

    run_frames(frames, set_up, frame)


def to_facing():
    return jnp.where(lax.axis_index("py") == 0, 1.0, -1.0).astype(F32) * (2.0 * CUTOFF * UNIT)


def set_solutes(pairs, frames, solute_ref, coef_ref, start):
    for number, pair in enumerate(pairs, start):
        solute_ref[number] = pair_rows(
            *[solute_partner(ref[k, frames], shift, absent) for ref, k, shift, absent in pair]
        )
        for place, (ref, k, _, _) in enumerate(pair):
            cell = 2 * number + place
            coef_ref[cell, 0], coef_ref[cell, 1] = solute_levels(ref[k, frames])


def set_waters(pairs, f, left_ref, mono_ref):
    for number, pair in enumerate(pairs):
        left_ref[f, number] = pair_rows(
            *[water_partner(ref[k, f], shift, absent) for ref, k, shift, absent in pair]
        )
        mono_ref[f, number] = moment_rows(
            *[moment_partner(ref[k, f], shift) for ref, k, shift, _ in pair]
        )


def ends():
    px = lax.axis_index("px")
    no_low = jnp.where(px == 0, 1.0, 0.0).astype(F32)
    no_high = jnp.where(px == lax.axis_size("px") - 1, 1.0, 0.0).astype(F32)
    width = 2.0 * CUTOFF * UNIT
    return (-width, no_low), (width, no_high)


def column_kernel(
    feat_ref, low_ref, high_ref, own_ref, water_ref, atoms_ref, acc_ref,
    left_ref, mono_ref, solute_ref, coef_ref,
):
    frames = feat_ref.shape[1] - 1
    (low_x, no_low), (high_x, no_high) = ends()
    pairs = (
        tuple((low_ref, j, (low_x, 0.0), no_low) for j in range(2)),
        tuple((high_ref, j, (high_x, 0.0), no_high) for j in range(2)),
    )
    own_pairs = [[(feat_ref, 2 * i + j, (0.0, 0.0), 0.0) for j in range(2)] for i in range(2)]
    set_solutes(own_pairs, frames, solute_ref, coef_ref, 0)
    set_solutes(pairs, frames, solute_ref, coef_ref, 2)

    def set_up(f):
        set_waters(pairs, f, left_ref, mono_ref)

    def frame(f):
        for i in range(2):
            sides = [own_ref[f, i, rows] for rows in (P_ROWS, Q_ROWS, M_ROWS)]
            solute = atoms_ref[f] if i == 0 else jnp.zeros((8, 256), F32)
            columns = (2,) if i == 0 else (0, 1, 3)
            solute = atom_pairs(solute, columns, own_ref, f, i, solute_ref, coef_ref)
            acc_ref[f, i, 1] = solute
            full, part = (slice(64, 128), slice(0, 64)) if i == 0 else (slice(0, 64), slice(64, 128))
            lanes = slice(0, 128) if i == 0 else slice(128, 256)
            water = water_ref[f, i]
            for j in range(2):
                water = water_pairs(
                    water,
                    [
                        dot(left_ref[f, i, full], only(sides[0], j)),
                        dot(mono_ref[f, i, full], only(sides[2], j)),
                    ],
                )
            late = water_pairs(
                jnp.zeros((8, 256), F32),
                [
                    dot(left_ref[f, i, part], each(sides[0][:, lanes], sides[0][:, lanes])),
                    dot(mono_ref[f, i, part], each(sides[2][:, lanes], sides[2][:, lanes])),
                ],
            )
            late = [late[:, :128] + late[:, 128:], jnp.zeros((8, 128), F32)]
            acc_ref[f, i, 0] = water + jnp.concatenate(late if i == 0 else late[::-1], axis=1)

    run_frames(frames, set_up, frame)


def facing_kernel(
    feat_ref, side_ref, acc_ref, other_ref, comp_ref, send_ref,
    left_ref, mono_ref, solute_ref, coef_ref, face_ref, wall_ref, rec_ref,
):
    frames = feat_ref.shape[1] - 1
    facing = 1 - lax.axis_index("py")
    across = to_facing()
    (low_x, no_low), (high_x, no_high) = ends()
    pairs = (
        tuple((side_ref, k, (0.0, across), 0.0) for k in range(2)),
        ((side_ref, 2, (low_x, across), no_low), (side_ref, 3, (high_x, across), no_high)),
    )
    set_solutes(pairs, frames, solute_ref, coef_ref, 0)

    def set_up(f):
        set_waters(pairs, f, left_ref, mono_ref)
        face_ref[f] = jnp.concatenate(
            [own_side(feat_ref[facing, f]), own_side(feat_ref[2 + facing, f])], axis=1
        )

    def frame(f):
        faces = [face_ref[f, rows] for rows in (P_ROWS, Q_ROWS, M_ROWS)]
        water = jnp.zeros((8, 256), F32)
        solute = jnp.zeros((8, 256), F32)
        for meet, number, order in ((each, 0, (0, 1)), (crossed, 0, (1, 0)), (each, 1, (2, 3))):
            sides = [meet(face[:, :128], face[:, 128:]) for face in faces]
            water = water_pairs(
                water, [dot(left_ref[f, number], sides[0]), dot(mono_ref[f, number], sides[2])]
            )
            levels = [
                jnp.concatenate([coef_ref[order[0], k], coef_ref[order[1], k]], axis=1) for k in range(2)
            ]
            solute = solute_pairs(
                solute, *[dot(solute_ref[number], sides[q]) for q in range(2)], *levels
            )
        wall_ref[f, 0] = water
        wall_ref[f, 1] = solute

    run_frames(frames, set_up, frame)
    rec_ref[...] = comp_ref[...]
    self_root = P_SOFT**-0.5
    self_u15 = self_root**3
    for f in range(frames):
        walls = [jnp.sum(wall_ref[f, k], axis=0, keepdims=True) for k in range(2)]
        for i in range(2):
            sums = [jnp.sum(acc_ref[f, i, k], axis=0, keepdims=True) for k in range(2)]
            for j in range(2):
                near = (facing == j).astype(F32)
                water, solute = (
                    jnp.concatenate([value[:, 64 * j : 64 * j + 64], value[:, 128 + 64 * j : 192 + 64 * j]], axis=1)
                    + near * wall[:, 128 * i : 128 * i + 128]
                    for value, wall in zip(sums, walls)
                )
                if i == 1:
                    water = water + jnp.sum(other_ref[f, j], axis=0, keepdims=True)
                value = feat_ref[2 * i + j, f]
                filled = value[6:7]
                moment = value[3:4] * value[3:4] + value[4:5] * value[4:5] + value[5:6] * value[5:6]
                own = (self_u15 * P_CUT * P_CUT) * (
                    self_u15 * (self_u15 * self_u15 - 1.0) + KD * moment
                )
                fc = (2 * i + j) * frames + f
                rec_ref[fc, 6:7, :] = filled * (SCALE_SW * solute)
                rec_ref[fc, 7:8, :] = filled * (SCALE_WW * (water - own))
    send_ref[...] = rec_ref[...].reshape(128, 128).T.reshape(send_ref.shape)


def bin_kernel(frame_total, got_ref, out_ref, field_ref, rec_ref):
    share = out_ref.shape[-1]
    groups = -(-share // 128)
    number = lax.broadcasted_iota(jnp.int32, (128, 128), 0).astype(F32)
    field_ref[...] = got_ref[...].reshape(128, 128).T.reshape(field_ref.shape)
    filled = field_ref[:, 4, :]
    quaternion = [field_ref[:, k, :] for k in range(4)]
    rec_ref[:, 0, :] = filled
    rec_ref[:, 1, :] = field_ref[:, 6, :]
    rec_ref[:, 2, :] = field_ref[:, 7, :]
    for k, (a, b) in enumerate(pair_index):
        rec_ref[:, 3 + k, :] = quaternion[a] * quaternion[b] * filled
    for k in range(13, 16):
        rec_ref[:, k, :] = jnp.zeros_like(filled)
    for i in range(2):
        for j in range(2):
            totals = jnp.zeros((48 * groups, 128), F32)
            for f in range(4):
                fc = (2 * i + j) * 4 + f
                voxel = field_ref[fc, 5:6, :]
                group = jnp.floor((voxel + 0.5) * (1.0 / 128.0))
                chosen = jnp.where(number == voxel - 128.0 * group, 1.0, 0.0).astype(BF16)
                parts = jnp.concatenate(split3(rec_ref[fc]), axis=0)
                parts = jnp.concatenate(
                    [jnp.where(group == k, parts, 0.0) for k in range(groups)], axis=0
                ).astype(BF16)
                totals = totals + lax.dot_general(
                    parts, chosen, (((1,), (1,)), ((), ())), preferred_element_type=F32
                )
            for k in range(groups):
                lanes = min(128, share - 128 * k)
                part = totals[48 * k : 48 * k + 48]
                summed = (part[0:16] + part[16:32] + part[32:48])[:, :lanes]
                counted = summed[0:1]
                span = slice(128 * k, 128 * k + lanes)
                out_ref[0:1, i, j, span] = counted * (1.0 / (frame_total * rho_bulk * spacing**3))
                out_ref[1:13, i, j, span] = summed[1:13] / jnp.maximum(counted, 1.0)


def vmem():
    return pl.BlockSpec(memory_space=pltpu.VMEM)


PARAMS = pltpu.CompilerParams(vmem_limit_bytes=24 * 1024 * 1024)


def shards(
    water_voxel, water_offset, water_angles, water_count,
    solute_frac, solute_type, type_sigma, type_well, type_charge,
):
    frames = water_voxel.shape[0]
    cols = lax.axis_size("px")
    ranks = lax.axis_size("fr")
    total = 4 * frames
    rows = (-1, 2, 128)
    pieces = (
        water_voxel.reshape(rows),
        jnp.transpose(water_offset, (0, 1, 3, 2, 4)).reshape(rows),
        jnp.transpose(water_angles, (0, 1, 3, 2, 4)).reshape(rows),
        jnp.transpose(solute_frac, (0, 2, 1, 3)).reshape(rows),
        solute_type.reshape(rows),
        jnp.transpose(water_count, (1, 2, 0)),
        type_sigma.reshape(1, 1, -1), type_well.reshape(1, 1, -1), type_charge.reshape(1, 1, -1),
    )
    deep = sum(piece.shape[0] for piece in pieces)
    sums = {F32: jnp.zeros((deep, 2, 128), F32), jnp.int32: jnp.zeros((deep, 2, 128), jnp.int32)}
    start = 0
    for piece in pieces:
        size = piece.shape
        kind = F32 if piece.dtype == F32 else jnp.int32
        sums[kind] = sums[kind] + lax.pad(
            piece, jnp.zeros((), kind),
            ((start, deep - start - size[0], 0), (0, 2 - size[1], 0), (0, 128 - size[2], 0)),
        )
        start += size[0]
    packed = sums[F32] + sums[jnp.int32].astype(F32)
    feat, side_out, comp = pl.pallas_call(
        prepare_kernel,
        out_shape=(
            jax.ShapeDtypeStruct((4, frames + 1, 8, 128), F32),
            jax.ShapeDtypeStruct((2, frames + 1, 8, 128), F32),
            jax.ShapeDtypeStruct((total, 8, 128), F32),
        ),
        in_specs=[vmem()],
        out_specs=(vmem(),) * 3,
        scratch_shapes=[
            pltpu.VMEM((total, 8, 128), F32),
            pltpu.VMEM((total, 128), F32),
            pltpu.VMEM((8, total, 128), F32),
        ],
        compiler_params=PARAMS,
        name="prepare",
    )(packed)

    up = [(k, (k + 1) % cols) for k in range(cols)]
    down = [(k, (k - 1) % cols) for k in range(cols)]
    low = lax.ppermute(feat[2:4], "px", up)
    high = lax.ppermute(feat[0:2], "px", down)

    work = pl.CostEstimate(flops=10**9, bytes_accessed=10**6, transcendentals=0)
    column_shape = jax.ShapeDtypeStruct((frames, 2, 8, 256), F32)
    water, other, own, atoms = pl.pallas_call(
        inner_kernel,
        out_shape=(
            column_shape,
            jax.ShapeDtypeStruct((frames, 2, 8, 128), F32),
            jax.ShapeDtypeStruct((frames, 2, HELD_ROWS, 256), BF16),
            jax.ShapeDtypeStruct((frames, 8, 256), F32),
        ),
        in_specs=[vmem()],
        out_specs=(vmem(),) * 4,
        scratch_shapes=[
            pltpu.VMEM((frames, 2, 128, 2 * ROWS), BF16),
            pltpu.VMEM((frames, 2, 128, 2 * MONO), BF16),
            pltpu.VMEM((frames, 2, 128, 128), F32),
            pltpu.VMEM((2, 128, 2 * ROWS), BF16),
            pltpu.VMEM((4, 2, 128, 128), F32),
        ],
        compiler_params=PARAMS,
        cost_estimate=work,
        name="inner",
    )(feat)

    low, high, water = lax.optimization_barrier((low, high, water))
    facing = 1 - lax.axis_index("py")
    beyond = [lax.dynamic_slice_in_dim(column, facing, 1, axis=0) for column in (low, high)]
    side = lax.ppermute(jnp.concatenate([side_out, *beyond], axis=0), "py", [(0, 1), (1, 0)])
    acc = pl.pallas_call(
        column_kernel,
        out_shape=jax.ShapeDtypeStruct((frames, 2, 2, 8, 256), F32),
        in_specs=[vmem()] * 6,
        out_specs=vmem(),
        scratch_shapes=[
            pltpu.VMEM((frames, 2, 128, 2 * ROWS), BF16),
            pltpu.VMEM((frames, 2, 128, 2 * MONO), BF16),
            pltpu.VMEM((4, 128, 2 * ROWS), BF16),
            pltpu.VMEM((8, 2, 128, 128), F32),
        ],
        compiler_params=PARAMS,
        cost_estimate=work,
        name="columns",
    )(feat, low, high, own, water, atoms)

    send = pl.pallas_call(
        facing_kernel,
        out_shape=jax.ShapeDtypeStruct((ranks, 4, 128), F32),
        in_specs=[vmem()] * 5,
        out_specs=vmem(),
        scratch_shapes=[
            pltpu.VMEM((frames, 2, 128, 2 * ROWS), BF16),
            pltpu.VMEM((frames, 2, 128, 2 * MONO), BF16),
            pltpu.VMEM((2, 128, 2 * ROWS), BF16),
            pltpu.VMEM((4, 2, 128, 128), F32),
            pltpu.VMEM((frames, OWN_ROWS, 256), BF16),
            pltpu.VMEM((frames, 2, 8, 256), F32),
            pltpu.VMEM((total, 8, 128), F32),
        ],
        compiler_params=PARAMS,
        name="facing",
    )(feat, side, acc, other, comp)

    got = lax.all_to_all(send, "fr", 0, 0, tiled=True)
    share = CELL_XY * CELL_XY * SLAB // ranks
    return pl.pallas_call(
        functools.partial(bin_kernel, frames * ranks),
        out_shape=jax.ShapeDtypeStruct((13, 2, 2, share), F32),
        in_specs=[vmem()],
        out_specs=vmem(),
        scratch_shapes=[pltpu.VMEM((total, 8, 128), F32), pltpu.VMEM((total, 16, 128), F32)],
        compiler_params=PARAMS,
        name="bin",
    )(got)


def solution(mesh):
    placed = (
        P("fr", "px", "py", None),
        P("fr", "px", "py", None, None),
        P("fr", "px", "py", None, None),
        P("fr", "px", "py"),
        P("px", "py", None, None),
        P("px", "py", None),
        P(),
        P(),
        P(),
    )
    return jax.shard_map(
        shards, mesh=mesh, in_specs=placed, out_specs=P(None, "px", "py", "fr"), check_vma=False
    )
```
